512 devices in a mesh: dp: 16 (over y_lo, x, core), mp: 32 (over y_hi, z).
Axes of the slice: x: 4, y: 4 (y_hi: 2, y_lo: 2; y = y_hi * 2 + y_lo), z: 16, core: 2. Of those that a mesh axis runs over, the one named last changes fastest.
Arguments:
- tokens: bfloat16 [4096, 3072], P('dp', 'mp'), may hold values from -6 to 6
- gain: bfloat16 [3072], P('mp'), may hold values from 0.099609375 to 1.8984375
- w_qkv: bfloat16 [3072, 32, 384], P(None, 'mp'), may hold values from -0.21875 to 0.21875
- out_grad: bfloat16 [4096, 4096], P('dp', 'mp'), may hold values from -12 to 12
Outputs:
- attn_out: bfloat16 [4096, 4096], P('dp', 'mp')
- input_grad: bfloat16 [4096, 3072], P('dp', 'mp')
- weight_grad: float32 [3072, 32, 384], P('dp', 'mp')
- gain_grad: float32 [3072], P('mp')
The draws below stay inside these ranges and needn't reach their ends.
All inputs are finite; a program needn't handle non-finite values.
Results may differ from the reference program's by a relative error of at most 0.03.
Values may be sent and summed in bfloat16 or wider, within the bound.
A program may use at most 64 MiB of HBM per device.

```python
import math
import jax
import jax.numpy as jnp
from jax import lax

D = 3072
HDIM = 128
PATCHES = 256
HEADS = 32
TOK_DEV = 256
TOKENS = 4096
N_DP = 16


def with_spikes(drawn, own_key, source, target, shards_of, factor):
    owner, partner = [(jnp.arange(drawn.shape[dim]) // (drawn.shape[dim] // shards_of)).reshape([-1 if axis == dim else 1 for axis in range(drawn.ndim)]) for dim in (source, target)]
    chosen = jax.random.permutation(own_key, shards_of)[partner]
    strong = (owner == chosen) | (owner == (partner + shards_of // 2) % shards_of)
    return jnp.where(strong, factor * drawn, drawn)


def level_of(key, dims, cuts, low, top_value):
    def one(dim, parts):
        draws = jax.random.uniform(jax.random.fold_in(jax.random.fold_in(key, 6), dim), (parts,), jnp.float32, low / len(cuts), top_value / len(cuts))
        return jnp.repeat(jnp.exp(draws), dims[dim] // parts).reshape((-1,) + (1,) * (len(dims) - dim - 1))

    level = one(*cuts[0])
    for cut in cuts[1:]:
        level = level * one(*cut)
    return level


def bell_draw(rng, extent, spread, bound, shards=(), kind=jnp.bfloat16):
    values = jax.random.normal(rng, extent, jnp.float32) * spread
    if len(shards) > 0:
        values = level_of(rng, extent, shards, -0.22, 0.18) * values
    return jnp.clip(values, min=-bound, max=bound).astype(kind)


def gaussian_with(own_key, extent, scale, reach, shards, heavy, kind=jnp.bfloat16):
    values = scale * jax.random.normal(own_key, extent, jnp.float32)
    if shards:
        values = values * level_of(own_key, extent, shards, -0.22, 0.18)
    return jnp.clip(with_spikes(values, jax.random.fold_in(own_key, 3), *heavy), -reach, reach).astype(kind)


def setup_inputs(seed: int = 0) -> dict:
    streams_of = jax.random.split(jax.random.key(seed), 5)
    return {
        "tokens": gaussian_with(streams_of[0], (TOKENS, D), 1.0, 6.0, ((0, 16), (1, 32)), (0, 1, 32, 2.75)),
        "gain": jnp.clip(1.0 + 0.18 * jax.random.normal(streams_of[1], (D,), jnp.float32), 0.099609375, 1.8984375).astype(jnp.bfloat16),
        "w_qkv": gaussian_with(streams_of[2], (D, HEADS, 3 * HDIM), D ** -0.5, 0.21875, ((1, 32),), (1, 0, 32, 2.75)),
        "out_grad": bell_draw(streams_of[3], (TOKENS, HEADS * HDIM), 2.0, 12.0, ((0, 16), (1, 32))),
    }


epsilon = 1e-06

def unit_rows(matrix):
    centred = matrix - lax.optimization_barrier(jnp.mean(matrix, axis=-1, keepdims=True))
    return centred * lax.rsqrt(lax.optimization_barrier(jnp.mean(centred * centred, axis=-1, keepdims=True)) + epsilon)

def exact_attention(projected):
    head_width = projected.shape[1] // 3
    image_count = projected.shape[0] // PATCHES
    query = unit_rows(projected[:, :head_width]).reshape(image_count, PATCHES, head_width)
    key_rows = unit_rows(projected[:, head_width:2 * head_width]).reshape(image_count, PATCHES, head_width)
    value_rows = projected[:, 2 * head_width:].reshape(image_count, PATCHES, head_width)
    scores = jnp.einsum('nqd,nkd->nqk', query, key_rows) / math.sqrt(head_width)
    exponent = jnp.exp(scores)
    weights_soft = exponent / lax.optimization_barrier(jnp.sum(exponent, axis=-1, keepdims=True))
    return jnp.einsum('nqk,nkd->nqd', weights_soft, value_rows).reshape(-1, head_width)

def settle(matrix):
    return lax.optimization_barrier(matrix.astype(jnp.bfloat16)).astype(jnp.float32)

def rounded_attention(projected):
    head_width = projected.shape[1] // 3
    image_count = projected.shape[0] // PATCHES
    widened = projected.astype(jnp.float32)
    query = settle(unit_rows(widened[:, :head_width])).reshape(image_count, PATCHES, head_width)
    key_rows = settle(unit_rows(widened[:, head_width:2 * head_width])).reshape(image_count, PATCHES, head_width)
    value_rows = widened[:, 2 * head_width:].reshape(image_count, PATCHES, head_width)
    scores = jnp.einsum('nqd,nkd->nqk', query, key_rows) / math.sqrt(head_width)
    exponent = jnp.exp(scores)
    weights_soft = settle(exponent / lax.optimization_barrier(jnp.sum(exponent, axis=-1, keepdims=True)))
    result = jnp.einsum('nqk,nkd->nqd', weights_soft, value_rows).reshape(-1, head_width)
    return result.astype(jnp.bfloat16)

def reference(tokens, gain, w_qkv, out_grad):
    widened = tokens.astype(jnp.float32)
    normed = unit_rows(widened)
    normed_in = (normed * gain.astype(jnp.float32)).astype(jnp.bfloat16)
    token_blocks = normed_in.reshape(N_DP, TOK_DEV, D).astype(jnp.float32)

    def per_head(accum_sum, head_index):
        weights = lax.dynamic_index_in_dim(w_qkv, head_index, 1, keepdims=False)
        projected = jnp.dot(normed_in, weights, preferred_element_type=jnp.float32).astype(jnp.bfloat16)
        attended = rounded_attention(projected)
        cotangent = lax.dynamic_slice_in_dim(out_grad, head_index * HDIM, HDIM, 1).astype(jnp.float32)
        _, pullback = jax.vjp(exact_attention, projected.astype(jnp.float32))
        head_grad = pullback(cotangent)[0].astype(jnp.bfloat16)
        partials = jnp.einsum('itd,itc->idc', token_blocks, head_grad.reshape(N_DP, TOK_DEV, -1).astype(jnp.float32))
        weight_part = lax.optimization_barrier(jnp.sum(settle(partials), axis=0))
        backward = jnp.dot(head_grad, weights.T, preferred_element_type=jnp.float32)
        return (accum_sum + settle(backward), (attended, weight_part))
    start_sum = jnp.zeros((TOKENS, D), jnp.float32)
    input_pull, (attended_all, weight_all) = lax.scan(per_head, start_sum, jnp.arange(HEADS, dtype=jnp.int32))
    attn_out = attended_all.transpose(1, 0, 2).reshape(TOKENS, HEADS * HDIM)
    weight_grad = weight_all.transpose(1, 0, 2)
    _, norm_pullback = jax.vjp(unit_rows, widened)
    input_grad = norm_pullback(input_pull * gain.astype(jnp.float32))[0].astype(jnp.bfloat16)
    gain_grad = lax.optimization_barrier(jnp.sum(input_pull * normed, axis=0))
    return (attn_out, input_grad, weight_grad, gain_grad)
```

```python
import math

import jax
import jax.numpy as jnp
from jax import lax
from jax.experimental import pallas as pl
from jax.experimental.pallas import tpu as pltpu
from jax.sharding import PartitionSpec as P

D = 3072
PATCHES = 256
HDIM = 128
FEAT = 96
NZ = 16
NY = 2
NMP = NZ * NY
CHIPS = 8
ROWS = 192
EPS = 1e-06
F32 = jnp.float32
BF16 = jnp.bfloat16
MESH = pl.DeviceIdType.MESH
VMEM = pltpu.VMEM


def ring_places():
    mp = lax.axis_index("mp")
    row, z = mp // NZ, mp % NZ
    right = row * NZ + (z + 1) % NZ
    left = row * NZ + (z + NZ - 1) % NZ
    partner = (1 - row) * NZ + z
    return mp, row, z, right, left, partner


def remote(src, dst, send_sem, recv_sem, target):
    return pltpu.make_async_remote_copy(
        src_ref=src,
        dst_ref=dst,
        send_sem=send_sem,
        recv_sem=recv_sem,
        device_id=target,
        device_id_type=MESH,
    )


def hops_of(direction, stream):
    return NZ // 2 if direction == stream else NZ // 2 - 1


def gather_kernel(x_ref, gain_ref, g_ref, gg_ref, send, recv, gsend, grecv, ysend, yrecv):
    mp, row, z, right, left, partner = ring_places()
    barrier = pltpu.get_barrier_semaphore()
    for peer in (right, left, partner):
        pl.semaphore_signal(barrier, inc=1, device_id={"mp": peer}, device_id_type=MESH)
    g_ref[mp] = x_ref[...]
    gg_ref[z, row] = jnp.concatenate(
        [gain_ref[...].astype(F32), jnp.zeros((1, 128 - FEAT), F32)], axis=1
    )
    pl.semaphore_wait(barrier, 3)

    ring = (right, left)
    ends = (row, 1 - row)

    def block_copy(direction, stream, hop, distance):
        source = (z - distance + NZ) % NZ if direction == 0 else (z + distance) % NZ
        ref = g_ref.at[ends[stream] * NZ + source]
        return remote(
            ref,
            ref,
            send.at[direction, stream, hop],
            recv.at[direction, stream, hop],
            {"mp": ring[direction]},
        )

    def gain_copy(direction, hop, distance):
        source = (z - distance + NZ) % NZ if direction == 0 else (z + distance) % NZ
        ref = gg_ref.at[source]
        return remote(
            ref, ref, gsend.at[direction, hop], grecv.at[direction, hop], {"mp": ring[direction]}
        )

    own, other = g_ref.at[mp], g_ref.at[partner]
    across = remote(own, own, ysend.at[0], yrecv.at[0], {"mp": partner})
    across.start()
    gown = gg_ref.at[z, row]
    gacross = remote(gown, gown, ysend.at[1], yrecv.at[1], {"mp": partner})
    gacross.start()
    for direction in (0, 1):
        block_copy(direction, 0, 0, 0).start()
    remote(other, other, ysend.at[0], yrecv.at[0], {"mp": partner}).wait_recv()
    for direction in (0, 1):
        block_copy(direction, 1, 0, 0).start()
    gother = gg_ref.at[z, 1 - row]
    remote(gother, gother, ysend.at[1], yrecv.at[1], {"mp": partner}).wait_recv()
    for direction in (0, 1):
        gain_copy(direction, 0, 0).start()
    for hop in range(1, NZ // 2 + 1):
        for stream in (0, 1):
            for direction in (0, 1):
                hops = hops_of(direction, stream)
                if hop <= hops:
                    block_copy(direction, stream, hop - 1, hop).wait_recv()
                if hop < hops:
                    block_copy(direction, stream, hop, hop).start()
        for direction in (0, 1):
            hops = hops_of(direction, 0)
            if hop <= hops:
                gain_copy(direction, hop - 1, hop).wait_recv()
            if hop < hops:
                gain_copy(direction, hop, hop).start()
    across.wait_send()
    gacross.wait_send()
    for direction in (0, 1):
        for stream in (0, 1):
            for hop in range(hops_of(direction, stream)):
                block_copy(direction, stream, hop, hop).wait_send()
        for hop in range(hops_of(direction, 0)):
            gain_copy(direction, hop, hop).wait_send()


def gather(x, gain):
    return pl.pallas_call(
        gather_kernel,
        out_shape=(
            jax.ShapeDtypeStruct((NMP, FEAT, PATCHES), BF16),
            jax.ShapeDtypeStruct((NZ, NY, 1, 128), F32),
        ),
        in_specs=[pl.BlockSpec(memory_space=VMEM)] * 2,
        out_specs=(pl.BlockSpec(memory_space=VMEM), pl.BlockSpec(memory_space=VMEM)),
        scratch_shapes=[
            pltpu.SemaphoreType.DMA((2, 2, 8)),
            pltpu.SemaphoreType.DMA((2, 2, 8)),
            pltpu.SemaphoreType.DMA((2, 8)),
            pltpu.SemaphoreType.DMA((2, 8)),
            pltpu.SemaphoreType.DMA((2,)),
            pltpu.SemaphoreType.DMA((2,)),
        ],
        compiler_params=pltpu.CompilerParams(
            collective_id=0, has_side_effects=True, vmem_limit_bytes=16 << 20
        ),
    )(x, gain)


def folded(matrix):
    return jnp.sum(matrix.reshape(matrix.shape[0] // 8, 8, matrix.shape[1]), axis=0)


def column_mean(matrix):
    return jnp.sum(matrix, axis=0, keepdims=True) * (1.0 / matrix.shape[0])


def unit_columns(matrix):
    centred = matrix - column_mean(matrix)
    inverse = lax.rsqrt(column_mean(centred * centred) + EPS)
    return centred * inverse, inverse


def unit_pullback(normal, inverse, cotangent):
    return inverse * (
        cotangent - column_mean(cotangent) - normal * column_mean(cotangent * normal)
    )


def dot(a, b):
    return jnp.dot(a, b, preferred_element_type=F32)


def dot_rows(a, b):
    return lax.dot_general(a, b, (((1,), (1,)), ((), ())), preferred_element_type=F32)


def compute_kernel(
    g_ref,
    gg_ref,
    w_ref,
    do_ref,
    att_ref,
    pull_ref,
    ws_ref,
    sums_ref,
    stats_ref,
    gown_ref,
    nt_ref,
    wt_ref,
    rows_ref,
    gb_ref,
    hg_ref,
):
    mp = lax.axis_index("mp")
    for part in range(D // 256):
        wt_ref[:, part * 256 : (part + 1) * 256] = w_ref[part * 256 : (part + 1) * 256, :].T
    for block in range(NMP):
        rows_ref[block : block + 1, :] = gg_ref[block % NZ, block // NZ]
    turned = rows_ref[...].T
    for block in range(NMP):
        gb_ref[block] = jnp.broadcast_to(turned[:FEAT, block : block + 1], (FEAT, 128)).astype(BF16)
    gown_ref[...] = gb_ref[mp].astype(F32)
    gain_weights = dot(wt_ref[...], gb_ref[...].reshape(D, 128))

    def add_sum(block, total):
        return total + folded(g_ref[block].astype(F32))

    total = lax.fori_loop(0, NMP, add_sum, jnp.zeros((8, PATCHES), F32))
    average = jnp.sum(total, axis=0, keepdims=True) * (1.0 / D)

    def add_square(block, total):
        centred = g_ref[block].astype(F32) - average
        return total + folded(centred * centred)

    total = lax.fori_loop(0, NMP, add_square, jnp.zeros((8, PATCHES), F32))
    inverse = lax.rsqrt(jnp.sum(total, axis=0, keepdims=True) * (1.0 / D) + EPS)
    stats_ref[0] = average
    stats_ref[1] = inverse

    def normalize(block, carry):
        factor = gb_ref[block].astype(F32)
        factor = jnp.concatenate([factor, factor], axis=1)
        normed = (g_ref[block].astype(F32) - average) * inverse
        nt_ref[block] = (normed * factor).astype(BF16)
        return carry

    lax.fori_loop(0, NMP, normalize, 0)

    wide = dot(wt_ref[...], nt_ref[...].reshape(D, PATCHES))
    projected = wide.astype(BF16)
    query, query_inverse = unit_columns(projected[:HDIM].astype(F32))
    keys, keys_inverse = unit_columns(projected[HDIM : 2 * HDIM].astype(F32))
    values = projected[2 * HDIM :]
    query_r, keys_r = query.astype(BF16), keys.astype(BF16)
    scale = 1.0 / math.sqrt(HDIM)
    exponent = jnp.exp(dot(keys_r.T, query_r) * scale)
    soft = exponent / jnp.sum(exponent, axis=0, keepdims=True)
    soft_r = soft.astype(BF16)
    att_ref[...] = dot(values, soft_r).T.astype(BF16)
    cotangent = do_ref[...].T
    soft_grad = dot(values.T, cotangent)
    values_grad = dot_rows(cotangent, soft_r)
    score_grad = soft * (soft_grad - jnp.sum(soft * soft_grad, axis=0, keepdims=True))
    score_grad = (score_grad * scale).astype(BF16)
    query_grad = unit_pullback(query, query_inverse, dot(keys_r, score_grad))
    keys_grad = unit_pullback(keys, keys_inverse, dot_rows(query_r, score_grad))
    hg = jnp.concatenate([query_grad, keys_grad, values_grad], axis=0).astype(BF16)
    hg_ref[...] = hg
    hg_wide = hg.astype(F32)
    factor = jnp.concatenate([gain_weights, gain_weights], axis=1)
    sums_ref[0] = jnp.sum(hg_wide * factor, axis=0, keepdims=True)
    sums_ref[1] = jnp.sum(hg_wide * wide, axis=0, keepdims=True)

    def pull_part(part, carry):
        block = dot(w_ref[pl.ds(pl.multiple_of(part * 384, 384), 384), :], hg_ref[...])
        pull_ref[pl.ds(part * 4, 4)] = block.astype(BF16).reshape(4, FEAT, PATCHES)
        return carry

    lax.fori_loop(0, 8, pull_part, 0)

    def weight_part(part, carry):
        block = dot_rows(nt_ref[pl.ds(part * 4, 4)].reshape(384, PATCHES), hg_ref[...])
        ws_ref[pl.ds(part * 2, 2)] = block.astype(BF16).reshape(2, ROWS, 3 * HDIM)
        return carry

    lax.fori_loop(0, 8, weight_part, 0)


def compute(g, gg, weights, out_grad):
    return pl.pallas_call(
        compute_kernel,
        out_shape=(
            jax.ShapeDtypeStruct((PATCHES, HDIM), BF16),
            jax.ShapeDtypeStruct((NMP, FEAT, PATCHES), BF16),
            jax.ShapeDtypeStruct((2 * CHIPS, ROWS, 3 * HDIM), BF16),
            jax.ShapeDtypeStruct((2, 1, PATCHES), F32),
            jax.ShapeDtypeStruct((2, 1, PATCHES), F32),
            jax.ShapeDtypeStruct((FEAT, 128), F32),
        ),
        in_specs=[pl.BlockSpec(memory_space=VMEM)] * 4,
        out_specs=tuple([pl.BlockSpec(memory_space=VMEM)] * 6),
        scratch_shapes=[
            VMEM((NMP, FEAT, PATCHES), BF16),
            VMEM((3 * HDIM, D), BF16),
            VMEM((NMP, 128), F32),
            VMEM((NMP, FEAT, 128), BF16),
            VMEM((3 * HDIM, PATCHES), BF16),
        ],
        compiler_params=pltpu.CompilerParams(vmem_limit_bytes=40 << 20),
    )(g, gg, weights, out_grad)


def scatter_kernel(
    pull_ref,
    ws_ref,
    sums_ref,
    stats_ref,
    gown_ref,
    x_ref,
    ig_ref,
    wg_ref,
    gg_ref,
    land,
    ystage,
    yland,
    tot,
    spair,
    sland,
    cland,
    dland,
    gland,
    gstage,
    send,
    recv,
    ssend,
    srecv,
    ysend,
    yrecv,
    csend,
    crecv,
    dsend,
    drecv,
    gsend,
    grecv,
):
    mp, row, z, right, left, partner = ring_places()
    dp = lax.axis_index("dp")
    chip, core = dp // 2, dp % 2
    barrier = pltpu.get_barrier_semaphore()
    for peer in (right, left, partner):
        pl.semaphore_signal(barrier, inc=1, device_id={"mp": peer}, device_id_type=MESH)
    mate = chip * 2 + 1 - core
    pl.semaphore_signal(barrier, inc=1, device_id={"dp": mate}, device_id_type=MESH)

    def chip_at(shift):
        line, place = chip // 4, chip % 4
        return ((line + shift // 4) % 2) * 4 + (place + shift % 4) % 4

    for shift in range(1, CHIPS):
        pl.semaphore_signal(
            barrier, inc=1, device_id={"dp": chip_at(shift) * 2 + core}, device_id_type=MESH
        )
    pl.semaphore_wait(barrier, 3 + 1 + CHIPS - 1)

    ring = (right, left)
    ends = (row, 1 - row)

    def target(direction, stream, left_over):
        place = (z + left_over) % NZ if direction == 0 else (z - left_over + NZ) % NZ
        return ends[stream] * NZ + place

    def ring_copy(direction, stream, hop):
        hops = hops_of(direction, stream)
        if hop == 0:
            src = pull_ref.at[target(direction, stream, hops)]
        else:
            src = land.at[direction, stream, hop - 1]
        return remote(
            src,
            land.at[direction, stream, hop],
            send.at[direction, stream, hop],
            recv.at[direction, stream, hop],
            {"mp": ring[direction]},
        )

    def sum_copy(direction, hop, distance):
        source = (z - distance + NZ) % NZ if direction == 0 else (z + distance) % NZ
        ref = sland.at[source]
        return remote(
            ref, ref, ssend.at[direction, hop], srecv.at[direction, hop], {"mp": ring[direction]}
        )

    def core_copy(shift):
        to = chip_at(shift)
        return remote(
            ws_ref.at[to * 2 + 1 - core],
            cland.at[to],
            csend.at[shift],
            crecv.at[shift],
            {"dp": mate},
        )

    def chip_copy(shift):
        to = chip_at(shift)
        return remote(
            cland.at[to],
            dland.at[shift],
            dsend.at[shift],
            drecv.at[shift],
            {"dp": to * 2 + core},
        )

    def chip_step(shift):
        core_copy(shift).wait_recv()
        to = chip_at(shift)
        both = cland[to].astype(F32) + ws_ref[to * 2 + core].astype(F32)
        if shift == 0:
            wg_ref[...] = both
        else:
            cland[to] = both.astype(BF16)
            chip_copy(shift).start()

    sums_across = remote(sums_ref, spair, ysend.at[1], yrecv.at[1], {"mp": partner})
    sums_across.start()
    for stream in (1, 0):
        for direction in (0, 1):
            ring_copy(direction, stream, 0).start()
    order = (6, 2, 5, 7, 4, 1, 3, 0)
    for shift in order:
        core_copy(shift).start()
    sums_across.wait_recv()
    sland[z] = sums_ref[...] + spair[...]
    for direction in (0, 1):
        sum_copy(direction, 0, 0).start()
    for hop in range(1, NZ // 2 + 1):
        for stream in (1, 0):
            for direction in (0, 1):
                hops = hops_of(direction, stream)
                if hop <= hops:
                    ring_copy(direction, stream, hop - 1).wait_recv()
                if hop < hops:
                    slot = land.at[direction, stream, hop - 1]
                    mine = pull_ref[target(direction, stream, hops - hop)]
                    slot[...] = (slot[...].astype(F32) + mine.astype(F32)).astype(BF16)
                    ring_copy(direction, stream, hop).start()
        for direction in (0, 1):
            hops = hops_of(direction, 0)
            if hop <= hops:
                sum_copy(direction, hop - 1, hop).wait_recv()
            if hop < hops:
                sum_copy(direction, hop, hop).start()
        if hop < NZ // 2:
            chip_step(order[hop - 1])
    half = NZ // 2
    ystage[...] = (
        pull_ref[partner].astype(F32)
        + land[0, 1, half - 2].astype(F32)
        + land[1, 1, half - 1].astype(F32)
    ).astype(BF16)
    across = remote(ystage, yland, ysend.at[0], yrecv.at[0], {"mp": partner})
    across.start()
    chip_step(order[half - 1])
    tot[...] = (
        pull_ref[mp].astype(F32)
        + land[0, 0, half - 1].astype(F32)
        + land[1, 0, half - 2].astype(F32)
    )
    sums = sland[0]
    for place in range(1, NZ):
        sums = sums + sland[place]
    average, inverse = stats_ref[0], stats_ref[1]
    normed = (x_ref[...].astype(F32) - average) * inverse
    across.wait_recv()
    pull = tot[...] + yland[...].astype(F32)
    cross = pull * normed
    turned = (cross[:, :128] + cross[:, 128:]).T
    gstage[0] = jnp.concatenate(
        [jnp.sum(turned, axis=0, keepdims=True), jnp.zeros((1, 128 - FEAT), F32)], axis=1
    )
    gain_core = remote(gstage.at[0], gland.at[0], gsend.at[0], grecv.at[0], {"dp": mate})
    gain_core.start()
    gain_own = gown_ref[...]
    scaled = pull * jnp.concatenate([gain_own, gain_own], axis=1)
    ig_ref[...] = (
        inverse * (scaled - sums[0] * (1.0 / D) - normed * (sums[1] * (1.0 / D)))
    ).astype(BF16)
    gain_core.wait_recv()
    gstage[1] = gstage[0] + gland[0]

    def gain_copy(shift):
        return remote(
            gstage.at[1],
            gland.at[shift],
            gsend.at[shift],
            grecv.at[shift],
            {"dp": chip_at(shift) * 2 + core},
        )

    for shift in range(1, CHIPS):
        gain_copy(shift).start()
    for shift in order[:-1]:
        chip_copy(shift).wait_recv()
        wg_ref[...] += dland[shift].astype(F32)
    gain_total = gstage[1]
    for shift in range(1, CHIPS):
        gain_copy(shift).wait_recv()
        gain_total = gain_total + gland[shift]
    gg_ref[...] = gain_total
    sums_across.wait_send()
    across.wait_send()
    gain_core.wait_send()
    for direction in (0, 1):
        for stream in (0, 1):
            for hop in range(hops_of(direction, stream)):
                ring_copy(direction, stream, hop).wait_send()
        for hop in range(hops_of(direction, 0)):
            sum_copy(direction, hop, hop).wait_send()
    for shift in range(CHIPS):
        core_copy(shift).wait_send()
        if shift > 0:
            chip_copy(shift).wait_send()
            gain_copy(shift).wait_send()


def scatter(pull, share, sums, stats, gain_own, x):
    dma = pltpu.SemaphoreType.DMA
    return pl.pallas_call(
        scatter_kernel,
        out_shape=(
            jax.ShapeDtypeStruct((FEAT, PATCHES), BF16),
            jax.ShapeDtypeStruct((ROWS, 3 * HDIM), F32),
            jax.ShapeDtypeStruct((1, 128), F32),
        ),
        in_specs=[pl.BlockSpec(memory_space=VMEM)] * 6,
        out_specs=tuple([pl.BlockSpec(memory_space=VMEM)] * 3),
        scratch_shapes=[
            VMEM((2, 2, 8, FEAT, PATCHES), BF16),
            VMEM((FEAT, PATCHES), BF16),
            VMEM((FEAT, PATCHES), BF16),
            VMEM((FEAT, PATCHES), F32),
            VMEM((2, 1, PATCHES), F32),
            VMEM((NZ, 2, 1, PATCHES), F32),
            VMEM((CHIPS, ROWS, 3 * HDIM), BF16),
            VMEM((CHIPS, ROWS, 3 * HDIM), BF16),
            VMEM((CHIPS, 1, 128), F32),
            VMEM((2, 1, 128), F32),
            dma((2, 2, 8)),
            dma((2, 2, 8)),
            dma((2, 8)),
            dma((2, 8)),
            dma((2,)),
            dma((2,)),
            dma((CHIPS,)),
            dma((CHIPS,)),
            dma((CHIPS,)),
            dma((CHIPS,)),
            dma((CHIPS,)),
            dma((CHIPS,)),
        ],
        compiler_params=pltpu.CompilerParams(
            collective_id=1, has_side_effects=True, vmem_limit_bytes=40 << 20
        ),
    )(pull, share, sums, stats, gain_own, x)


def on_device(tokens, gain, w_qkv, out_grad):
    x = tokens.T
    gathered, gains = gather(x, gain.reshape(1, FEAT))
    attended, pull, share, sums, stats, gain_own = compute(
        gathered, gains, w_qkv[:, 0, :], out_grad
    )
    input_grad, weight_grad, gain_grad = scatter(pull, share, sums, stats, gain_own, x)
    return attended, input_grad.T, weight_grad[:, None, :], gain_grad[0, :FEAT]


def solution(mesh):
    in_specs = (P("dp", "mp"), P("mp"), P(None, "mp", None), P("dp", "mp"))
    out_specs = (P("dp", "mp"), P("dp", "mp"), P("dp", "mp", None), P("mp"))
    return jax.shard_map(
        on_device, mesh=mesh, in_specs=in_specs, out_specs=out_specs, check_vma=False
    )
```

```python
import math

import jax
import jax.numpy as jnp
from jax import lax
from jax.experimental import pallas as pl
from jax.experimental.pallas import tpu as pltpu
from jax.sharding import PartitionSpec as P

D = 3072
PATCHES = 256
HDIM = 128
FEAT = 96
NZ = 16
NY = 2
NMP = NZ * NY
CHIPS = 8
ROWS = 192
EPS = 1e-06
F32 = jnp.float32
BF16 = jnp.bfloat16
MESH = pl.DeviceIdType.MESH
VMEM = pltpu.VMEM


def remote(src, dst, send_sem, recv_sem, target):
    return pltpu.make_async_remote_copy(
        src_ref=src,
        dst_ref=dst,
        send_sem=send_sem,
        recv_sem=recv_sem,
        device_id=target,
        device_id_type=MESH,
    )


def folded(matrix):
    return jnp.sum(matrix.reshape(matrix.shape[0] // 8, 8, matrix.shape[1]), axis=0)


def column_mean(matrix):
    return jnp.sum(matrix, axis=0, keepdims=True) * (1.0 / matrix.shape[0])


def unit_columns(matrix):
    centred = matrix - column_mean(matrix)
    inverse = lax.rsqrt(column_mean(centred * centred) + EPS)
    return centred * inverse, inverse


def unit_pullback(normal, inverse, cotangent):
    return inverse * (
        cotangent - column_mean(cotangent) - normal * column_mean(cotangent * normal)
    )


def dot(a, b):
    return jnp.dot(a, b, preferred_element_type=F32)


def dot_rows(a, b):
    return lax.dot_general(a, b, (((1,), (1,)), ((), ())), preferred_element_type=F32)


def hub_of(offset):
    sign = 1 if offset > 0 else -1
    return sign * {1: 0, 3: 0, 2: 3, 4: 3, 6: 3, 5: 6, 7: 6}[abs(offset)]


LEAVES = (5, -5, 7, -7, 8, 2, -2, 4, -4)


def fused_kernel(
    x_any,
    gain_ref,
    w_any,
    do_any,
    att_ref,
    ig_ref,
    wg_ref,
    gg_ref,
    w_ref,
    do_ref,
    g_ref,
    gains,
    wt_ref,
    rows_ref,
    gb_ref,
    nt_ref,
    hg_ref,
    pull_ref,
    ws_ref,
    zland,
    yland,
    oland,
    ostage,
    sums,
    spair,
    sland,
    cland,
    xland,
    hland,
    hstage,
    gstage,
    gland,
    local,
    zsend,
    zrecv,
    ysend,
    yrecv,
    osend,
    orecv,
    psend,
    precv,
    psend2,
    precv2,
    qsend,
    qrecv,
    rzsend,
    rzrecv,
    rysend,
    ryrecv,
    rosend,
    rorecv,
    csend,
    crecv,
    xsend,
    xrecv,
    hsend,
    hrecv,
    gsend,
    grecv,
):
    mp = lax.axis_index("mp")
    row, z = mp // NZ, mp % NZ
    dp = lax.axis_index("dp")
    line, place, core = dp // 8, (dp // 2) % 4, dp % 2
    sign8 = 1 - 2 * core
    mine, theirs = row * NZ, (1 - row) * NZ
    partner = {"mp": theirs + z}

    def along(offset):
        return (z + offset + 2 * NZ) % NZ

    def at_z(offset):
        return {"mp": mine + along(offset)}

    def at_dp(line_of, place_of, core_of):
        return {"dp": (line_of * 4 + place_of) * 2 + core_of}

    def place_at(shift):
        return (place + shift) % 4

    mate = at_dp(line, place, 1 - core)
    across_line = at_dp(1 - line, place, core)

    own_copy = pltpu.make_async_copy(x_any, g_ref.at[mp], local.at[0])
    w_copy = pltpu.make_async_copy(w_any, w_ref, local.at[1])
    do_copy = pltpu.make_async_copy(do_any, do_ref, local.at[2])
    own_copy.start()
    w_copy.start()
    do_copy.start()
    barrier = pltpu.get_barrier_semaphore()
    peers = [at_z(offset) for offset in range(1, NZ)] + [partner, mate, across_line]
    peers += [at_dp(line, place_at(shift), core) for shift in (1, 2, 3)]
    for peer in peers:
        pl.semaphore_signal(barrier, inc=1, device_id=peer, device_id_type=MESH)
    gains[z, row] = jnp.concatenate(
        [gain_ref[...].astype(F32), jnp.zeros((1, 128 - FEAT), F32)], axis=1
    )
    own_copy.wait()
    pl.semaphore_wait(barrier, len(peers))

    def spread(offset):
        hub = 6 * sign8 if offset == 8 else hub_of(offset)
        block = g_ref.at[mine + along(-hub)]
        step = offset - hub
        slot = offset % NZ
        return remote(block, block, zsend.at[slot], zrecv.at[slot], at_z(step))

    def arrived(offset):
        block = g_ref.at[mine + along(-offset)]
        slot = offset % NZ
        remote(block, block, zsend.at[slot], zrecv.at[slot], at_z(1)).wait_recv()

    def over(offset):
        block = g_ref.at[mine + along(-offset)]
        slot = offset % NZ
        return remote(block, block, ysend.at[slot], yrecv.at[slot], partner)

    def over_arrived(offset):
        block = g_ref.at[theirs + along(-offset)]
        slot = offset % NZ
        remote(block, block, ysend.at[slot], yrecv.at[slot], partner).wait_recv()

    def other(which, offset):
        block = g_ref.at[theirs + z]
        return remote(block, block, osend.at[which], orecv.at[which], at_z(offset))

    def other_arrived(which, offset):
        block = g_ref.at[theirs + along(-offset)]
        remote(block, block, osend.at[which], orecv.at[which], at_z(offset)).wait_recv()

    def gain_to(offset):
        pair = gains.at[z]
        return remote(pair, pair, psend.at[offset], precv.at[offset], at_z(offset))

    for offset in (3, -3):
        spread(offset).start()
    over(0).start()
    for offset in (1, -1):
        spread(offset).start()
    gown = gains.at[z, row]
    gain_over = remote(gown, gown, psend2.at[0], precv2.at[0], partner)
    gain_over.start()
    w_copy.wait()
    for part in range(D // 256):
        wt_ref[:, part * 256 : (part + 1) * 256] = w_ref[part * 256 : (part + 1) * 256, :].T
    over_arrived(0)
    for which, offset in enumerate((1, -1)):
        other(which, offset).start()
    for sign in (1, -1):
        arrived(3 * sign)
        for offset in (6 * sign, 4 * sign, 2 * sign):
            spread(offset).start()
        over(3 * sign).start()
    gother = gains.at[z, 1 - row]
    remote(gother, gother, psend2.at[0], precv2.at[0], partner).wait_recv()
    for offset in range(1, NZ):
        gain_to(offset).start()
    for sign in (1, -1):
        arrived(6 * sign)
        for offset in (5 * sign, 7 * sign):
            spread(offset).start()
        over(6 * sign).start()
    spread(8).start()
    arrived(1)
    arrived(-1)
    for offset in (2, -2, 4, -4, 5, -5, 7, -7, 8):
        arrived(offset)
        over(offset).start()
    for offset in range(1, NZ):
        pair = gains.at[along(-offset)]
        remote(pair, pair, psend.at[offset], precv.at[offset], at_z(offset)).wait_recv()
    for block in range(NMP):
        rows_ref[block : block + 1, :] = gains[block % NZ, block // NZ]
    turned = rows_ref[...].T
    for block in range(NMP):
        gb_ref[block] = jnp.broadcast_to(turned[:FEAT, block : block + 1], (FEAT, 128)).astype(BF16)
    gain_weights = dot(wt_ref[...], gb_ref[...].reshape(D, 128))
    do_copy.wait()
    cotangent = do_ref[...].T

    shift_row = jnp.sum(g_ref[mp].astype(F32), axis=0, keepdims=True) * (1.0 / FEAT)

    def add_block(block, totals):
        moved = g_ref[block].astype(F32) - shift_row
        return totals[0] + folded(moved), totals[1] + folded(moved * moved)

    zero = jnp.zeros((8, PATCHES), F32)
    totals = lax.fori_loop(mine, mine + NZ, add_block, (zero, zero))
    other_arrived(0, 1)
    other_arrived(1, -1)
    for offset in (3, -3, 6, -6, 2, -2, 4, -4, 5, -5, 7, -7, 8):
        over_arrived(offset)
    totals = lax.fori_loop(theirs, theirs + NZ, add_block, totals)
    first = jnp.sum(totals[0], axis=0, keepdims=True) * (1.0 / D)
    second = jnp.sum(totals[1], axis=0, keepdims=True) * (1.0 / D)
    average = shift_row + first
    inverse = lax.rsqrt(second - first * first + EPS)

    def normalize(block, carry):
        factor = gb_ref[block].astype(F32)
        factor = jnp.concatenate([factor, factor], axis=1)
        normed = (g_ref[block].astype(F32) - average) * inverse
        nt_ref[block] = (normed * factor).astype(BF16)
        return carry

    lax.fori_loop(0, NMP, normalize, 0)

    wide = dot(wt_ref[...], nt_ref[...].reshape(D, PATCHES))
    projected = wide.astype(BF16)
    query, query_inverse = unit_columns(projected[:HDIM].astype(F32))
    keys, keys_inverse = unit_columns(projected[HDIM : 2 * HDIM].astype(F32))
    values = projected[2 * HDIM :]
    query_r, keys_r = query.astype(BF16), keys.astype(BF16)
    scale = 1.0 / math.sqrt(HDIM)
    exponent = jnp.exp(dot(keys_r.T, query_r) * scale)
    soft = exponent / jnp.sum(exponent, axis=0, keepdims=True)
    soft_r = soft.astype(BF16)
    soft_grad = dot(values.T, cotangent)
    values_grad = dot_rows(cotangent, soft_r)
    score_grad = soft * (soft_grad - jnp.sum(soft * soft_grad, axis=0, keepdims=True))
    score_grad = (score_grad * scale).astype(BF16)
    query_grad = unit_pullback(query, query_inverse, dot(keys_r, score_grad))
    keys_grad = unit_pullback(keys, keys_inverse, dot_rows(query_r, score_grad))
    hg = jnp.concatenate([query_grad, keys_grad, values_grad], axis=0).astype(BF16)
    hg_ref[...] = hg

    def pull_rows(start):
        def pull_part(part, carry):
            block = start + part * 4
            rows = pl.ds(pl.multiple_of(block * FEAT, 4 * FEAT), 4 * FEAT)
            pull_ref[pl.ds(block, 4)] = (
                dot(w_ref[rows, :], hg_ref[...]).astype(BF16).reshape(4, FEAT, PATCHES)
            )
            return carry

        lax.fori_loop(0, 4, pull_part, 0)

    def back_over(offset):
        slot = offset % NZ
        src = ostage if offset == 0 else pull_ref.at[theirs + along(-offset)]
        return remote(src, yland.at[slot], rysend.at[slot], ryrecv.at[slot], partner)

    def back_other(which, offset):
        return remote(
            pull_ref.at[theirs + along(-offset)],
            oland.at[which],
            rosend.at[which],
            rorecv.at[which],
            at_z(-offset),
        )

    def back(offset):
        hub = 6 * sign8 if offset == 8 else hub_of(offset)
        slot = offset % NZ
        return remote(
            pull_ref.at[mine + along(-offset)],
            zland.at[slot],
            rzsend.at[slot],
            rzrecv.at[slot],
            at_z(hub - offset),
        )

    def gathered(offset, inputs):
        slot = offset % NZ
        back_over(offset).wait_recv()
        total = pull_ref[mine + along(-offset)].astype(F32) + yland[slot].astype(F32)
        for at in inputs:
            back(at).wait_recv()
            total = total + zland[at % NZ].astype(F32)
        return total

    def pass_on(offset, total):
        pull_ref[mine + along(-offset)] = total.astype(BF16)
        back(offset).start()

    pull_rows(theirs)
    for which, offset in enumerate((1, -1)):
        back_other(which, offset).start()
    for offset in (5, -5, 7, -7, 8, 6, -6, 2, -2, 4, -4, 3, -3):
        back_over(offset).start()

    def core_copy(shift, line_of):
        chip = line_of * 4 + place_at(shift)
        slot = shift * 2 + line_of
        return remote(
            ws_ref.at[chip * 2 + 1 - core],
            cland.at[shift, line_of],
            csend.at[slot],
            crecv.at[slot],
            mate,
        )

    def core_sum(shift, line_of):
        chip = line_of * 4 + place_at(shift)
        core_copy(shift, line_of).wait_recv()
        both = cland[shift, line_of].astype(F32) + ws_ref[chip * 2 + core].astype(F32)
        cland[shift, line_of] = both.astype(BF16)

    def place_copy(shift):
        return remote(
            cland.at[shift],
            xland.at[shift - 1],
            xsend.at[shift - 1],
            xrecv.at[shift - 1],
            at_dp(line, place_at(shift), core),
        )

    shifts = (2, 1, 3, 0)
    for shift in shifts:
        for line_of in (0, 1):
            chip = line_of * 4 + place_at(shift)
            block = dot_rows(nt_ref[pl.ds(chip * 4, 4)].reshape(4 * FEAT, PATCHES), hg_ref[...])
            ws_ref[pl.ds(chip * 2, 2)] = block.astype(BF16).reshape(2, ROWS, 3 * HDIM)
            core_copy(shift, line_of).start()
    hg_wide = hg.astype(F32)
    factor = jnp.concatenate([gain_weights, gain_weights], axis=1)
    sums[0] = jnp.sum(hg_wide * factor, axis=0, keepdims=True)
    sums[1] = jnp.sum(hg_wide * wide, axis=0, keepdims=True)
    sums_over = remote(sums, spair, psend2.at[1], precv2.at[1], partner)
    sums_over.start()
    pull_rows(mine)
    for offset in (1, -1):
        back(offset).start()
    att_ref[...] = dot(values, soft_r).T.astype(BF16)

    def leaf(offset):
        pass_on(offset, gathered(offset, ()))

    for offset in (5, -5, 7, -7):
        leaf(offset)
    for shift in shifts[:-1]:
        core_sum(shift, 0)
        core_sum(shift, 1)
        place_copy(shift).start()
    leaf(8)
    sums_over.wait_recv()
    sland[z] = sums[...] + spair[...]

    def sums_to(offset):
        pair = sland.at[z]
        return remote(pair, pair, qsend.at[offset], qrecv.at[offset], at_z(offset))

    for offset in range(1, NZ):
        sums_to(offset).start()
    for which, offset in enumerate((1, -1)):
        back_other(which, offset).wait_recv()
    ostage[...] = (
        pull_ref[theirs + z].astype(F32) + oland[0].astype(F32) + oland[1].astype(F32)
    ).astype(BF16)
    back_over(0).start()
    for sign in (1, -1):
        total = gathered(6 * sign, (5 * sign, 7 * sign))
        if sign > 0:
            back(8).wait_recv()
        mask = (1 - core if sign > 0 else core).astype(F32)
        pass_on(6 * sign, total + mask * zland[8].astype(F32))
    for offset in (2, -2, 4, -4):
        leaf(offset)
    core_sum(0, 0)
    core_sum(0, 1)
    for sign in (1, -1):
        pass_on(3 * sign, gathered(3 * sign, (2 * sign, 4 * sign, 6 * sign)))
    far = cland[0, 1 - line].astype(F32)
    for shift in (1, 2, 3):
        place_copy(shift).wait_recv()
        far = far + xland[shift - 1, 1 - line].astype(F32)
    hstage[...] = far.astype(BF16)
    line_copy = remote(hstage, hland, hsend.at[0], hrecv.at[0], across_line)
    line_copy.start()
    near = cland[0, line].astype(F32)
    for shift in (1, 2, 3):
        near = near + xland[shift - 1, line].astype(F32)
    wg_ref[...] = near

    sum_all = sland[z]
    for offset in range(1, NZ):
        pair = sland.at[along(-offset)]
        remote(pair, pair, qsend.at[offset], qrecv.at[offset], at_z(offset)).wait_recv()
        sum_all = sum_all + sland[along(-offset)]
    normed = (g_ref[mp].astype(F32) - average) * inverse
    pull = gathered(0, (1, -1, 3, -3))
    product = pull * normed
    turned = (product[:, :128] + product[:, 128:]).T
    gstage[0] = jnp.concatenate(
        [jnp.sum(turned, axis=0, keepdims=True), jnp.zeros((1, 128 - FEAT), F32)], axis=1
    )

    def gain_copy(stage, peer):
        src = gstage.at[min(stage, 1) if stage < 4 else 2]
        return remote(src, gland.at[stage], gsend.at[stage], grecv.at[stage], peer)

    gain_copy(0, mate).start()
    own_gain = gb_ref[mp].astype(F32)
    scaled = pull * jnp.concatenate([own_gain, own_gain], axis=1)
    ig_ref[...] = (
        inverse * (scaled - sum_all[0] * (1.0 / D) - normed * (sum_all[1] * (1.0 / D)))
    ).astype(BF16)
    gain_copy(0, mate).wait_recv()
    gstage[1] = gstage[0] + gland[0]
    for shift in (1, 2, 3):
        gain_copy(shift, at_dp(line, place_at(shift), core)).start()
    line_copy.wait_recv()
    wg_ref[...] += hland[...].astype(F32)
    gain_total = gstage[1]
    for shift in (1, 2, 3):
        gain_copy(shift, mate).wait_recv()
        gain_total = gain_total + gland[shift]
    gstage[2] = gain_total
    gain_copy(4, across_line).start()
    for which in (0, 1):
        other(which, 1).wait_send()
        back_other(which, 1 - 2 * which).wait_send()
    gain_over.wait_send()
    sums_over.wait_send()
    for offset in range(1, NZ):
        gain_to(offset).wait_send()
        sums_to(offset).wait_send()
    for offset in (1, 2, 3, 4, 5, 6, 7, 8, -1, -2, -3, -4, -5, -6, -7):
        spread(offset).wait_send()
        back(offset).wait_send()
        if abs(offset) > 1:
            over(offset).wait_send()
            back_over(offset).wait_send()
    over(0).wait_send()
    back_over(0).wait_send()
    for shift in shifts:
        core_copy(shift, 0).wait_send()
        core_copy(shift, 1).wait_send()
        if shift > 0:
            place_copy(shift).wait_send()
            gain_copy(shift, mate).wait_send()
    line_copy.wait_send()
    gain_copy(0, mate).wait_send()
    gain_copy(4, across_line).wait()
    gg_ref[...] = gain_total + gland[4]


def fused(x, gain, weights, out_grad):
    dma = pltpu.SemaphoreType.DMA
    return pl.pallas_call(
        fused_kernel,
        out_shape=(
            jax.ShapeDtypeStruct((PATCHES, HDIM), BF16),
            jax.ShapeDtypeStruct((FEAT, PATCHES), BF16),
            jax.ShapeDtypeStruct((ROWS, 3 * HDIM), F32),
            jax.ShapeDtypeStruct((1, 128), F32),
        ),
        in_specs=[
            pl.BlockSpec(memory_space=pl.ANY),
            pl.BlockSpec(memory_space=VMEM),
            pl.BlockSpec(memory_space=pl.ANY),
            pl.BlockSpec(memory_space=pl.ANY),
        ],
        out_specs=tuple([pl.BlockSpec(memory_space=VMEM)] * 4),
        scratch_shapes=[
            VMEM((D, 3 * HDIM), BF16),
            VMEM((PATCHES, HDIM), BF16),
            VMEM((NMP, FEAT, PATCHES), BF16),
            VMEM((NZ, NY, 1, 128), F32),
            VMEM((3 * HDIM, D), BF16),
            VMEM((NMP, 128), F32),
            VMEM((NMP, FEAT, 128), BF16),
            VMEM((NMP, FEAT, PATCHES), BF16),
            VMEM((3 * HDIM, PATCHES), BF16),
            VMEM((NMP, FEAT, PATCHES), BF16),
            VMEM((2 * CHIPS, ROWS, 3 * HDIM), BF16),
            VMEM((NZ, FEAT, PATCHES), BF16),
            VMEM((NZ, FEAT, PATCHES), BF16),
            VMEM((2, FEAT, PATCHES), BF16),
            VMEM((FEAT, PATCHES), BF16),
            VMEM((2, 1, PATCHES), F32),
            VMEM((2, 1, PATCHES), F32),
            VMEM((NZ, 2, 1, PATCHES), F32),
            VMEM((4, 2, ROWS, 3 * HDIM), BF16),
            VMEM((3, 2, ROWS, 3 * HDIM), BF16),
            VMEM((ROWS, 3 * HDIM), BF16),
            VMEM((ROWS, 3 * HDIM), BF16),
            VMEM((3, 1, 128), F32),
            VMEM((5, 1, 128), F32),
            dma((3,)),
            dma((NZ,)),
            dma((NZ,)),
            dma((NZ,)),
            dma((NZ,)),
            dma((2,)),
            dma((2,)),
            dma((NZ,)),
            dma((NZ,)),
            dma((2,)),
            dma((2,)),
            dma((NZ,)),
            dma((NZ,)),
            dma((NZ,)),
            dma((NZ,)),
            dma((NZ,)),
            dma((NZ,)),
            dma((2,)),
            dma((2,)),
            dma((8,)),
            dma((8,)),
            dma((3,)),
            dma((3,)),
            dma((1,)),
            dma((1,)),
            dma((5,)),
            dma((5,)),
        ],
        compiler_params=pltpu.CompilerParams(
            collective_id=0, has_side_effects=True, vmem_limit_bytes=56 << 20
        ),
    )(x, gain, weights, out_grad)


def on_device(tokens, gain, w_qkv, out_grad):
    attended, input_grad, weight_grad, gain_grad = fused(
        tokens.T, gain.reshape(1, FEAT), w_qkv[:, 0, :], out_grad
    )
    return attended, input_grad.T, weight_grad[:, None, :], gain_grad[0, :FEAT]


def solution(mesh):
    in_specs = (P("dp", "mp"), P("mp"), P(None, "mp", None), P("dp", "mp"))
    out_specs = (P("dp", "mp"), P("dp", "mp"), P("dp", "mp", None), P("mp"))
    return jax.shard_map(
        on_device, mesh=mesh, in_specs=in_specs, out_specs=out_specs, check_vma=False
    )
```

```python
import math

import jax
import jax.numpy as jnp
from jax import lax
from jax.experimental import pallas as pl
from jax.experimental.pallas import tpu as pltpu
from jax.sharding import PartitionSpec as P

D = 3072
PATCHES = 256
HDIM = 128
FEAT = 96
NZ = 16
NY = 2
NMP = NZ * NY
CHIPS = 8
ROWS = 192
EPS = 1e-06
F32 = jnp.float32
BF16 = jnp.bfloat16
MESH = pl.DeviceIdType.MESH
VMEM = pltpu.VMEM


def remote(src, dst, send_sem, recv_sem, target):
    return pltpu.make_async_remote_copy(
        src_ref=src,
        dst_ref=dst,
        send_sem=send_sem,
        recv_sem=recv_sem,
        device_id=target,
        device_id_type=MESH,
    )


def folded(matrix):
    return jnp.sum(matrix.reshape(matrix.shape[0] // 8, 8, matrix.shape[1]), axis=0)


def column_mean(matrix):
    return jnp.sum(matrix, axis=0, keepdims=True) * (1.0 / matrix.shape[0])


def unit_columns(matrix):
    centred = matrix - column_mean(matrix)
    inverse = lax.rsqrt(column_mean(centred * centred) + EPS)
    return centred * inverse, inverse


def unit_pullback(normal, inverse, cotangent):
    return inverse * (
        cotangent - column_mean(cotangent) - normal * column_mean(cotangent * normal)
    )


def dot(a, b):
    return jnp.dot(a, b, preferred_element_type=F32)


def dot_rows(a, b):
    return lax.dot_general(a, b, (((1,), (1,)), ((), ())), preferred_element_type=F32)


def hub_of(offset):
    sign = 1 if offset > 0 else -1
    return sign * {1: 0, 3: 0, 2: 3, 4: 3, 6: 3, 5: 6, 7: 6}[abs(offset)]


FAR = (5, -5, 7, -7, 8)
NEAR = (2, -2, 4, -4)


def fused_kernel(
    x_any,
    gain_ref,
    w_any,
    do_any,
    att_ref,
    ig_ref,
    wg_ref,
    gg_ref,
    w_ref,
    do_ref,
    g_ref,
    gains,
    wt_ref,
    rows_ref,
    gb_ref,
    nt_ref,
    hg_ref,
    hgt_ref,
    pull_ref,
    ws_ref,
    zland,
    yland,
    oland,
    sums,
    spair,
    sland,
    spart,
    cland,
    xland,
    hland,
    hstage,
    gstage,
    gland,
    local,
    zsend,
    zrecv,
    ysend,
    yrecv,
    osend,
    orecv,
    ssend,
    srecv,
    psend,
    precv,
    rzsend,
    rzrecv,
    rysend,
    ryrecv,
    rosend,
    rorecv,
    csend,
    crecv,
    xsend,
    xrecv,
    hsend,
    hrecv,
    gsend,
    grecv,
):
    mp = lax.axis_index("mp")
    row, z = mp // NZ, mp % NZ
    dp = lax.axis_index("dp")
    line, place, core = dp // 8, (dp // 2) % 4, dp % 2
    sign8 = 1 - 2 * core
    mine, theirs = row * NZ, (1 - row) * NZ
    partner = {"mp": theirs + z}

    def along(offset):
        return (z + offset + 2 * NZ) % NZ

    def at_z(offset):
        return {"mp": mine + along(offset)}

    def at_dp(lines, places, cores):
        return {"dp": (((line + lines) % 2) * 4 + place_at(places)) * 2 + (core + cores) % 2}

    def place_at(shift):
        return (place + shift) % 4

    def hub(offset):
        return 6 * sign8 if offset == 8 else hub_of(offset)

    mate = at_dp(0, 0, 1)
    across_line = at_dp(1, 0, 0)
    others = [(i, j, k) for i in (0, 1) for j in range(4) for k in (0, 1) if i + j + k > 0]

    own_copy = pltpu.make_async_copy(x_any, g_ref.at[mp], local.at[0])
    w_copy = pltpu.make_async_copy(w_any, w_ref, local.at[1])
    do_copy = pltpu.make_async_copy(do_any, do_ref, local.at[2])
    own_copy.start()
    barrier = pltpu.get_barrier_semaphore()
    peers = [at_z(offset) for offset in (3, -3, 2, -2, 1, -1)] + [partner]
    peers += [at_dp(*steps) for steps in others]
    for peer in peers:
        pl.semaphore_signal(barrier, inc=1, device_id=peer, device_id_type=MESH)
    w_copy.start()
    do_copy.start()
    gains[mp] = jnp.concatenate(
        [gain_ref[...].astype(F32), jnp.zeros((1, 128 - FEAT), F32)], axis=1
    )
    own_copy.wait()
    pl.semaphore_wait(barrier, len(peers))

    class Both:
        def __init__(self, block, send, recv, offset, target):
            slot = offset % NZ
            self.copies = [
                remote(ref.at[block], ref.at[block], send.at[i, slot], recv.at[i, slot], target)
                for i, ref in enumerate((g_ref, gains))
            ]

        def start(self):
            for copy in self.copies:
                copy.start()

        def wait_send(self):
            for copy in self.copies:
                copy.wait_send()

        def wait_recv(self):
            for copy in self.copies:
                copy.wait_recv()

    def spread(offset):
        block = mine + along(-hub(offset))
        return Both(block, zsend, zrecv, offset, at_z(offset - hub(offset)))

    def arrived(offset):
        Both(mine + along(-offset), zsend, zrecv, offset, at_z(1)).wait_recv()

    def over(offset):
        return Both(mine + along(-offset), ysend, yrecv, offset, partner)

    def over_arrived(offset):
        Both(theirs + along(-offset), ysend, yrecv, offset, partner).wait_recv()

    def other(offset):
        block = theirs + along(-hub(offset))
        return Both(block, osend, orecv, offset, at_z(offset - hub(offset)))

    def other_arrived(offset):
        Both(theirs + along(-offset), osend, orecv, offset, at_z(1)).wait_recv()

    for offset in (3, -3):
        spread(offset).start()
    over(0).start()
    for offset in (1, -1):
        spread(offset).start()
    w_copy.wait()
    for part in range(D // 256):
        wt_ref[:, part * 256 : (part + 1) * 256] = w_ref[part * 256 : (part + 1) * 256, :].T
    do_copy.wait()
    cotangent = do_ref[...].T
    for sign in (1, -1):
        arrived(3 * sign)
        for offset in (6 * sign, 4 * sign, 2 * sign):
            spread(offset).start()
        over(3 * sign).start()
    for offset in (1, -1, 2, -2, 4, -4):
        arrived(offset)
        over(offset).start()
    for sign in (1, -1):
        arrived(6 * sign)
        over(6 * sign).start()
        for offset in (5 * sign, 7 * sign):
            spread(offset).start()
    spread(8).start()
    for sign in (1, -1):
        over_arrived(6 * sign)
        for offset in (5 * sign, 7 * sign):
            other(offset).start()
    other(8).start()
    for offset in FAR:
        arrived(offset)

    shift_row = jnp.sum(g_ref[mp].astype(F32), axis=0, keepdims=True) * (1.0 / FEAT)

    def add_block(block, totals):
        moved = g_ref[block].astype(F32) - shift_row
        return totals[0] + folded(moved), totals[1] + folded(moved * moved)

    def gain_columns(start):
        for i in range(NZ):
            rows_ref[i : i + 1, :] = gains[start + i]
        turned = rows_ref[...].T
        for i in range(NZ):
            gb_ref[start + i] = jnp.broadcast_to(turned[:FEAT, i : i + 1], (FEAT, 128)).astype(BF16)

    def gain_product(start):
        half = NZ * FEAT
        columns = pl.ds(pl.multiple_of(start * FEAT, half), half)
        return dot(wt_ref[:, columns], gb_ref[pl.ds(start, NZ)].reshape(half, 128))

    zero = jnp.zeros((8, PATCHES), F32)
    totals = lax.fori_loop(mine, mine + NZ, add_block, (zero, zero))
    gain_columns(mine)
    gain_weights = gain_product(mine)
    for offset in (0, 3, -3, 1, -1, 2, -2, 4, -4):
        over_arrived(offset)
    for offset in FAR:
        other_arrived(offset)
    gain_columns(theirs)
    totals = lax.fori_loop(theirs, theirs + NZ, add_block, totals)
    first = jnp.sum(totals[0], axis=0, keepdims=True) * (1.0 / D)
    second = jnp.sum(totals[1], axis=0, keepdims=True) * (1.0 / D)
    average = shift_row + first
    inverse = lax.rsqrt(second - first * first + EPS)

    def normalize(block, carry):
        factor = gb_ref[block].astype(F32)
        factor = jnp.concatenate([factor, factor], axis=1)
        normed = (g_ref[block].astype(F32) - average) * inverse
        nt_ref[block] = (normed * factor).astype(BF16)
        return carry

    lax.fori_loop(0, NMP, normalize, 0)

    wide = dot(wt_ref[...], nt_ref[...].reshape(D, PATCHES))
    projected = wide.astype(BF16)
    query, query_inverse = unit_columns(projected[:HDIM].astype(F32))
    keys, keys_inverse = unit_columns(projected[HDIM : 2 * HDIM].astype(F32))
    values = projected[2 * HDIM :]
    query_r, keys_r = query.astype(BF16), keys.astype(BF16)
    scale = 1.0 / math.sqrt(HDIM)
    exponent = jnp.exp(dot(keys_r.T, query_r) * scale)
    soft = exponent / jnp.sum(exponent, axis=0, keepdims=True)
    soft_r = soft.astype(BF16)
    soft_grad = dot(values.T, cotangent)
    values_grad = dot_rows(cotangent, soft_r)
    score_grad = soft * (soft_grad - jnp.sum(soft * soft_grad, axis=0, keepdims=True))
    score_grad = (score_grad * scale).astype(BF16)
    query_grad = unit_pullback(query, query_inverse, dot(keys_r, score_grad))
    keys_grad = unit_pullback(keys, keys_inverse, dot_rows(query_r, score_grad))
    hg = jnp.concatenate([query_grad, keys_grad, values_grad], axis=0).astype(BF16)
    hg_ref[...] = hg

    def pull_rows(start):
        def pull_part(part, carry):
            block = start + part * 8
            rows = pl.ds(pl.multiple_of(block * FEAT, 8 * FEAT), 8 * FEAT)
            pull_ref[pl.ds(block, 8)] = (
                dot(w_ref[rows, :], hg_ref[...]).astype(BF16).reshape(8, FEAT, PATCHES)
            )
            return carry

        lax.fori_loop(0, 2, pull_part, 0)

    def back_over(offset):
        slot = offset % NZ
        src = pull_ref.at[theirs + along(-offset)]
        return remote(src, yland.at[slot], rysend.at[slot], ryrecv.at[slot], partner)

    def back_along(start, land, send, recv, offset):
        slot = offset % NZ
        return remote(
            pull_ref.at[start + along(-offset)],
            land.at[slot],
            send.at[slot],
            recv.at[slot],
            at_z(hub(offset) - offset),
        )

    def back_other(offset):
        return back_along(theirs, oland, rosend, rorecv, offset)

    def back(offset):
        return back_along(mine, zland, rzsend, rzrecv, offset)

    def back_sums(offset, src):
        slot = offset % NZ
        return remote(
            src, sland.at[slot], ssend.at[slot], srecv.at[slot], at_z(hub(offset) - offset)
        )

    def landed(copy, land, offset):
        copy(offset).wait_recv()
        return land[offset % NZ].astype(F32)

    pull_rows(theirs)
    for offset in FAR:
        back_other(offset).start()
    pull_rows(mine)
    for offset in FAR:
        back(offset).start()
    gain_weights = gain_weights + gain_product(theirs)
    hg_wide = hg.astype(F32)
    factor = jnp.concatenate([gain_weights, gain_weights], axis=1)
    sums[0] = jnp.sum(hg_wide * factor, axis=0, keepdims=True)
    sums[1] = jnp.sum(hg_wide * wide, axis=0, keepdims=True)
    sums_over = remote(sums, spair, psend.at[0], precv.at[0], partner)
    sums_over.start()
    for offset in NEAR + (3, -3):
        back_over(offset).start()

    def core_copy(shift, line_of):
        chip = line_of * 4 + place_at(shift)
        slot = shift * 2 + line_of
        return remote(
            ws_ref.at[chip * 2 + 1 - core],
            cland.at[shift, line_of],
            csend.at[slot],
            crecv.at[slot],
            mate,
        )

    def core_sum(shift, line_of):
        chip = line_of * 4 + place_at(shift)
        core_copy(shift, line_of).wait_recv()
        both = cland[shift, line_of].astype(F32) + ws_ref[chip * 2 + core].astype(F32)
        cland[shift, line_of] = both.astype(BF16)

    def place_copy(shift):
        return remote(
            cland.at[shift],
            xland.at[shift - 1],
            xsend.at[shift - 1],
            xrecv.at[shift - 1],
            at_dp(0, shift, 0),
        )

    hgt_ref[...] = hg.T
    shifts = (2, 1, 3, 0)
    for shift in shifts:
        for line_of in (0, 1):
            chip = line_of * 4 + place_at(shift)
            block = dot(nt_ref[pl.ds(chip * 4, 4)].reshape(4 * FEAT, PATCHES), hgt_ref[...])
            ws_ref[pl.ds(chip * 2, 2)] = block.astype(BF16).reshape(2, ROWS, 3 * HDIM)
            core_copy(shift, line_of).start()
    att_ref[...] = dot(values, soft_r).T.astype(BF16)
    sums_over.wait_recv()
    spair[...] = spair[...] + sums[...]
    for offset in FAR + NEAR + (1, -1):
        back_sums(offset, spair).start()

    for sign in (1, -1):
        total = pull_ref[theirs + along(-6 * sign)].astype(F32)
        total = total + landed(back_other, oland, 5 * sign) + landed(back_other, oland, 7 * sign)
        if sign > 0:
            back_other(8).wait_recv()
        mask = (1 - core if sign > 0 else core).astype(F32)
        total = total + mask * oland[8].astype(F32)
        pull_ref[theirs + along(-6 * sign)] = total.astype(BF16)
        back_over(6 * sign).start()
    for offset in (1, -1, 0):
        back_over(offset).start()
    for shift in shifts[:-1]:
        core_sum(shift, 0)
        core_sum(shift, 1)
        place_copy(shift).start()

    def gathered(offset, inputs):
        total = pull_ref[mine + along(-offset)].astype(F32) + landed(back_over, yland, offset)
        for at in inputs:
            total = total + landed(back, zland, at)
        return total

    def pass_on(offset, total):
        pull_ref[mine + along(-offset)] = total.astype(BF16)
        back(offset).start()

    def sums_of(inputs):
        total = spair[...]
        for at in inputs:
            back_sums(at, spair).wait_recv()
            total = total + sland[at % NZ]
        return total

    for offset in NEAR:
        pass_on(offset, gathered(offset, ()))
    for sign in (1, -1):
        total = gathered(6 * sign, (5 * sign, 7 * sign))
        if sign > 0:
            back(8).wait_recv()
        mask = (1 - core if sign > 0 else core).astype(F32)
        pass_on(6 * sign, total + mask * zland[8].astype(F32))
    for which, sign in enumerate((1, -1)):
        if sign > 0:
            back_sums(8, spair).wait_recv()
        mask = (1 - core if sign > 0 else core).astype(F32)
        spart[which] = sums_of((5 * sign, 7 * sign)) + mask * sland[8]
        back_sums(6 * sign, spart.at[which]).start()
    for offset in (1, -1):
        pass_on(offset, gathered(offset, ()))
    core_sum(0, 0)
    core_sum(0, 1)
    for sign in (1, -1):
        pass_on(3 * sign, gathered(3 * sign, (2 * sign, 4 * sign, 6 * sign)))
    for which, sign in enumerate((1, -1)):
        spart[2 + which] = sums_of((2 * sign, 4 * sign, 6 * sign))
        back_sums(3 * sign, spart.at[2 + which]).start()
    far = cland[0, 1 - line].astype(F32)
    for shift in (1, 2, 3):
        place_copy(shift).wait_recv()
        far = far + xland[shift - 1, 1 - line].astype(F32)
    hstage[...] = far.astype(BF16)
    line_copy = remote(hstage, hland, hsend.at[0], hrecv.at[0], across_line)
    line_copy.start()
    near = cland[0, line].astype(F32)
    for shift in (1, 2, 3):
        near = near + xland[shift - 1, line].astype(F32)
    wg_ref[...] = near

    normed = (g_ref[mp].astype(F32) - average) * inverse
    pull = gathered(0, (1, -1, 3, -3))
    product = pull * normed
    turned = (product[:, :128] + product[:, 128:]).T
    gstage[...] = jnp.concatenate(
        [jnp.sum(turned, axis=0, keepdims=True), jnp.zeros((1, 128 - FEAT), F32)], axis=1
    )

    def gain_copy(steps):
        slot = steps[0] * 8 + steps[1] * 2 + steps[2]
        return remote(gstage, gland.at[slot], gsend.at[slot], grecv.at[slot], at_dp(*steps))

    for steps in others:
        gain_copy(steps).start()
    sum_all = sums_of((1, -1, 3, -3))
    own_gain = gb_ref[mp].astype(F32)
    scaled = pull * jnp.concatenate([own_gain, own_gain], axis=1)
    ig_ref[...] = (
        inverse * (scaled - sum_all[0] * (1.0 / D) - normed * (sum_all[1] * (1.0 / D)))
    ).astype(BF16)
    line_copy.wait_recv()
    wg_ref[...] += hland[...].astype(F32)
    sums_over.wait_send()
    for offset in (1, 2, 3, 4, 5, 6, 7, 8, -1, -2, -3, -4, -5, -6, -7):
        spread(offset).wait_send()
        back(offset).wait_send()
        back_sums(offset, spair).wait_send()
        if offset in FAR:
            other(offset).wait_send()
            back_other(offset).wait_send()
        else:
            over(offset).wait_send()
            back_over(offset).wait_send()
    over(0).wait_send()
    back_over(0).wait_send()
    for shift in shifts:
        core_copy(shift, 0).wait_send()
        core_copy(shift, 1).wait_send()
        if shift > 0:
            place_copy(shift).wait_send()
    line_copy.wait_send()
    gain_total = gstage[...]
    for steps in others:
        gain_copy(steps).wait()
        gain_total = gain_total + gland[steps[0] * 8 + steps[1] * 2 + steps[2]]
    gg_ref[...] = gain_total


def fused(x, gain, weights, out_grad):
    dma = pltpu.SemaphoreType.DMA
    return pl.pallas_call(
        fused_kernel,
        out_shape=(
            jax.ShapeDtypeStruct((PATCHES, HDIM), BF16),
            jax.ShapeDtypeStruct((FEAT, PATCHES), BF16),
            jax.ShapeDtypeStruct((ROWS, 3 * HDIM), F32),
            jax.ShapeDtypeStruct((1, 128), F32),
        ),
        in_specs=[
            pl.BlockSpec(memory_space=pltpu.HBM),
            pl.BlockSpec(memory_space=VMEM),
            pl.BlockSpec(memory_space=pltpu.HBM),
            pl.BlockSpec(memory_space=pltpu.HBM),
        ],
        out_specs=tuple([pl.BlockSpec(memory_space=VMEM)] * 4),
        scratch_shapes=[
            VMEM((D, 3 * HDIM), BF16),
            VMEM((PATCHES, HDIM), BF16),
            VMEM((NMP, FEAT, PATCHES), BF16),
            VMEM((NMP, 1, 128), F32),
            VMEM((3 * HDIM, D), BF16),
            VMEM((NZ, 128), F32),
            VMEM((NMP, FEAT, 128), BF16),
            VMEM((NMP, FEAT, PATCHES), BF16),
            VMEM((3 * HDIM, PATCHES), BF16),
            VMEM((PATCHES, 3 * HDIM), BF16),
            VMEM((NMP, FEAT, PATCHES), BF16),
            VMEM((2 * CHIPS, ROWS, 3 * HDIM), BF16),
            VMEM((NZ, FEAT, PATCHES), BF16),
            VMEM((NZ, FEAT, PATCHES), BF16),
            VMEM((NZ, FEAT, PATCHES), BF16),
            VMEM((2, 1, PATCHES), F32),
            VMEM((2, 1, PATCHES), F32),
            VMEM((NZ, 2, 1, PATCHES), F32),
            VMEM((4, 2, 1, PATCHES), F32),
            VMEM((4, 2, ROWS, 3 * HDIM), BF16),
            VMEM((3, 2, ROWS, 3 * HDIM), BF16),
            VMEM((ROWS, 3 * HDIM), BF16),
            VMEM((ROWS, 3 * HDIM), BF16),
            VMEM((1, 128), F32),
            VMEM((2 * CHIPS, 1, 128), F32),
            dma((3,)),
            dma((2, NZ)),
            dma((2, NZ)),
            dma((2, NZ)),
            dma((2, NZ)),
            dma((2, NZ)),
            dma((2, NZ)),
            dma((NZ,)),
            dma((NZ,)),
            dma((1,)),
            dma((1,)),
            dma((NZ,)),
            dma((NZ,)),
            dma((NZ,)),
            dma((NZ,)),
            dma((NZ,)),
            dma((NZ,)),
            dma((8,)),
            dma((8,)),
            dma((3,)),
            dma((3,)),
            dma((1,)),
            dma((1,)),
            dma((2 * CHIPS,)),
            dma((2 * CHIPS,)),
        ],
        compiler_params=pltpu.CompilerParams(
            collective_id=0, has_side_effects=True, vmem_limit_bytes=28 << 20
        ),
    )(x, gain, weights, out_grad)


def on_device(tokens, gain, w_qkv, out_grad):
    attended, input_grad, weight_grad, gain_grad = fused(
        tokens.T, gain.reshape(1, FEAT), w_qkv[:, 0, :], out_grad
    )
    return attended, input_grad.T, weight_grad[:, None, :], gain_grad[0, :FEAT]


def solution(mesh):
    in_specs = (P("dp", "mp"), P("mp"), P(None, "mp", None), P("dp", "mp"))
    out_specs = (P("dp", "mp"), P("dp", "mp"), P("dp", "mp", None), P("mp"))
    return jax.shard_map(
        on_device, mesh=mesh, in_specs=in_specs, out_specs=out_specs, check_vma=False
    )
```

```python
import math

import jax
import jax.numpy as jnp
from jax import lax
from jax.experimental import pallas as pl
from jax.experimental.pallas import tpu as pltpu
from jax.sharding import PartitionSpec as P

D = 3072
PATCHES = 256
HDIM = 128
FEAT = 96
NZ = 16
NY = 2
NMP = NZ * NY
CHIPS = 8
ROWS = 192
EPS = 1e-06
F32 = jnp.float32
BF16 = jnp.bfloat16
MESH = pl.DeviceIdType.MESH
VMEM = pltpu.VMEM


def remote(src, dst, send_sem, recv_sem, target):
    return pltpu.make_async_remote_copy(
        src_ref=src,
        dst_ref=dst,
        send_sem=send_sem,
        recv_sem=recv_sem,
        device_id=target,
        device_id_type=MESH,
    )


def folded(matrix):
    return jnp.sum(matrix.reshape(matrix.shape[0] // 8, 8, matrix.shape[1]), axis=0)


def column_mean(matrix):
    return jnp.sum(matrix, axis=0, keepdims=True) * (1.0 / matrix.shape[0])


def unit_columns(matrix):
    centred = matrix - column_mean(matrix)
    inverse = lax.rsqrt(column_mean(centred * centred) + EPS)
    return centred * inverse, inverse


def unit_pullback(normal, inverse, cotangent):
    return inverse * (
        cotangent - column_mean(cotangent) - normal * column_mean(cotangent * normal)
    )


def dot(a, b):
    return jnp.dot(a, b, preferred_element_type=F32)


def dot_rows(a, b):
    return lax.dot_general(a, b, (((1,), (1,)), ((), ())), preferred_element_type=F32)


def hub_of(offset):
    sign = 1 if offset > 0 else -1
    return sign * {1: 0, 3: 0, 2: 3, 4: 3, 6: 3, 5: 6, 7: 6}[abs(offset)]


FAR = (5, -5, 7, -7, 8)
FIVES = (5, -5)
NEAR = (2, -2, 4, -4)
GATHER_SLOTS = (
    *(("z", offset) for offset in (3, -3, 1, -1, 6, -6) + NEAR),
    *(("y", offset) for offset in (6, -6)),
    "z far",
    "y near",
    "other",
)
SCATTER_SLOTS = (
    *(("z", offset) for offset in NEAR + (6, -6, 3, -3, 1, -1)),
    *(("y", offset) for offset in (8, 7, -7, 6, -6, 3, -3, 1, -1, 0) + NEAR),
    "z far",
    "other",
)


def fused_kernel(
    x_any,
    gain_ref,
    w_any,
    do_any,
    att_any,
    ig_any,
    wg_any,
    gg_ref,
    att_ref,
    ig_ref,
    wg_ref,
    w_ref,
    do_ref,
    g_ref,
    gains,
    wt_ref,
    rows_ref,
    gb_ref,
    nt_ref,
    hg_ref,
    hgt_ref,
    pull_ref,
    ws_ref,
    zland,
    yland,
    oland,
    sums,
    spair,
    sland,
    spart,
    cland,
    mland,
    xland,
    hland,
    hstage,
    gstage,
    gland,
    local,
    bsend,
    brecv,
    rsend,
    rrecv,
    ssend,
    srecv,
    csend,
    crecv,
    xsend,
    xrecv,
    hsend,
    hrecv,
    gsend,
    grecv,
):
    mp = lax.axis_index("mp")
    row, z = mp // NZ, mp % NZ
    dp = lax.axis_index("dp")
    line, place, core = dp // 8, (dp // 2) % 4, dp % 2
    sign8 = 1 - 2 * core
    mine, theirs = row * NZ, (1 - row) * NZ
    partner = {"mp": theirs + z}

    def along(offset):
        return (z + offset + 2 * NZ) % NZ

    def at_z(offset):
        return {"mp": mine + along(offset)}

    def at_dp(lines, places, cores):
        return {"dp": (((line + lines) % 2) * 4 + place_at(places)) * 2 + (core + cores) % 2}

    def place_at(shift):
        return (place + shift) % 4

    def hub(offset):
        return 6 * sign8 if offset == 8 else hub_of(offset)

    mate = at_dp(0, 0, 1)
    across_line = at_dp(1, 0, 0)
    others = [(i, j, k) for i in (0, 1) for j in range(4) for k in (0, 1) if i + j + k > 0]

    own_copy = pltpu.make_async_copy(x_any, g_ref.at[mp], local.at[0])
    w_copy = pltpu.make_async_copy(w_any, w_ref, local.at[1])
    do_copy = pltpu.make_async_copy(do_any, do_ref, local.at[2])
    own_copy.start()
    barrier = pltpu.get_barrier_semaphore()
    peers = [at_z(offset) for offset in (3, -3, 2, -2, 1, -1)] + [partner]
    peers += [at_dp(*steps) for steps in others]
    for peer in peers:
        pl.semaphore_signal(barrier, inc=1, device_id=peer, device_id_type=MESH)
    w_copy.start()
    do_copy.start()
    gains[mp] = jnp.concatenate(
        [gain_ref[...].astype(F32), jnp.zeros((1, 128 - FEAT), F32)], axis=1
    )
    own_copy.wait()
    pl.semaphore_wait(barrier, len(peers))

    class Both:
        def __init__(self, key, target, block, count=1):
            slot = GATHER_SLOTS.index(key)
            part = block if count == 1 else pl.ds(block, count)
            self.copies = [
                remote(ref.at[part], ref.at[part], bsend.at[i], brecv.at[i, slot], target)
                for i, ref in enumerate((g_ref, gains))
            ]

        def start(self):
            for copy in self.copies:
                copy.start()

        def wait_send(self):
            for copy in self.copies:
                copy.wait_send()

        def wait_recv(self):
            for copy in self.copies:
                copy.wait_recv()

    def spread(offset):
        key = "z far" if offset in FAR else ("z", offset)
        return Both(key, at_z(offset - hub(offset)), mine + along(-hub(offset)))

    def arrived(offset):
        Both(("z", offset), at_z(1), mine + along(-offset)).wait_recv()

    def over(offset):
        key = ("y", offset) if abs(offset) == 6 else "y near"
        return Both(key, partner, mine + along(-offset))

    def over_arrived(offset):
        Both(("y", offset), partner, theirs + along(-offset)).wait_recv()

    def other(offset):
        return Both("other", at_z(offset - hub(offset)), theirs + along(-hub(offset)))

    def all_arrived(key, count):
        Both(key, partner, 0, count).wait_recv()

    for offset in (3, -3):
        spread(offset).start()
    over(0).start()
    for offset in (1, -1):
        spread(offset).start()
    w_copy.wait()
    for part in range(D // 256):
        wt_ref[:, part * 256 : (part + 1) * 256] = w_ref[part * 256 : (part + 1) * 256, :].T
    do_copy.wait()
    cotangent = do_ref[...].T
    for sign in (1, -1):
        arrived(3 * sign)
        for offset in (6 * sign, 4 * sign, 2 * sign):
            spread(offset).start()
        over(3 * sign).start()
    for offset in (1, -1):
        arrived(offset)
        over(offset).start()
    for sign in (1, -1):
        arrived(6 * sign)
        over(6 * sign).start()
        for offset in (5 * sign, 7 * sign):
            spread(offset).start()
    spread(8).start()
    for offset in NEAR:
        arrived(offset)
        over(offset).start()
    for sign in (1, -1):
        over_arrived(6 * sign)
        for offset in (5 * sign, 7 * sign):
            other(offset).start()
    other(8).start()
    all_arrived("z far", len(FAR))

    shift_row = jnp.sum(g_ref[mp].astype(F32), axis=0, keepdims=True) * (1.0 / FEAT)

    def add_block(block, totals):
        moved = g_ref[block].astype(F32) - shift_row
        return totals[0] + folded(moved), totals[1] + folded(moved * moved)

    def gain_columns(start):
        for i in range(NZ):
            rows_ref[i : i + 1, :] = gains[start + i]
        turned = rows_ref[...].T
        for i in range(NZ):
            gb_ref[start + i] = jnp.broadcast_to(turned[:FEAT, i : i + 1], (FEAT, 128)).astype(BF16)

    def gain_product(start):
        half = NZ * FEAT
        columns = pl.ds(pl.multiple_of(start * FEAT, half), half)
        return dot(wt_ref[:, columns], gb_ref[pl.ds(start, NZ)].reshape(half, 128))

    zero = jnp.zeros((8, PATCHES), F32)
    totals = lax.fori_loop(mine, mine + NZ, add_block, (zero, zero))
    gain_columns(mine)
    gain_weights = gain_product(mine)
    all_arrived("y near", 9)
    all_arrived("other", len(FAR))
    gain_columns(theirs)
    totals = lax.fori_loop(theirs, theirs + NZ, add_block, totals)
    first = jnp.sum(totals[0], axis=0, keepdims=True) * (1.0 / D)
    second = jnp.sum(totals[1], axis=0, keepdims=True) * (1.0 / D)
    average = shift_row + first
    inverse = lax.rsqrt(second - first * first + EPS)

    def normalize(block, carry):
        factor = gb_ref[block].astype(F32)
        factor = jnp.concatenate([factor, factor], axis=1)
        normed = (g_ref[block].astype(F32) - average) * inverse
        nt_ref[block] = (normed * factor).astype(BF16)
        return carry

    lax.fori_loop(0, NMP, normalize, 0)

    wide = dot(wt_ref[...], nt_ref[...].reshape(D, PATCHES))
    projected = wide.astype(BF16)
    query, query_inverse = unit_columns(projected[:HDIM].astype(F32))
    keys, keys_inverse = unit_columns(projected[HDIM : 2 * HDIM].astype(F32))
    values = projected[2 * HDIM :]
    query_r, keys_r = query.astype(BF16), keys.astype(BF16)
    scale = 1.0 / math.sqrt(HDIM)
    exponent = jnp.exp(dot(keys_r.T, query_r) * scale)
    soft = exponent / jnp.sum(exponent, axis=0, keepdims=True)
    soft_r = soft.astype(BF16)
    soft_grad = dot(values.T, cotangent)
    values_grad = dot_rows(cotangent, soft_r)
    score_grad = soft * (soft_grad - jnp.sum(soft * soft_grad, axis=0, keepdims=True))
    score_grad = (score_grad * scale).astype(BF16)
    query_grad = unit_pullback(query, query_inverse, dot(keys_r, score_grad))
    keys_grad = unit_pullback(keys, keys_inverse, dot_rows(query_r, score_grad))
    hg = jnp.concatenate([query_grad, keys_grad, values_grad], axis=0).astype(BF16)
    hg_ref[...] = hg

    def pull_rows(start):
        def pull_part(part, carry):
            block = start + part * 8
            rows = pl.ds(pl.multiple_of(block * FEAT, 8 * FEAT), 8 * FEAT)
            pull_ref[pl.ds(block, 8)] = (
                dot(w_ref[rows, :], hg_ref[...]).astype(BF16).reshape(8, FEAT, PATCHES)
            )
            return carry

        lax.fori_loop(0, 2, pull_part, 0)

    def scatter_copy(key, src, dst, target):
        return remote(src, dst, rsend.at[0], rrecv.at[SCATTER_SLOTS.index(key)], target)

    def back_over(offset):
        src = pull_ref.at[theirs + along(-offset)]
        return scatter_copy(("y", offset), src, yland.at[offset % NZ], partner)

    def back_other(offset):
        src = pull_ref.at[theirs + along(-offset)]
        return scatter_copy("other", src, oland.at[FIVES.index(offset)], at_z(hub(offset) - offset))

    def back(offset):
        key = "z far" if offset in FAR else ("z", offset)
        src = pull_ref.at[mine + along(-offset)]
        return scatter_copy(key, src, zland.at[offset % NZ], at_z(hub(offset) - offset))

    def all_landed(key, land, count):
        part = land.at[pl.ds(0, count)]
        scatter_copy(key, part, part, partner).wait_recv()

    def back_sums(offset, src):
        stage = 0 if offset in FAR else (2 if abs(offset) in (1, 3) else 1)
        return remote(
            src,
            sland.at[offset % NZ],
            ssend.at[0],
            srecv.at[stage],
            at_z(hub(offset) - offset),
        )

    def sums_landed(stage, count):
        part = sland.at[pl.ds(0, count)]
        remote(part, part, ssend.at[0], srecv.at[stage], partner).wait_recv()

    def landed(copy, land, offset):
        copy(offset).wait_recv()
        return land[offset % NZ].astype(F32)

    def gathered(offset, inputs):
        total = pull_ref[mine + along(-offset)].astype(F32) + landed(back_over, yland, offset)
        for at in inputs:
            total = total + landed(back, zland, at)
        return total

    def pass_on(offset, total):
        pull_ref[mine + along(-offset)] = total.astype(BF16)
        back(offset).start()

    pull_rows(theirs)
    for offset in FIVES:
        back_other(offset).start()
    for offset in (8, 7, -7):
        back_over(offset).start()
    pull_rows(mine)
    for offset in FIVES:
        back(offset).start()
    gain_weights = gain_weights + gain_product(theirs)
    hg_wide = hg.astype(F32)
    factor = jnp.concatenate([gain_weights, gain_weights], axis=1)
    sums[0] = jnp.sum(hg_wide * factor, axis=0, keepdims=True)
    sums[1] = jnp.sum(hg_wide * wide, axis=0, keepdims=True)
    sums_over = remote(sums, spair, ssend.at[1], srecv.at[3], partner)
    sums_over.start()

    def core_copy(shift, line_of):
        chip = line_of * 4 + place_at(shift)
        slot = shift * 2 + line_of
        return remote(
            ws_ref.at[chip * 2 + 1 - core],
            cland.at[shift, line_of],
            csend.at[0],
            crecv.at[slot],
            mate,
        )

    def core_sum(shift, line_of):
        chip = line_of * 4 + place_at(shift)
        core_copy(shift, line_of).wait_recv()
        both = cland[shift, line_of].astype(F32) + ws_ref[chip * 2 + core].astype(F32)
        cland[shift, line_of] = both.astype(BF16)

    def place_copy(shift, line_of):
        up = shift == 1 or (shift == 2 and line_of == 0)
        land = mland.at[line_of] if shift == 2 else xland.at[0 if up else 1, line_of]
        return remote(
            cland.at[shift, line_of],
            land,
            xsend.at[0],
            xrecv.at[shift * 2 - 2 + line_of],
            at_dp(0, 1 if up else 3, 0),
        )

    def merge(shift, line_of):
        place_copy(2, line_of).wait_recv()
        both = cland[shift, line_of].astype(F32) + mland[line_of].astype(F32)
        cland[shift, line_of] = both.astype(BF16)
        place_copy(shift, line_of).start()

    hgt_ref[...] = hg.T

    def share(shift):
        for line_of in (0, 1):
            chip = line_of * 4 + place_at(shift)
            block = dot(nt_ref[pl.ds(chip * 4, 4)].reshape(4 * FEAT, PATCHES), hgt_ref[...])
            ws_ref[pl.ds(chip * 2, 2)] = block.astype(BF16).reshape(2, ROWS, 3 * HDIM)
            core_copy(shift, line_of).start()

    share(2)
    share(1)
    all_landed("other", oland, 2)
    for which, sign in enumerate((1, -1)):
        total = pull_ref[theirs + along(-6 * sign)].astype(F32) + oland[which].astype(F32)
        pull_ref[theirs + along(-6 * sign)] = total.astype(BF16)
        back_over(6 * sign).start()
    for offset in NEAR + (3, -3, 1, -1, 0):
        back_over(offset).start()
    share(3)
    for offset in (8, 7, -7):
        pass_on(offset, gathered(offset, ()))
    share(0)
    for shift in (2, 1, 3):
        core_sum(shift, 0)
        core_sum(shift, 1)
        if shift == 2:
            place_copy(2, 0).start()
            place_copy(2, 1).start()
    place_copy(1, 1).start()
    place_copy(3, 0).start()
    sums_over.wait_recv()
    spair[...] = spair[...] + sums[...]
    for offset in FAR + NEAR + (1, -1):
        back_sums(offset, spair).start()
    att_ref[...] = dot(values, soft_r).T.astype(BF16)
    att_copy = pltpu.make_async_copy(att_ref, att_any, local.at[3])
    att_copy.start()

    def eighth(sign):
        return (1 - core if sign > 0 else core).astype(F32)

    all_landed("z far", zland, len(FAR))
    for sign in (1, -1):
        total = gathered(6 * sign, ())
        for offset in (5 * sign, 7 * sign):
            total = total + zland[offset % NZ].astype(F32)
        pass_on(6 * sign, total + eighth(sign) * zland[8].astype(F32))
    sums_landed(0, len(FAR))
    for which, sign in enumerate((1, -1)):
        total = spair[...] + eighth(sign) * sland[8]
        spart[which] = total + sland[(5 * sign) % NZ] + sland[(7 * sign) % NZ]
        back_sums(6 * sign, spart.at[which]).start()
    for offset in NEAR:
        pass_on(offset, gathered(offset, ()))
    merge(1, 0)
    merge(3, 1)
    for offset in (1, -1):
        pass_on(offset, gathered(offset, ()))
    core_sum(0, 0)
    core_sum(0, 1)
    for sign in (1, -1):
        pass_on(3 * sign, gathered(3 * sign, (2 * sign, 4 * sign, 6 * sign)))
    sums_landed(1, 6)
    for which, sign in enumerate((1, -1)):
        total = spair[...]
        for offset in (2 * sign, 4 * sign, 6 * sign):
            total = total + sland[offset % NZ]
        spart[2 + which] = total
        back_sums(3 * sign, spart.at[2 + which]).start()
    for shift in (1, 3):
        place_copy(shift, 0).wait_recv()
        place_copy(shift, 1).wait_recv()
    far = cland[0, 1 - line].astype(F32)
    for side in (0, 1):
        far = far + xland[side, 1 - line].astype(F32)
    hstage[...] = far.astype(BF16)
    line_copy = remote(hstage, hland, hsend.at[0], hrecv.at[0], across_line)
    line_copy.start()
    near = cland[0, line].astype(F32)
    for side in (0, 1):
        near = near + xland[side, line].astype(F32)
    wg_ref[...] = near

    normed = (g_ref[mp].astype(F32) - average) * inverse
    pull = gathered(0, (1, -1, 3, -3))
    product = pull * normed
    turned = (product[:, :128] + product[:, 128:]).T
    gstage[...] = jnp.concatenate(
        [jnp.sum(turned, axis=0, keepdims=True), jnp.zeros((1, 128 - FEAT), F32)], axis=1
    )

    for i, steps in enumerate(others):
        remote(gstage, gland.at[i], gsend.at[0], grecv.at[0], at_dp(*steps)).start()
    sums_landed(2, 4)
    sum_all = spair[...]
    for offset in (1, -1, 3, -3):
        sum_all = sum_all + sland[offset % NZ]
    own_gain = gb_ref[mp].astype(F32)
    scaled = pull * jnp.concatenate([own_gain, own_gain], axis=1)
    ig_ref[...] = (
        inverse * (scaled - sum_all[0] * (1.0 / D) - normed * (sum_all[1] * (1.0 / D)))
    ).astype(BF16)
    ig_copy = pltpu.make_async_copy(ig_ref, ig_any, local.at[4])
    ig_copy.start()
    line_copy.wait_recv()
    wg_ref[...] += hland[...].astype(F32)
    wg_copy = pltpu.make_async_copy(wg_ref, wg_any, local.at[5])
    wg_copy.start()
    Both("z far", partner, 0, NMP - 1).wait_send()
    part = pull_ref.at[pl.ds(0, 15 + 14 + 2)]
    scatter_copy("z far", part, part, partner).wait_send()
    part = sland.at[pl.ds(0, NZ - 1)]
    remote(part, part, ssend.at[0], srecv.at[0], partner).wait_send()
    sums_over.wait_send()
    part = ws_ref.at[pl.ds(0, 8)]
    remote(part, part, csend.at[0], crecv.at[0], mate).wait_send()
    part = ws_ref.at[pl.ds(0, 6)]
    remote(part, part, xsend.at[0], xrecv.at[0], mate).wait_send()
    line_copy.wait_send()
    remote(gland, gland, gsend.at[0], grecv.at[0], mate).wait()
    gain_total = gstage[...]
    for i in range(len(others)):
        gain_total = gain_total + gland[i]
    gg_ref[...] = gain_total
    att_copy.wait()
    ig_copy.wait()
    wg_copy.wait()


def fused(x, gain, weights, out_grad):
    dma = pltpu.SemaphoreType.DMA
    return pl.pallas_call(
        fused_kernel,
        out_shape=(
            jax.ShapeDtypeStruct((PATCHES, HDIM), BF16),
            jax.ShapeDtypeStruct((FEAT, PATCHES), BF16),
            jax.ShapeDtypeStruct((ROWS, 3 * HDIM), F32),
            jax.ShapeDtypeStruct((1, 128), F32),
        ),
        in_specs=[
            pl.BlockSpec(memory_space=pltpu.HBM),
            pl.BlockSpec(memory_space=VMEM),
            pl.BlockSpec(memory_space=pltpu.HBM),
            pl.BlockSpec(memory_space=pltpu.HBM),
        ],
        out_specs=(
            pl.BlockSpec(memory_space=pltpu.HBM),
            pl.BlockSpec(memory_space=pltpu.HBM),
            pl.BlockSpec(memory_space=pltpu.HBM),
            pl.BlockSpec(memory_space=VMEM),
        ),
        scratch_shapes=[
            VMEM((PATCHES, HDIM), BF16),
            VMEM((FEAT, PATCHES), BF16),
            VMEM((ROWS, 3 * HDIM), F32),
            VMEM((D, 3 * HDIM), BF16),
            VMEM((PATCHES, HDIM), BF16),
            VMEM((NMP, FEAT, PATCHES), BF16),
            VMEM((NMP, 1, 128), F32),
            VMEM((3 * HDIM, D), BF16),
            VMEM((NZ, 128), F32),
            VMEM((NMP, FEAT, 128), BF16),
            VMEM((NMP, FEAT, PATCHES), BF16),
            VMEM((3 * HDIM, PATCHES), BF16),
            VMEM((PATCHES, 3 * HDIM), BF16),
            VMEM((NMP, FEAT, PATCHES), BF16),
            VMEM((2 * CHIPS, ROWS, 3 * HDIM), BF16),
            VMEM((NZ, FEAT, PATCHES), BF16),
            VMEM((NZ, FEAT, PATCHES), BF16),
            VMEM((2, FEAT, PATCHES), BF16),
            VMEM((2, 1, PATCHES), F32),
            VMEM((2, 1, PATCHES), F32),
            VMEM((NZ, 2, 1, PATCHES), F32),
            VMEM((4, 2, 1, PATCHES), F32),
            VMEM((4, 2, ROWS, 3 * HDIM), BF16),
            VMEM((2, ROWS, 3 * HDIM), BF16),
            VMEM((2, 2, ROWS, 3 * HDIM), BF16),
            VMEM((ROWS, 3 * HDIM), BF16),
            VMEM((ROWS, 3 * HDIM), BF16),
            VMEM((1, 128), F32),
            VMEM((2 * CHIPS - 1, 1, 128), F32),
            dma((6,)),
            dma((2,)),
            dma((2, len(GATHER_SLOTS))),
            dma((1,)),
            dma((len(SCATTER_SLOTS),)),
            dma((2,)),
            dma((4,)),
            dma((1,)),
            dma((8,)),
            dma((1,)),
            dma((6,)),
            dma((1,)),
            dma((1,)),
            dma((1,)),
            dma((1,)),
        ],
        compiler_params=pltpu.CompilerParams(
            collective_id=0, has_side_effects=True, vmem_limit_bytes=56 << 20
        ),
    )(x, gain, weights, out_grad)


def finish_kernel(
    att_in, ig_in, wg_in, gg_in, att_ref, ig_ref, wg_ref, gg_ref, att, ig, wg, local
):
    loads = [
        pltpu.make_async_copy(source, held, local.at[i])
        for i, (source, held) in enumerate(((wg_in, wg), (att_in, att), (ig_in, ig)))
    ]
    for load in loads:
        load.start()
    stores = [
        pltpu.make_async_copy(held, target, local.at[3 + i])
        for i, (held, target) in enumerate(((wg, wg_ref.at[:, 0, :]), (att, att_ref), (ig, ig_ref)))
    ]
    gg_ref[...] = gg_in[:, :FEAT]
    for load, store in zip(loads, stores):
        load.wait()
        store.start()
    for store in stores:
        store.wait()


def finish(attended, input_grad, weight_grad, gain_grad):
    hbm, vmem = pl.BlockSpec(memory_space=pltpu.HBM), pl.BlockSpec(memory_space=VMEM)
    return pl.pallas_call(
        finish_kernel,
        out_shape=(
            jax.ShapeDtypeStruct((PATCHES, HDIM), BF16),
            jax.ShapeDtypeStruct((FEAT, PATCHES), BF16),
            jax.ShapeDtypeStruct((ROWS, 1, 3 * HDIM), F32),
            jax.ShapeDtypeStruct((1, FEAT), F32),
        ),
        in_specs=[hbm, hbm, hbm, vmem],
        out_specs=(hbm, hbm, hbm, vmem),
        scratch_shapes=[
            VMEM((PATCHES, HDIM), BF16),
            VMEM((FEAT, PATCHES), BF16),
            VMEM((ROWS, 3 * HDIM), F32),
            pltpu.SemaphoreType.DMA((6,)),
        ],
        compiler_params=pltpu.CompilerParams(vmem_limit_bytes=56 << 20),
    )(attended, input_grad, weight_grad, gain_grad)


def on_device(tokens, gain, w_qkv, out_grad):
    attended, input_grad, weight_grad, gain_grad = finish(
        *fused(tokens.T, gain.reshape(1, FEAT), w_qkv[:, 0, :], out_grad)
    )
    return attended, input_grad.T, weight_grad, gain_grad.reshape(FEAT)


def solution(mesh):
    in_specs = (P("dp", "mp"), P("mp"), P(None, "mp", None), P("dp", "mp"))
    out_specs = (P("dp", "mp"), P("dp", "mp"), P("dp", "mp", None), P("mp"))
    return jax.shard_map(
        on_device, mesh=mesh, in_specs=in_specs, out_specs=out_specs, check_vma=False
    )
```

```python
import math

import jax
import jax.numpy as jnp
from jax import lax
from jax.experimental import pallas as pl
from jax.experimental.pallas import tpu as pltpu
from jax.sharding import PartitionSpec as P

D = 3072
PATCHES = 256
HDIM = 128
FEAT = 96
NZ = 16
NY = 2
NMP = NZ * NY
CHIPS = 8
ROWS = 192
EPS = 1e-06
F32 = jnp.float32
BF16 = jnp.bfloat16
MESH = pl.DeviceIdType.MESH
VMEM = pltpu.VMEM


def remote(src, dst, send_sem, recv_sem, target):
    return pltpu.make_async_remote_copy(
        src_ref=src,
        dst_ref=dst,
        send_sem=send_sem,
        recv_sem=recv_sem,
        device_id=target,
        device_id_type=MESH,
    )


def folded(matrix):
    return jnp.sum(matrix.reshape(matrix.shape[0] // 8, 8, matrix.shape[1]), axis=0)


def column_mean(matrix):
    return jnp.sum(matrix, axis=0, keepdims=True) * (1.0 / matrix.shape[0])


def unit_columns(matrix):
    centred = matrix - column_mean(matrix)
    inverse = lax.rsqrt(column_mean(centred * centred) + EPS)
    return centred * inverse, inverse


def unit_pullback(normal, inverse, cotangent):
    return inverse * (
        cotangent - column_mean(cotangent) - normal * column_mean(cotangent * normal)
    )


def dot(a, b):
    return jnp.dot(a, b, preferred_element_type=F32)


def dot_rows(a, b):
    return lax.dot_general(a, b, (((1,), (1,)), ((), ())), preferred_element_type=F32)


def hub_of(offset):
    sign = 1 if offset > 0 else -1
    return sign * {1: 0, 3: 0, 2: 3, 4: 3, 6: 3, 5: 6, 7: 6}[abs(offset)]


FAR = (5, -5, 7, -7, 8)
FIVES = (5, -5)
NEAR = (2, -2, 4, -4)
HALVES = (0, 1)
GATHER_SLOTS = (
    *(("z", offset, half) for offset in (3, -3, 6, -6) for half in HALVES),
    *(("z", offset, None) for offset in (1, -1) + NEAR),
    *(("y", offset, half) for offset in (6, -6) for half in HALVES),
    "z far",
    "y near",
    "other",
)
SCATTER_SLOTS = (
    *(("z", offset, half) for offset in (6, -6, 3, -3) for half in HALVES),
    *(("z", offset, None) for offset in NEAR + (1, -1)),
    *(("y", offset, half) for offset in (8, 7, -7) for half in HALVES),
    *(("y", offset, None) for offset in (6, -6, 3, -3, 1, -1, 0) + NEAR),
    *(("z far", half) for half in HALVES),
    "other",
)


def rows_of(half):
    return slice(None) if half is None else pl.ds(half * (FEAT // 2), FEAT // 2)


def fused_kernel(
    x_any,
    gain_ref,
    w_any,
    do_any,
    att_any,
    ig_any,
    wg_any,
    gg_ref,
    att_ref,
    ig_ref,
    wg_ref,
    w_ref,
    do_ref,
    g_ref,
    gains,
    wt_ref,
    rows_ref,
    gb_ref,
    nt_ref,
    hg_ref,
    hgt_ref,
    pull_ref,
    ws_ref,
    zland,
    yland,
    oland,
    sums,
    spair,
    sland,
    spart,
    cland,
    mland,
    xland,
    hland,
    hstage,
    gstage,
    gland,
    local,
    bsend,
    brecv,
    rsend,
    rrecv,
    ssend,
    srecv,
    csend,
    crecv,
    xsend,
    xrecv,
    hsend,
    hrecv,
    gsend,
    grecv,
):
    mp = lax.axis_index("mp")
    row, z = mp // NZ, mp % NZ
    dp = lax.axis_index("dp")
    line, place, core = dp // 8, (dp // 2) % 4, dp % 2
    sign8 = 1 - 2 * core
    mine, theirs = row * NZ, (1 - row) * NZ
    partner = {"mp": theirs + z}

    def along(offset):
        return (z + offset + 2 * NZ) % NZ

    def at_z(offset):
        return {"mp": mine + along(offset)}

    def at_dp(lines, places, cores):
        return {"dp": (((line + lines) % 2) * 4 + place_at(places)) * 2 + (core + cores) % 2}

    def place_at(shift):
        return (place + shift) % 4

    def hub(offset):
        return 6 * sign8 if offset == 8 else hub_of(offset)

    mate = at_dp(0, 0, 1)
    across_line = at_dp(1, 0, 0)
    others = [(i, j, k) for i in (0, 1) for j in range(4) for k in (0, 1) if i + j + k > 0]

    own_copy = pltpu.make_async_copy(x_any, g_ref.at[mp], local.at[0])
    w_copy = pltpu.make_async_copy(w_any, w_ref, local.at[1])
    do_copy = pltpu.make_async_copy(do_any, do_ref, local.at[2])
    own_copy.start()
    barrier = pltpu.get_barrier_semaphore()
    peers = [at_z(offset) for offset in (3, -3, 2, -2, 1, -1)] + [partner]
    peers += [at_dp(*steps) for steps in others]
    for peer in peers:
        pl.semaphore_signal(barrier, inc=1, device_id=peer, device_id_type=MESH)
    w_copy.start()
    do_copy.start()
    gains[mp] = jnp.concatenate(
        [gain_ref[...].astype(F32), jnp.zeros((1, 128 - FEAT), F32)], axis=1
    )
    own_copy.wait()
    pl.semaphore_wait(barrier, len(peers))

    class Both:
        def __init__(self, key, target, block, half=None):
            slot = GATHER_SLOTS.index(key)
            part = g_ref.at[block, rows_of(half)]
            self.copies = [remote(part, part, bsend.at[0], brecv.at[0, slot], target)]
            if half != 1:
                part = gains.at[block]
                self.copies.append(remote(part, part, bsend.at[1], brecv.at[1, slot], target))

        def start(self):
            for copy in self.copies:
                copy.start()

        def wait_send(self):
            for copy in self.copies:
                copy.wait_send()

        def wait_recv(self):
            for copy in self.copies:
                copy.wait_recv()

    def spread(offset, half=None):
        key = "z far" if offset in FAR else ("z", offset, half)
        return Both(key, at_z(offset - hub(offset)), mine + along(-hub(offset)), half)

    def arrived(offset, half=None):
        Both(("z", offset, half), at_z(1), mine + along(-offset), half).wait_recv()

    def over(offset, half=None):
        key = ("y", offset, half) if abs(offset) == 6 else "y near"
        return Both(key, partner, mine + along(-offset), half)

    def over_arrived(offset, half=None):
        Both(("y", offset, half), partner, theirs + along(-offset), half).wait_recv()

    def other(offset, half=None):
        return Both("other", at_z(offset - hub(offset)), theirs + along(-hub(offset)), half)

    def all_arrived(key, count):
        Both(key, partner, pl.ds(0, count)).wait_recv()

    for half in HALVES:
        for offset in (3, -3):
            spread(offset, half).start()
    over(0).start()
    for offset in (1, -1):
        spread(offset).start()
    w_copy.wait()
    for part in range(D // 256):
        wt_ref[:, part * 256 : (part + 1) * 256] = w_ref[part * 256 : (part + 1) * 256, :].T
    do_copy.wait()
    cotangent = do_ref[...].T
    for half in HALVES:
        for sign in (1, -1):
            arrived(3 * sign, half)
            spread(6 * sign, half).start()
    for sign in (1, -1):
        spread(4 * sign).start()
        spread(2 * sign).start()
        over(3 * sign).start()
    for offset in (1, -1):
        arrived(offset)
        over(offset).start()
    for half in HALVES:
        for sign in (1, -1):
            arrived(6 * sign, half)
            over(6 * sign, half).start()
            spread(5 * sign, half).start()
            spread(7 * sign, half).start()
        spread(8, half).start()
    for offset in NEAR:
        arrived(offset)
        over(offset).start()
    for half in HALVES:
        for sign in (1, -1):
            over_arrived(6 * sign, half)
            other(5 * sign, half).start()
            other(7 * sign, half).start()
        other(8, half).start()
    all_arrived("z far", len(FAR))

    shift_row = jnp.sum(g_ref[mp].astype(F32), axis=0, keepdims=True) * (1.0 / FEAT)

    def add_block(block, totals):
        moved = g_ref[block].astype(F32) - shift_row
        return totals[0] + folded(moved), totals[1] + folded(moved * moved)

    def gain_columns(start):
        for i in range(NZ):
            rows_ref[i : i + 1, :] = gains[start + i]
        turned = rows_ref[...].T
        for i in range(NZ):
            gb_ref[start + i] = jnp.broadcast_to(turned[:FEAT, i : i + 1], (FEAT, 128)).astype(BF16)

    def gain_product(start):
        half = NZ * FEAT
        columns = pl.ds(pl.multiple_of(start * FEAT, half), half)
        return dot(wt_ref[:, columns], gb_ref[pl.ds(start, NZ)].reshape(half, 128))

    zero = jnp.zeros((8, PATCHES), F32)
    totals = lax.fori_loop(mine, mine + NZ, add_block, (zero, zero))
    gain_columns(mine)
    gain_weights = gain_product(mine)
    all_arrived("y near", 9)
    for offset in (0, 1, -1, 2, -2, 3, -3, 4, -4, 6, -6):
        totals = add_block(theirs + along(-offset), totals)
    all_arrived("other", len(FAR))
    gain_columns(theirs)
    for offset in FAR:
        totals = add_block(theirs + along(-offset), totals)
    first = jnp.sum(totals[0], axis=0, keepdims=True) * (1.0 / D)
    second = jnp.sum(totals[1], axis=0, keepdims=True) * (1.0 / D)
    average = shift_row + first
    inverse = lax.rsqrt(second - first * first + EPS)

    def normalize(block, carry):
        factor = gb_ref[block].astype(F32)
        factor = jnp.concatenate([factor, factor], axis=1)
        normed = (g_ref[block].astype(F32) - average) * inverse
        nt_ref[block] = (normed * factor).astype(BF16)
        return carry

    lax.fori_loop(0, NMP, normalize, 0)

    wide = dot(wt_ref[...], nt_ref[...].reshape(D, PATCHES))
    projected = wide.astype(BF16)
    query, query_inverse = unit_columns(projected[:HDIM].astype(F32))
    keys, keys_inverse = unit_columns(projected[HDIM : 2 * HDIM].astype(F32))
    values = projected[2 * HDIM :]
    query_r, keys_r = query.astype(BF16), keys.astype(BF16)
    scale = 1.0 / math.sqrt(HDIM)
    exponent = jnp.exp(dot(keys_r.T, query_r) * scale)
    soft = exponent / jnp.sum(exponent, axis=0, keepdims=True)
    soft_r = soft.astype(BF16)
    soft_grad = dot(values.T, cotangent)
    values_grad = dot_rows(cotangent, soft_r)
    score_grad = soft * (soft_grad - jnp.sum(soft * soft_grad, axis=0, keepdims=True))
    score_grad = (score_grad * scale).astype(BF16)
    query_grad = unit_pullback(query, query_inverse, dot(keys_r, score_grad))
    keys_grad = unit_pullback(keys, keys_inverse, dot_rows(query_r, score_grad))
    hg = jnp.concatenate([query_grad, keys_grad, values_grad], axis=0).astype(BF16)
    hg_ref[...] = hg

    def pull_rows(start):
        def pull_part(part, carry):
            block = start + part * 8
            rows = pl.ds(pl.multiple_of(block * FEAT, 8 * FEAT), 8 * FEAT)
            pull_ref[pl.ds(block, 8)] = (
                dot(w_ref[rows, :], hg_ref[...]).astype(BF16).reshape(8, FEAT, PATCHES)
            )
            return carry

        lax.fori_loop(0, 2, pull_part, 0)

    def scatter_copy(key, src, dst, target):
        return remote(src, dst, rsend.at[0], rrecv.at[SCATTER_SLOTS.index(key)], target)

    def back_over(offset, half=None):
        rows = rows_of(half)
        src = pull_ref.at[theirs + along(-offset), rows]
        return scatter_copy(("y", offset, half), src, yland.at[offset % NZ, rows], partner)

    def back_other(offset):
        src = pull_ref.at[theirs + along(-offset)]
        return scatter_copy("other", src, oland.at[FIVES.index(offset)], at_z(hub(offset) - offset))

    def back(offset, half=None):
        rows = rows_of(half)
        key = ("z far", half) if offset in FAR else ("z", offset, half)
        src = pull_ref.at[mine + along(-offset), rows]
        return scatter_copy(key, src, zland.at[offset % NZ, rows], at_z(hub(offset) - offset))

    def all_landed(key, part):
        scatter_copy(key, part, part, partner).wait_recv()

    def back_sums(offset, src):
        stage = 0 if offset in FAR else (2 if abs(offset) in (1, 3) else 1)
        return remote(
            src,
            sland.at[offset % NZ],
            ssend.at[0],
            srecv.at[stage],
            at_z(hub(offset) - offset),
        )

    def sums_landed(stage, count):
        part = sland.at[pl.ds(0, count)]
        remote(part, part, ssend.at[0], srecv.at[stage], partner).wait_recv()

    def part_of(ref, block, half):
        return ref[block, rows_of(half)].astype(F32)

    def gathered(offset, half, over_half, inputs):
        total = part_of(pull_ref, mine + along(-offset), half)
        if over_half == half:
            back_over(offset, half).wait_recv()
        total = total + part_of(yland, offset % NZ, half)
        for at, at_half in inputs:
            if at_half == half:
                back(at, half).wait_recv()
            total = total + part_of(zland, at % NZ, half)
        return total

    def pass_on(offset, half, total):
        pull_ref[mine + along(-offset), rows_of(half)] = total.astype(BF16)
        back(offset, half).start()

    pull_rows(theirs)
    for offset in FIVES:
        back_other(offset).start()
    for half in HALVES:
        for offset in (8, 7, -7):
            back_over(offset, half).start()
    pull_rows(mine)
    for half in HALVES:
        for offset in FIVES:
            back(offset, half).start()
    gain_weights = gain_weights + gain_product(theirs)
    hg_wide = hg.astype(F32)
    factor = jnp.concatenate([gain_weights, gain_weights], axis=1)
    sums[0] = jnp.sum(hg_wide * factor, axis=0, keepdims=True)
    sums[1] = jnp.sum(hg_wide * wide, axis=0, keepdims=True)
    sums_over = remote(sums, spair, ssend.at[1], srecv.at[3], partner)
    sums_over.start()

    def core_copy(shift, line_of):
        chip = line_of * 4 + place_at(shift)
        slot = shift * 2 + line_of
        return remote(
            ws_ref.at[chip * 2 + 1 - core],
            cland.at[shift, line_of],
            csend.at[0],
            crecv.at[slot],
            mate,
        )

    def core_sum(shift, line_of):
        chip = line_of * 4 + place_at(shift)
        core_copy(shift, line_of).wait_recv()
        both = cland[shift, line_of].astype(F32) + ws_ref[chip * 2 + core].astype(F32)
        cland[shift, line_of] = both.astype(BF16)

    def place_copy(shift, line_of):
        up = shift == 1 or (shift == 2 and line_of == 0)
        land = mland.at[line_of] if shift == 2 else xland.at[0 if up else 1, line_of]
        return remote(
            cland.at[shift, line_of],
            land,
            xsend.at[0],
            xrecv.at[shift * 2 - 2 + line_of],
            at_dp(0, 1 if up else 3, 0),
        )

    def merge(shift, line_of):
        place_copy(2, line_of).wait_recv()
        both = cland[shift, line_of].astype(F32) + mland[line_of].astype(F32)
        cland[shift, line_of] = both.astype(BF16)
        place_copy(shift, line_of).start()

    hgt_ref[...] = hg.T

    def share(shift):
        for line_of in (0, 1):
            chip = line_of * 4 + place_at(shift)
            block = dot(nt_ref[pl.ds(chip * 4, 4)].reshape(4 * FEAT, PATCHES), hgt_ref[...])
            ws_ref[pl.ds(chip * 2, 2)] = block.astype(BF16).reshape(2, ROWS, 3 * HDIM)
            core_copy(shift, line_of).start()

    share(2)
    share(1)
    all_landed("other", oland)
    for which, sign in enumerate((1, -1)):
        total = pull_ref[theirs + along(-6 * sign)].astype(F32) + oland[which].astype(F32)
        pull_ref[theirs + along(-6 * sign)] = total.astype(BF16)
        back_over(6 * sign).start()
    for offset in NEAR + (3, -3, 1, -1, 0):
        back_over(offset).start()
    share(3)
    for half in HALVES:
        for offset in (8, 7, -7):
            pass_on(offset, half, gathered(offset, half, half, ()))
    share(0)
    for shift in (2, 1, 3):
        core_sum(shift, 0)
        core_sum(shift, 1)
        if shift == 2:
            place_copy(2, 0).start()
            place_copy(2, 1).start()
    place_copy(1, 1).start()
    place_copy(3, 0).start()
    sums_over.wait_recv()
    spair[...] = spair[...] + sums[...]
    for offset in FAR + NEAR + (1, -1):
        back_sums(offset, spair).start()
    att_ref[...] = dot(values, soft_r).T.astype(BF16)
    att_copy = pltpu.make_async_copy(att_ref, att_any, local.at[3])
    att_copy.start()

    def eighth(sign):
        return (1 - core if sign > 0 else core).astype(F32)

    back_over(6).wait_recv()
    back_over(-6).wait_recv()
    for half in HALVES:
        all_landed(("z far", half), zland.at[pl.ds(0, len(FAR)), rows_of(half)])
        for sign in (1, -1):
            total = gathered(6 * sign, half, -1, ((5 * sign, -1), (7 * sign, -1)))
            pass_on(6 * sign, half, total + eighth(sign) * part_of(zland, 8, half))
    sums_landed(0, len(FAR))
    for which, sign in enumerate((1, -1)):
        total = spair[...] + eighth(sign) * sland[8]
        spart[which] = total + sland[(5 * sign) % NZ] + sland[(7 * sign) % NZ]
        back_sums(6 * sign, spart.at[which]).start()
    for offset in NEAR:
        pass_on(offset, None, gathered(offset, None, None, ()))
    merge(1, 0)
    merge(3, 1)
    for offset in (1, -1):
        pass_on(offset, None, gathered(offset, None, None, ()))
    core_sum(0, 0)
    core_sum(0, 1)
    for sign in (1, -1):
        back_over(3 * sign).wait_recv()
        back(2 * sign).wait_recv()
        back(4 * sign).wait_recv()
    for half in HALVES:
        for sign in (1, -1):
            inputs = ((2 * sign, -1), (4 * sign, -1), (6 * sign, half))
            pass_on(3 * sign, half, gathered(3 * sign, half, -1, inputs))
    sums_landed(1, 6)
    for which, sign in enumerate((1, -1)):
        total = spair[...]
        for offset in (2 * sign, 4 * sign, 6 * sign):
            total = total + sland[offset % NZ]
        spart[2 + which] = total
        back_sums(3 * sign, spart.at[2 + which]).start()
    for shift in (1, 3):
        place_copy(shift, 0).wait_recv()
        place_copy(shift, 1).wait_recv()
    far = cland[0, 1 - line].astype(F32)
    for side in (0, 1):
        far = far + xland[side, 1 - line].astype(F32)
    hstage[...] = far.astype(BF16)
    line_copy = remote(hstage, hland, hsend.at[0], hrecv.at[0], across_line)
    line_copy.start()
    near = cland[0, line].astype(F32)
    for side in (0, 1):
        near = near + xland[side, line].astype(F32)
    wg_ref[...] = near

    normed = (g_ref[mp].astype(F32) - average) * inverse
    pull = gathered(0, None, None, ((1, None), (-1, None)))
    for offset in (3, -3):
        for half in HALVES:
            back(offset, half).wait_recv()
        pull = pull + part_of(zland, offset % NZ, None)
    product = pull * normed
    turned = (product[:, :128] + product[:, 128:]).T
    gstage[...] = jnp.concatenate(
        [jnp.sum(turned, axis=0, keepdims=True), jnp.zeros((1, 128 - FEAT), F32)], axis=1
    )

    for i, steps in enumerate(others):
        remote(gstage, gland.at[i], gsend.at[0], grecv.at[0], at_dp(*steps)).start()
    sums_landed(2, 4)
    sum_all = spair[...]
    for offset in (1, -1, 3, -3):
        sum_all = sum_all + sland[offset % NZ]
    own_gain = gb_ref[mp].astype(F32)
    scaled = pull * jnp.concatenate([own_gain, own_gain], axis=1)
    ig_ref[...] = (
        inverse * (scaled - sum_all[0] * (1.0 / D) - normed * (sum_all[1] * (1.0 / D)))
    ).astype(BF16)
    ig_copy = pltpu.make_async_copy(ig_ref, ig_any, local.at[4])
    ig_copy.start()
    line_copy.wait_recv()
    wg_ref[...] += hland[...].astype(F32)
    wg_copy = pltpu.make_async_copy(wg_ref, wg_any, local.at[5])
    wg_copy.start()
    Both("z far", partner, pl.ds(0, NMP - 1)).wait_send()
    part = pull_ref.at[pl.ds(0, 15 + 14 + 2)]
    scatter_copy("other", part, part, partner).wait_send()
    part = sland.at[pl.ds(0, NZ - 1)]
    remote(part, part, ssend.at[0], srecv.at[0], partner).wait_send()
    sums_over.wait_send()
    part = ws_ref.at[pl.ds(0, 8)]
    remote(part, part, csend.at[0], crecv.at[0], mate).wait_send()
    part = ws_ref.at[pl.ds(0, 6)]
    remote(part, part, xsend.at[0], xrecv.at[0], mate).wait_send()
    line_copy.wait_send()
    remote(gland, gland, gsend.at[0], grecv.at[0], mate).wait()
    gain_total = gstage[...]
    for i in range(len(others)):
        gain_total = gain_total + gland[i]
    gg_ref[...] = gain_total
    att_copy.wait()
    ig_copy.wait()
    wg_copy.wait()


def fused(x, gain, weights, out_grad):
    dma = pltpu.SemaphoreType.DMA
    return pl.pallas_call(
        fused_kernel,
        out_shape=(
            jax.ShapeDtypeStruct((PATCHES, HDIM), BF16),
            jax.ShapeDtypeStruct((FEAT, PATCHES), BF16),
            jax.ShapeDtypeStruct((ROWS, 3 * HDIM), F32),
            jax.ShapeDtypeStruct((1, 128), F32),
        ),
        in_specs=[
            pl.BlockSpec(memory_space=pltpu.HBM),
            pl.BlockSpec(memory_space=VMEM),
            pl.BlockSpec(memory_space=pltpu.HBM),
            pl.BlockSpec(memory_space=pltpu.HBM),
        ],
        out_specs=(
            pl.BlockSpec(memory_space=pltpu.HBM),
            pl.BlockSpec(memory_space=pltpu.HBM),
            pl.BlockSpec(memory_space=pltpu.HBM),
            pl.BlockSpec(memory_space=VMEM),
        ),
        scratch_shapes=[
            VMEM((PATCHES, HDIM), BF16),
            VMEM((FEAT, PATCHES), BF16),
            VMEM((ROWS, 3 * HDIM), F32),
            VMEM((D, 3 * HDIM), BF16),
            VMEM((PATCHES, HDIM), BF16),
            VMEM((NMP, FEAT, PATCHES), BF16),
            VMEM((NMP, 1, 128), F32),
            VMEM((3 * HDIM, D), BF16),
            VMEM((NZ, 128), F32),
            VMEM((NMP, FEAT, 128), BF16),
            VMEM((NMP, FEAT, PATCHES), BF16),
            VMEM((3 * HDIM, PATCHES), BF16),
            VMEM((PATCHES, 3 * HDIM), BF16),
            VMEM((NMP, FEAT, PATCHES), BF16),
            VMEM((2 * CHIPS, ROWS, 3 * HDIM), BF16),
            VMEM((NZ, FEAT, PATCHES), BF16),
            VMEM((NZ, FEAT, PATCHES), BF16),
            VMEM((2, FEAT, PATCHES), BF16),
            VMEM((2, 1, PATCHES), F32),
            VMEM((2, 1, PATCHES), F32),
            VMEM((NZ, 2, 1, PATCHES), F32),
            VMEM((4, 2, 1, PATCHES), F32),
            VMEM((4, 2, ROWS, 3 * HDIM), BF16),
            VMEM((2, ROWS, 3 * HDIM), BF16),
            VMEM((2, 2, ROWS, 3 * HDIM), BF16),
            VMEM((ROWS, 3 * HDIM), BF16),
            VMEM((ROWS, 3 * HDIM), BF16),
            VMEM((1, 128), F32),
            VMEM((2 * CHIPS - 1, 1, 128), F32),
            dma((6,)),
            dma((2,)),
            dma((2, len(GATHER_SLOTS))),
            dma((1,)),
            dma((len(SCATTER_SLOTS),)),
            dma((2,)),
            dma((4,)),
            dma((1,)),
            dma((8,)),
            dma((1,)),
            dma((6,)),
            dma((1,)),
            dma((1,)),
            dma((1,)),
            dma((1,)),
        ],
        compiler_params=pltpu.CompilerParams(
            collective_id=0, has_side_effects=True, vmem_limit_bytes=56 << 20
        ),
    )(x, gain, weights, out_grad)


def finish_kernel(
    att_in, ig_in, wg_in, gg_in, att_ref, ig_ref, wg_ref, gg_ref, att, ig, wg, gg, ggs, local
):
    moves = (
        (wg_in, wg, wg, wg_ref.at[:, 0, :]),
        (att_in, att, att, att_ref),
        (gg_in, gg, ggs, gg_ref),
        (ig_in, ig, ig, ig_ref),
    )
    loads = [
        pltpu.make_async_copy(move[0], move[1], local.at[0, i]) for i, move in enumerate(moves)
    ]
    stores = [
        pltpu.make_async_copy(move[2], move[3], local.at[1, i]) for i, move in enumerate(moves)
    ]
    for load in loads:
        load.start()
    for i in range(4):
        loads[i].wait()
        if i == 2:
            ggs[...] = gg[:, :FEAT]
        stores[i].start()
    for store in stores:
        store.wait()


def finish(attended, input_grad, weight_grad, gain_grad):
    hbm = pl.BlockSpec(memory_space=pltpu.HBM)
    return pl.pallas_call(
        finish_kernel,
        out_shape=(
            jax.ShapeDtypeStruct((PATCHES, HDIM), BF16),
            jax.ShapeDtypeStruct((FEAT, PATCHES), BF16),
            jax.ShapeDtypeStruct((ROWS, 1, 3 * HDIM), F32),
            jax.ShapeDtypeStruct((1, FEAT), F32),
        ),
        in_specs=[hbm] * 4,
        out_specs=(hbm,) * 4,
        scratch_shapes=[
            VMEM((PATCHES, HDIM), BF16),
            VMEM((FEAT, PATCHES), BF16),
            VMEM((ROWS, 3 * HDIM), F32),
            VMEM((1, 128), F32),
            VMEM((1, FEAT), F32),
            pltpu.SemaphoreType.DMA((2, 4)),
        ],
        compiler_params=pltpu.CompilerParams(vmem_limit_bytes=56 << 20),
    )(attended, input_grad, weight_grad, gain_grad)


def on_device(tokens, gain, w_qkv, out_grad):
    attended, input_grad, weight_grad, gain_grad = finish(
        *fused(tokens.T, gain.reshape(1, FEAT), w_qkv[:, 0, :], out_grad)
    )
    return attended, input_grad.T, weight_grad, gain_grad.reshape(FEAT)


def solution(mesh):
    in_specs = (P("dp", "mp"), P("mp"), P(None, "mp", None), P("dp", "mp"))
    out_specs = (P("dp", "mp"), P("dp", "mp"), P("dp", "mp", None), P("mp"))
    return jax.shard_map(
        on_device, mesh=mesh, in_specs=in_specs, out_specs=out_specs, check_vma=False
    )
```

```python
import math

import jax
import jax.numpy as jnp
from jax import lax
from jax.experimental import pallas as pl
from jax.experimental.pallas import tpu as pltpu
from jax.sharding import PartitionSpec as P

D = 3072
PATCHES = 256
HDIM = 128
FEAT = 96
NZ = 16
NY = 2
NMP = NZ * NY
CHIPS = 8
ROWS = 192
EPS = 1e-06
F32 = jnp.float32
BF16 = jnp.bfloat16
MESH = pl.DeviceIdType.MESH
VMEM = pltpu.VMEM


def remote(src, dst, send_sem, recv_sem, target):
    return pltpu.make_async_remote_copy(
        src_ref=src,
        dst_ref=dst,
        send_sem=send_sem,
        recv_sem=recv_sem,
        device_id=target,
        device_id_type=MESH,
    )


def folded(matrix):
    return jnp.sum(matrix.reshape(matrix.shape[0] // 8, 8, matrix.shape[1]), axis=0)


def column_mean(matrix):
    return jnp.sum(matrix, axis=0, keepdims=True) * (1.0 / matrix.shape[0])


def unit_columns(matrix):
    centred = matrix - column_mean(matrix)
    inverse = lax.rsqrt(column_mean(centred * centred) + EPS)
    return centred * inverse, inverse


def unit_pullback(normal, inverse, cotangent):
    return inverse * (
        cotangent - column_mean(cotangent) - normal * column_mean(cotangent * normal)
    )


def dot(a, b):
    return jnp.dot(a, b, preferred_element_type=F32)


def dot_rows(a, b):
    return lax.dot_general(a, b, (((1,), (1,)), ((), ())), preferred_element_type=F32)


def hub_of(offset):
    sign = 1 if offset > 0 else -1
    return sign * {1: 0, 3: 0, 2: 3, 4: 3, 6: 3, 5: 6, 7: 6}[abs(offset)]


FAR = (5, -5, 7, -7, 8)
FIVES = (5, -5)
NEAR = (2, -2, 4, -4)
HALVES = (0, 1)
GATHER_SLOTS = (
    *(("z", offset, half) for offset in (3, -3, 6, -6) for half in HALVES),
    *(("z", offset, None) for offset in (1, -1) + NEAR),
    *(("y", offset, half) for offset in (6, -6) for half in HALVES),
    "z far",
    "y near",
    "other",
)
SCATTER_SLOTS = (
    *(("z", offset, half) for offset in (6, -6, 3, -3) for half in HALVES),
    *(("z", offset, None) for offset in (1, -1)),
    *(("y", offset, half) for offset in (8, 7, -7, 6, -6) for half in HALVES),
    *(("y", offset, None) for offset in (3, -3, 1, -1, 0)),
    *(("z far", half) for half in HALVES),
    "z near",
    "other",
    "other near",
)


def rows_of(half):
    return slice(None) if half is None else pl.ds(half * (FEAT // 2), FEAT // 2)


def fused_kernel(
    x_any,
    gain_ref,
    w_any,
    do_any,
    att_any,
    ig_any,
    wg_any,
    gg_ref,
    att_ref,
    ig_ref,
    wg_ref,
    w_ref,
    do_ref,
    g_ref,
    gains,
    wt_ref,
    rows_ref,
    gb_ref,
    nt_ref,
    hg_ref,
    hgt_ref,
    pull_ref,
    ws_ref,
    zland,
    yland,
    oland,
    sums,
    spair,
    sland,
    spart,
    cland,
    mland,
    xland,
    hland,
    hstage,
    gstage,
    gland,
    local,
    bsend,
    brecv,
    rsend,
    rrecv,
    ssend,
    srecv,
    csend,
    crecv,
    xsend,
    xrecv,
    hsend,
    hrecv,
    gsend,
    grecv,
):
    mp = lax.axis_index("mp")
    row, z = mp // NZ, mp % NZ
    dp = lax.axis_index("dp")
    line, place, core = dp // 8, (dp // 2) % 4, dp % 2
    sign8 = 1 - 2 * core
    mine, theirs = row * NZ, (1 - row) * NZ
    partner = {"mp": theirs + z}

    def along(offset):
        return (z + offset + 2 * NZ) % NZ

    def at_z(offset):
        return {"mp": mine + along(offset)}

    def at_dp(lines, places, cores):
        return {"dp": (((line + lines) % 2) * 4 + place_at(places)) * 2 + (core + cores) % 2}

    def place_at(shift):
        return (place + shift) % 4

    def hub(offset):
        return 6 * sign8 if offset == 8 else hub_of(offset)

    mate = at_dp(0, 0, 1)
    across_line = at_dp(1, 0, 0)
    others = [(i, j, k) for i in (0, 1) for j in range(4) for k in (0, 1) if i + j + k > 0]

    own_copy = pltpu.make_async_copy(x_any, g_ref.at[mp], local.at[0])
    w_copy = pltpu.make_async_copy(w_any, w_ref, local.at[1])
    do_copy = pltpu.make_async_copy(do_any, do_ref, local.at[2])
    own_copy.start()
    barrier = pltpu.get_barrier_semaphore()
    peers = [at_z(offset) for offset in (3, -3, 2, -2, 1, -1)] + [partner]
    peers += [at_dp(*steps) for steps in others]
    for peer in peers:
        pl.semaphore_signal(barrier, inc=1, device_id=peer, device_id_type=MESH)
    w_copy.start()
    do_copy.start()
    gains[mp] = jnp.concatenate(
        [gain_ref[...].astype(F32), jnp.zeros((1, 128 - FEAT), F32)], axis=1
    )
    own_copy.wait()
    pl.semaphore_wait(barrier, len(peers))

    class Both:
        def __init__(self, key, target, block, half=None):
            slot = GATHER_SLOTS.index(key)
            part = g_ref.at[block, rows_of(half)]
            self.copies = [remote(part, part, bsend.at[0], brecv.at[0, slot], target)]
            if half != 1:
                part = gains.at[block]
                self.copies.append(remote(part, part, bsend.at[1], brecv.at[1, slot], target))

        def start(self):
            for copy in self.copies:
                copy.start()

        def wait_send(self):
            for copy in self.copies:
                copy.wait_send()

        def wait_recv(self):
            for copy in self.copies:
                copy.wait_recv()

    def spread(offset, half=None):
        key = "z far" if offset in FAR else ("z", offset, half)
        return Both(key, at_z(offset - hub(offset)), mine + along(-hub(offset)), half)

    def arrived(offset, half=None):
        Both(("z", offset, half), at_z(1), mine + along(-offset), half).wait_recv()

    def over(offset, half=None):
        key = ("y", offset, half) if abs(offset) == 6 else "y near"
        return Both(key, partner, mine + along(-offset), half)

    def over_arrived(offset, half=None):
        Both(("y", offset, half), partner, theirs + along(-offset), half).wait_recv()

    def other(offset, half=None):
        return Both("other", at_z(offset - hub(offset)), theirs + along(-hub(offset)), half)

    def all_arrived(key, count):
        Both(key, partner, pl.ds(0, count)).wait_recv()

    for half in HALVES:
        for offset in (3, -3):
            spread(offset, half).start()
    over(0).start()
    for offset in (1, -1):
        spread(offset).start()
    w_copy.wait()
    for part in range(D // 256):
        wt_ref[:, part * 256 : (part + 1) * 256] = w_ref[part * 256 : (part + 1) * 256, :].T
    do_copy.wait()
    cotangent = do_ref[...].T
    for half in HALVES:
        for sign in (1, -1):
            arrived(3 * sign, half)
            spread(6 * sign, half).start()
    for sign in (1, -1):
        spread(4 * sign).start()
        spread(2 * sign).start()
        over(3 * sign).start()
    for offset in (1, -1):
        arrived(offset)
        over(offset).start()
    for half in HALVES:
        for sign in (1, -1):
            arrived(6 * sign, half)
            over(6 * sign, half).start()
            spread(5 * sign, half).start()
            spread(7 * sign, half).start()
        spread(8, half).start()
    for offset in NEAR:
        arrived(offset)
        over(offset).start()
    for half in HALVES:
        for sign in (1, -1):
            over_arrived(6 * sign, half)
            other(5 * sign, half).start()
            other(7 * sign, half).start()
        other(8, half).start()
    all_arrived("z far", len(FAR))

    shift_row = jnp.sum(g_ref[mp].astype(F32), axis=0, keepdims=True) * (1.0 / FEAT)

    def add_block(block, totals):
        moved = g_ref[block].astype(F32) - shift_row
        return totals[0] + folded(moved), totals[1] + folded(moved * moved)

    def gain_columns(blocks):
        for i, block in enumerate(blocks):
            rows_ref[i : i + 1, :] = gains[block]
        turned = rows_ref[...].T
        for i, block in enumerate(blocks):
            gb_ref[block] = jnp.broadcast_to(turned[:FEAT, i : i + 1], (FEAT, 128)).astype(BF16)

    def gain_product(start):
        half = NZ * FEAT
        columns = pl.ds(pl.multiple_of(start * FEAT, half), half)
        return dot(wt_ref[:, columns], gb_ref[pl.ds(start, NZ)].reshape(half, 128))

    zero = jnp.zeros((8, PATCHES), F32)
    totals = lax.fori_loop(mine, mine + NZ, add_block, (zero, zero))
    gain_columns([mine + i for i in range(NZ)])
    gain_weights = gain_product(mine)
    all_arrived("y near", 9)
    over_blocks = [theirs + along(-offset) for offset in (0, 1, -1, 3, -3, 6, -6) + NEAR]
    far_blocks = [theirs + along(-offset) for offset in FAR]
    for block in over_blocks:
        totals = add_block(block, totals)
    gain_columns(over_blocks)
    all_arrived("other", len(FAR))
    for block in far_blocks:
        totals = add_block(block, totals)
    gain_columns(far_blocks)
    first = jnp.sum(totals[0], axis=0, keepdims=True) * (1.0 / D)
    second = jnp.sum(totals[1], axis=0, keepdims=True) * (1.0 / D)
    average = shift_row + first
    inverse = lax.rsqrt(second - first * first + EPS)

    def normalize(block, carry):
        factor = gb_ref[block].astype(F32)
        factor = jnp.concatenate([factor, factor], axis=1)
        normed = (g_ref[block].astype(F32) - average) * inverse
        nt_ref[block] = (normed * factor).astype(BF16)
        return carry

    lax.fori_loop(0, NMP, normalize, 0, unroll=4)

    wide = dot(wt_ref[...], nt_ref[...].reshape(D, PATCHES))
    projected = wide.astype(BF16)
    query, query_inverse = unit_columns(projected[:HDIM].astype(F32))
    keys, keys_inverse = unit_columns(projected[HDIM : 2 * HDIM].astype(F32))
    values = projected[2 * HDIM :]
    query_r, keys_r = query.astype(BF16), keys.astype(BF16)
    scale = 1.0 / math.sqrt(HDIM)
    exponent = jnp.exp(dot(keys_r.T, query_r) * scale)
    soft = exponent / jnp.sum(exponent, axis=0, keepdims=True)
    soft_r = soft.astype(BF16)
    soft_grad = dot(values.T, cotangent)
    values_grad = dot_rows(cotangent, soft_r)
    score_grad = soft * (soft_grad - jnp.sum(soft * soft_grad, axis=0, keepdims=True))
    score_grad = (score_grad * scale).astype(BF16)
    query_grad = unit_pullback(query, query_inverse, dot(keys_r, score_grad))
    keys_grad = unit_pullback(keys, keys_inverse, dot_rows(query_r, score_grad))
    hg = jnp.concatenate([query_grad, keys_grad, values_grad], axis=0).astype(BF16)
    hg_ref[...] = hg

    def pull_rows(start):
        def pull_part(part, carry):
            block = start + part * 8
            rows = pl.ds(pl.multiple_of(block * FEAT, 8 * FEAT), 8 * FEAT)
            pull_ref[pl.ds(block, 8)] = (
                dot(w_ref[rows, :], hg_ref[...]).astype(BF16).reshape(8, FEAT, PATCHES)
            )
            return carry

        lax.fori_loop(0, 2, pull_part, 0)

    def scatter_copy(key, src, dst, target):
        return remote(src, dst, rsend.at[0], rrecv.at[SCATTER_SLOTS.index(key)], target)

    def back_over(offset, half=None):
        rows = rows_of(half)
        src = pull_ref.at[theirs + along(-offset), rows]
        return scatter_copy(("y", offset, half), src, yland.at[offset % NZ, rows], partner)

    def back_other(offset):
        key = "other" if offset in FIVES else "other near"
        src = pull_ref.at[theirs + along(-offset)]
        land = oland.at[(FIVES + NEAR).index(offset)]
        return scatter_copy(key, src, land, at_z(hub(offset) - offset))

    def back(offset, half=None):
        rows = rows_of(half)
        key = ("z far", half) if offset in FAR else ("z", offset, half)
        key = "z near" if offset in NEAR else key
        src = pull_ref.at[mine + along(-offset), rows]
        return scatter_copy(key, src, zland.at[offset % NZ, rows], at_z(hub(offset) - offset))

    def all_landed(key, part):
        scatter_copy(key, part, part, partner).wait_recv()

    def back_sums(offset, src):
        stage = 0 if offset in FAR else (2 if abs(offset) in (1, 3) else 1)
        return remote(
            src,
            sland.at[offset % NZ],
            ssend.at[0],
            srecv.at[stage],
            at_z(hub(offset) - offset),
        )

    def sums_landed(stage, count):
        part = sland.at[pl.ds(0, count)]
        remote(part, part, ssend.at[0], srecv.at[stage], partner).wait_recv()

    def part_of(ref, block, half):
        return ref[block, rows_of(half)].astype(F32)

    def gathered(offset, half, over_half, inputs):
        total = part_of(pull_ref, mine + along(-offset), half)
        if over_half == half:
            back_over(offset, half).wait_recv()
        total = total + part_of(yland, offset % NZ, half)
        for at, at_half in inputs:
            if at_half == half:
                back(at, half).wait_recv()
            total = total + part_of(zland, at % NZ, half)
        return total

    def pass_on(offset, half, total):
        pull_ref[mine + along(-offset), rows_of(half)] = total.astype(BF16)
        back(offset, half).start()

    def core_copy(shift, line_of):
        chip = line_of * 4 + place_at(shift)
        slot = shift * 2 + line_of
        return remote(
            ws_ref.at[chip * 2 + 1 - core],
            cland.at[shift, line_of],
            csend.at[0],
            crecv.at[slot],
            mate,
        )

    def core_sum(shift, line_of):
        chip = line_of * 4 + place_at(shift)
        core_copy(shift, line_of).wait_recv()
        both = cland[shift, line_of].astype(F32) + ws_ref[chip * 2 + core].astype(F32)
        cland[shift, line_of] = both.astype(BF16)

    def place_copy(shift, line_of):
        up = shift == 1 or (shift == 2 and line_of == 0)
        land = mland.at[line_of] if shift == 2 else xland.at[0 if up else 1, line_of]
        return remote(
            cland.at[shift, line_of],
            land,
            xsend.at[0],
            xrecv.at[shift * 2 - 2 + line_of],
            at_dp(0, 1 if up else 3, 0),
        )

    def merge(shift, line_of):
        place_copy(2, line_of).wait_recv()
        both = cland[shift, line_of].astype(F32) + mland[line_of].astype(F32)
        cland[shift, line_of] = both.astype(BF16)
        place_copy(shift, line_of).start()

    hgt_ref[...] = hg.T

    shifts = (2, 1, 3, 0)

    def share(shift):
        for line_of in (0, 1):
            chip = line_of * 4 + place_at(shift)
            block = dot(nt_ref[pl.ds(chip * 4, 4)].reshape(4 * FEAT, PATCHES), hgt_ref[...])
            ws_ref[pl.ds(chip * 2, 2)] = block.astype(BF16).reshape(2, ROWS, 3 * HDIM)
            core_copy(shift, line_of).start()

    @pl.when(core == 1)
    def _():
        for shift in shifts:
            share(shift)

    pull_rows(theirs)
    for offset in FIVES:
        back_other(offset).start()
    for half in HALVES:
        for offset in (8, 7, -7):
            back_over(offset, half).start()
    for offset in NEAR:
        back_other(offset).start()
    pull_rows(mine)
    for half in HALVES:
        for offset in FIVES:
            back(offset, half).start()
    gain_weights = gain_weights + gain_product(theirs)
    hg_wide = hg.astype(F32)
    factor = jnp.concatenate([gain_weights, gain_weights], axis=1)
    sums[0] = jnp.sum(hg_wide * factor, axis=0, keepdims=True)
    sums[1] = jnp.sum(hg_wide * wide, axis=0, keepdims=True)
    sums_over = remote(sums, spair, ssend.at[1], srecv.at[3], partner)
    sums_over.start()

    @pl.when(core == 0)
    def _():
        share(2)
        share(1)

    all_landed("other", oland.at[pl.ds(0, 2)])
    for which, sign in enumerate((1, -1)):
        total = pull_ref[theirs + along(-6 * sign)].astype(F32) + oland[which].astype(F32)
        pull_ref[theirs + along(-6 * sign)] = total.astype(BF16)
    for half in HALVES:
        for sign in (1, -1):
            back_over(6 * sign, half).start()
    for line_of in (0, 1):
        core_sum(2, line_of)
        place_copy(2, line_of).start()
    for half in HALVES:
        for offset in (8, 7, -7):
            pass_on(offset, half, gathered(offset, half, half, ()))
    sums_over.wait_recv()
    spair[...] = spair[...] + sums[...]
    for offset in FAR + NEAR + (1, -1):
        back_sums(offset, spair).start()
    all_landed("other near", oland.at[pl.ds(0, 4)])
    for which, sign in enumerate((1, -1)):
        total = pull_ref[theirs + along(-3 * sign)].astype(F32)
        total = total + oland[2 + which].astype(F32) + oland[4 + which].astype(F32)
        pull_ref[theirs + along(-3 * sign)] = total.astype(BF16)
        back_over(3 * sign).start()
    for offset in (1, -1, 0):
        back_over(offset).start()
    for offset in NEAR:
        back(offset).start()

    @pl.when(core == 0)
    def _():
        share(3)
        share(0)

    for shift in (1, 3):
        core_sum(shift, 0)
        core_sum(shift, 1)
    place_copy(1, 1).start()
    place_copy(3, 0).start()
    att_ref[...] = dot(values, soft_r).T.astype(BF16)
    att_copy = pltpu.make_async_copy(att_ref, att_any, local.at[3])
    att_copy.start()

    def eighth(sign):
        return (1 - core if sign > 0 else core).astype(F32)

    for half in HALVES:
        back_over(6, half).wait_recv()
        back_over(-6, half).wait_recv()
        all_landed(("z far", half), zland.at[pl.ds(0, len(FAR)), rows_of(half)])
        for sign in (1, -1):
            total = gathered(6 * sign, half, -1, ((5 * sign, -1), (7 * sign, -1)))
            pass_on(6 * sign, half, total + eighth(sign) * part_of(zland, 8, half))
    sums_landed(0, len(FAR))
    for which, sign in enumerate((1, -1)):
        total = spair[...] + eighth(sign) * sland[8]
        spart[which] = total + sland[(5 * sign) % NZ] + sland[(7 * sign) % NZ]
        back_sums(6 * sign, spart.at[which]).start()
    merge(1, 0)
    merge(3, 1)
    core_sum(0, 0)
    core_sum(0, 1)
    for sign in (1, -1):
        back_over(3 * sign).wait_recv()
    all_landed("z near", zland.at[pl.ds(0, len(NEAR))])
    for half in HALVES:
        for sign in (1, -1):
            inputs = ((2 * sign, -1), (4 * sign, -1), (6 * sign, half))
            pass_on(3 * sign, half, gathered(3 * sign, half, -1, inputs))
    sums_landed(1, 6)
    for which, sign in enumerate((1, -1)):
        total = spair[...]
        for offset in (2 * sign, 4 * sign, 6 * sign):
            total = total + sland[offset % NZ]
        spart[2 + which] = total
        back_sums(3 * sign, spart.at[2 + which]).start()
    for offset in (1, -1):
        pass_on(offset, None, gathered(offset, None, None, ()))
    for shift in (1, 3):
        place_copy(shift, 0).wait_recv()
        place_copy(shift, 1).wait_recv()
    far = cland[0, 1 - line].astype(F32)
    for side in (0, 1):
        far = far + xland[side, 1 - line].astype(F32)
    hstage[...] = far.astype(BF16)
    line_copy = remote(hstage, hland, hsend.at[0], hrecv.at[0], across_line)
    line_copy.start()
    near = cland[0, line].astype(F32)
    for side in (0, 1):
        near = near + xland[side, line].astype(F32)
    wg_ref[...] = near

    normed = (g_ref[mp].astype(F32) - average) * inverse
    pull = gathered(0, None, None, ((1, None), (-1, None)))
    for offset in (3, -3):
        for half in HALVES:
            back(offset, half).wait_recv()
        pull = pull + part_of(zland, offset % NZ, None)
    product = pull * normed
    turned = (product[:, :128] + product[:, 128:]).T
    gstage[...] = jnp.concatenate(
        [jnp.sum(turned, axis=0, keepdims=True), jnp.zeros((1, 128 - FEAT), F32)], axis=1
    )

    for i, steps in enumerate(others):
        remote(gstage, gland.at[i], gsend.at[0], grecv.at[0], at_dp(*steps)).start()
    sums_landed(2, 4)
    sum_all = spair[...]
    for offset in (1, -1, 3, -3):
        sum_all = sum_all + sland[offset % NZ]
    own_gain = gb_ref[mp].astype(F32)
    scaled = pull * jnp.concatenate([own_gain, own_gain], axis=1)
    ig_ref[...] = (
        inverse * (scaled - sum_all[0] * (1.0 / D) - normed * (sum_all[1] * (1.0 / D)))
    ).astype(BF16)
    ig_copy = pltpu.make_async_copy(ig_ref, ig_any, local.at[4])
    ig_copy.start()
    line_copy.wait_recv()
    wg_ref[...] += hland[...].astype(F32)
    wg_copy = pltpu.make_async_copy(wg_ref, wg_any, local.at[5])
    wg_copy.start()
    Both("z far", partner, pl.ds(0, NMP - 1)).wait_send()
    part = pull_ref.at[pl.ds(0, 15 + 10 + 6)]
    scatter_copy("other", part, part, partner).wait_send()
    part = sland.at[pl.ds(0, NZ - 1)]
    remote(part, part, ssend.at[0], srecv.at[0], partner).wait_send()
    sums_over.wait_send()
    part = ws_ref.at[pl.ds(0, 8)]
    remote(part, part, csend.at[0], crecv.at[0], mate).wait_send()
    part = ws_ref.at[pl.ds(0, 6)]
    remote(part, part, xsend.at[0], xrecv.at[0], mate).wait_send()
    line_copy.wait_send()
    remote(gland, gland, gsend.at[0], grecv.at[0], mate).wait()
    gain_total = gstage[...]
    for i in range(len(others)):
        gain_total = gain_total + gland[i]
    gg_ref[...] = gain_total
    att_copy.wait()
    ig_copy.wait()
    wg_copy.wait()


def fused(x, gain, weights, out_grad):
    dma = pltpu.SemaphoreType.DMA
    return pl.pallas_call(
        fused_kernel,
        out_shape=(
            jax.ShapeDtypeStruct((PATCHES, HDIM), BF16),
            jax.ShapeDtypeStruct((FEAT, PATCHES), BF16),
            jax.ShapeDtypeStruct((ROWS, 3 * HDIM), F32),
            jax.ShapeDtypeStruct((1, 128), F32),
        ),
        in_specs=[
            pl.BlockSpec(memory_space=pltpu.HBM),
            pl.BlockSpec(memory_space=VMEM),
            pl.BlockSpec(memory_space=pltpu.HBM),
            pl.BlockSpec(memory_space=pltpu.HBM),
        ],
        out_specs=(
            pl.BlockSpec(memory_space=pltpu.HBM),
            pl.BlockSpec(memory_space=pltpu.HBM),
            pl.BlockSpec(memory_space=pltpu.HBM),
            pl.BlockSpec(memory_space=VMEM),
        ),
        scratch_shapes=[
            VMEM((PATCHES, HDIM), BF16),
            VMEM((FEAT, PATCHES), BF16),
            VMEM((ROWS, 3 * HDIM), F32),
            VMEM((D, 3 * HDIM), BF16),
            VMEM((PATCHES, HDIM), BF16),
            VMEM((NMP, FEAT, PATCHES), BF16),
            VMEM((NMP, 1, 128), F32),
            VMEM((3 * HDIM, D), BF16),
            VMEM((NZ, 128), F32),
            VMEM((NMP, FEAT, 128), BF16),
            VMEM((NMP, FEAT, PATCHES), BF16),
            VMEM((3 * HDIM, PATCHES), BF16),
            VMEM((PATCHES, 3 * HDIM), BF16),
            VMEM((NMP, FEAT, PATCHES), BF16),
            VMEM((2 * CHIPS, ROWS, 3 * HDIM), BF16),
            VMEM((NZ, FEAT, PATCHES), BF16),
            VMEM((NZ, FEAT, PATCHES), BF16),
            VMEM((6, FEAT, PATCHES), BF16),
            VMEM((2, 1, PATCHES), F32),
            VMEM((2, 1, PATCHES), F32),
            VMEM((NZ, 2, 1, PATCHES), F32),
            VMEM((4, 2, 1, PATCHES), F32),
            VMEM((4, 2, ROWS, 3 * HDIM), BF16),
            VMEM((2, ROWS, 3 * HDIM), BF16),
            VMEM((2, 2, ROWS, 3 * HDIM), BF16),
            VMEM((ROWS, 3 * HDIM), BF16),
            VMEM((ROWS, 3 * HDIM), BF16),
            VMEM((1, 128), F32),
            VMEM((2 * CHIPS - 1, 1, 128), F32),
            dma((6,)),
            dma((2,)),
            dma((2, len(GATHER_SLOTS))),
            dma((1,)),
            dma((len(SCATTER_SLOTS),)),
            dma((2,)),
            dma((4,)),
            dma((1,)),
            dma((8,)),
            dma((1,)),
            dma((6,)),
            dma((1,)),
            dma((1,)),
            dma((1,)),
            dma((1,)),
        ],
        compiler_params=pltpu.CompilerParams(
            collective_id=0, has_side_effects=True, vmem_limit_bytes=56 << 20
        ),
    )(x, gain, weights, out_grad)


def finish_kernel(
    att_in, ig_in, wg_in, gg_in, att_ref, ig_ref, wg_ref, gg_ref, att, ig, wg, gg, ggs, local
):
    moves = (
        (wg_in, wg, wg, wg_ref.at[:, 0, :]),
        (att_in, att, att, att_ref),
        (gg_in, gg, ggs, gg_ref),
        (ig_in, ig, ig, ig_ref),
    )
    loads = [
        pltpu.make_async_copy(move[0], move[1], local.at[0, i]) for i, move in enumerate(moves)
    ]
    stores = [
        pltpu.make_async_copy(move[2], move[3], local.at[1, i]) for i, move in enumerate(moves)
    ]
    for load in loads:
        load.start()
    for i in range(4):
        loads[i].wait()
        if i == 2:
            ggs[...] = gg[:, :FEAT]
        stores[i].start()
    for store in stores:
        store.wait()


def finish(attended, input_grad, weight_grad, gain_grad):
    hbm = pl.BlockSpec(memory_space=pltpu.HBM)
    return pl.pallas_call(
        finish_kernel,
        out_shape=(
            jax.ShapeDtypeStruct((PATCHES, HDIM), BF16),
            jax.ShapeDtypeStruct((FEAT, PATCHES), BF16),
            jax.ShapeDtypeStruct((ROWS, 1, 3 * HDIM), F32),
            jax.ShapeDtypeStruct((1, FEAT), F32),
        ),
        in_specs=[hbm] * 4,
        out_specs=(hbm,) * 4,
        scratch_shapes=[
            VMEM((PATCHES, HDIM), BF16),
            VMEM((FEAT, PATCHES), BF16),
            VMEM((ROWS, 3 * HDIM), F32),
            VMEM((1, 128), F32),
            VMEM((1, FEAT), F32),
            pltpu.SemaphoreType.DMA((2, 4)),
        ],
        compiler_params=pltpu.CompilerParams(vmem_limit_bytes=56 << 20),
    )(attended, input_grad, weight_grad, gain_grad)


def on_device(tokens, gain, w_qkv, out_grad):
    attended, input_grad, weight_grad, gain_grad = finish(
        *fused(tokens.T, gain.reshape(1, FEAT), w_qkv[:, 0, :], out_grad)
    )
    return attended, input_grad.T, weight_grad, gain_grad.reshape(FEAT)


def solution(mesh):
    in_specs = (P("dp", "mp"), P("mp"), P(None, "mp", None), P("dp", "mp"))
    out_specs = (P("dp", "mp"), P("dp", "mp"), P("dp", "mp", None), P("mp"))
    return jax.shard_map(
        on_device, mesh=mesh, in_specs=in_specs, out_specs=out_specs, check_vma=False
    )
```

```python
import math

import jax
import jax.numpy as jnp
from jax import lax
from jax.experimental import pallas as pl
from jax.experimental.pallas import tpu as pltpu
from jax.sharding import PartitionSpec as P

D = 3072
PATCHES = 256
HDIM = 128
FEAT = 96
NZ = 16
NY = 2
NMP = NZ * NY
CHIPS = 8
ROWS = 192
EPS = 1e-06
F32 = jnp.float32
BF16 = jnp.bfloat16
MESH = pl.DeviceIdType.MESH
VMEM = pltpu.VMEM


def remote(src, dst, send_sem, recv_sem, target):
    return pltpu.make_async_remote_copy(
        src_ref=src,
        dst_ref=dst,
        send_sem=send_sem,
        recv_sem=recv_sem,
        device_id=target,
        device_id_type=MESH,
    )


def folded(matrix):
    return jnp.sum(matrix.reshape(matrix.shape[0] // 8, 8, matrix.shape[1]), axis=0)


def column_mean(matrix):
    return jnp.sum(matrix, axis=0, keepdims=True) * (1.0 / matrix.shape[0])


def unit_columns(matrix):
    centred = matrix - column_mean(matrix)
    inverse = lax.rsqrt(column_mean(centred * centred) + EPS)
    return centred * inverse, inverse


def unit_pullback(normal, inverse, cotangent):
    return inverse * (
        cotangent - column_mean(cotangent) - normal * column_mean(cotangent * normal)
    )


def dot(a, b):
    return jnp.dot(a, b, preferred_element_type=F32)


def dot_rows(a, b):
    return lax.dot_general(a, b, (((1,), (1,)), ((), ())), preferred_element_type=F32)


def hub_of(offset):
    sign = 1 if offset > 0 else -1
    return sign * {1: 0, 3: 0, 2: 3, 4: 3, 6: 3, 5: 6, 7: 6}[abs(offset)]


FAR = (5, -5, 7, -7, 8)
FIVES = (5, -5)
NEAR = (2, -2, 4, -4)
HALVES = (0, 1)
GATHER_SLOTS = (
    *(("z", offset, half) for offset in (3, -3, 6, -6) for half in HALVES),
    *(("z", offset, None) for offset in (1, -1) + NEAR),
    *(("y", offset, half) for offset in (6, -6) for half in HALVES),
    "z far",
    "y near",
    "other",
)
SCATTER_SLOTS = (
    *(("z", offset, half) for offset in (6, -6, 3, -3) for half in HALVES),
    *(("z", offset, None) for offset in (1, -1)),
    *(("y", offset, half) for offset in (8, 7, -7, 6, -6) for half in HALVES),
    *(("y", offset, None) for offset in (3, -3, 1, -1, 0)),
    *(("z far", half) for half in HALVES),
    "z near",
    "other",
    "other near",
)


def rows_of(half):
    return slice(None) if half is None else pl.ds(half * (FEAT // 2), FEAT // 2)


def fused_kernel(
    x_any,
    gain_any,
    w_any,
    do_any,
    att_any,
    ig_any,
    wg_any,
    gg_ref,
    att_ref,
    ig_ref,
    wg_ref,
    w_ref,
    gain_ref,
    do_ref,
    g_ref,
    gains,
    wt_ref,
    rows_ref,
    gb_ref,
    nt_ref,
    hg_ref,
    hgt_ref,
    pull_ref,
    ws_ref,
    zland,
    yland,
    oland,
    sums,
    spair,
    sland,
    spart,
    cland,
    mland,
    xland,
    hland,
    hstage,
    gstage,
    gland,
    local,
    bsend,
    brecv,
    rsend,
    rrecv,
    ssend,
    srecv,
    csend,
    crecv,
    xsend,
    xrecv,
    hsend,
    hrecv,
    gsend,
    grecv,
):
    mp = lax.axis_index("mp")
    row, z = mp // NZ, mp % NZ
    dp = lax.axis_index("dp")
    line, place, core = dp // 8, (dp // 2) % 4, dp % 2
    sign8 = 1 - 2 * core
    mine, theirs = row * NZ, (1 - row) * NZ
    partner = {"mp": theirs + z}

    def along(offset):
        return (z + offset + 2 * NZ) % NZ

    def at_z(offset):
        return {"mp": mine + along(offset)}

    def at_dp(lines, places, cores):
        return {"dp": (((line + lines) % 2) * 4 + place_at(places)) * 2 + (core + cores) % 2}

    def place_at(shift):
        return (place + shift) % 4

    def hub(offset):
        return 6 * sign8 if offset == 8 else hub_of(offset)

    mate = at_dp(0, 0, 1)
    across_line = at_dp(1, 0, 0)
    others = [(i, j, k) for i in (0, 1) for j in range(4) for k in (0, 1) if i + j + k > 0]

    own_copy = pltpu.make_async_copy(x_any, g_ref.at[mp], local.at[0])
    w_copy = pltpu.make_async_copy(w_any, w_ref, local.at[1])
    do_copy = pltpu.make_async_copy(do_any, do_ref, local.at[2])
    own_copy.start()
    gain_copy = pltpu.make_async_copy(gain_any, gain_ref, local.at[6])
    gain_copy.start()
    barrier = pltpu.get_barrier_semaphore()
    peers = [at_z(offset) for offset in (3, -3, 2, -2, 1, -1)] + [partner]
    peers += [at_dp(*steps) for steps in others]
    for peer in peers:
        pl.semaphore_signal(barrier, inc=1, device_id=peer, device_id_type=MESH)
    w_copy.start()
    do_copy.start()
    gain_copy.wait()
    gains[mp] = jnp.concatenate(
        [gain_ref[...].astype(F32), jnp.zeros((1, 128 - FEAT), F32)], axis=1
    )
    own_copy.wait()
    pl.semaphore_wait(barrier, len(peers))

    class Both:
        def __init__(self, key, target, block, half=None):
            slot = GATHER_SLOTS.index(key)
            part = g_ref.at[block, rows_of(half)]
            self.copies = [remote(part, part, bsend.at[0], brecv.at[0, slot], target)]
            if half != 1:
                part = gains.at[block]
                self.copies.append(remote(part, part, bsend.at[1], brecv.at[1, slot], target))

        def start(self):
            for copy in self.copies:
                copy.start()

        def wait_send(self):
            for copy in self.copies:
                copy.wait_send()

        def wait_recv(self):
            for copy in self.copies:
                copy.wait_recv()

    def spread(offset, half=None):
        key = "z far" if offset in FAR else ("z", offset, half)
        return Both(key, at_z(offset - hub(offset)), mine + along(-hub(offset)), half)

    def arrived(offset, half=None):
        Both(("z", offset, half), at_z(1), mine + along(-offset), half).wait_recv()

    def over(offset, half=None):
        key = ("y", offset, half) if abs(offset) == 6 else "y near"
        return Both(key, partner, mine + along(-offset), half)

    def over_arrived(offset, half=None):
        Both(("y", offset, half), partner, theirs + along(-offset), half).wait_recv()

    def other(offset, half=None):
        return Both("other", at_z(offset - hub(offset)), theirs + along(-hub(offset)), half)

    def all_arrived(key, count):
        Both(key, partner, pl.ds(0, count)).wait_recv()

    for half in HALVES:
        for offset in (3, -3):
            spread(offset, half).start()
    over(0).start()
    for offset in (1, -1):
        spread(offset).start()
    w_copy.wait()
    for part in range(D // 256):
        wt_ref[:, part * 256 : (part + 1) * 256] = w_ref[part * 256 : (part + 1) * 256, :].T
    do_copy.wait()
    cotangent = do_ref[...].T
    for half in HALVES:
        for sign in (1, -1):
            arrived(3 * sign, half)
            spread(6 * sign, half).start()
    for sign in (1, -1):
        spread(4 * sign).start()
        spread(2 * sign).start()
        over(3 * sign).start()
    for offset in (1, -1):
        arrived(offset)
        over(offset).start()
    for half in HALVES:
        for sign in (1, -1):
            arrived(6 * sign, half)
            over(6 * sign, half).start()
        spread(8, half).start()
        for sign in (1, -1):
            spread(5 * sign, half).start()
            spread(7 * sign, half).start()
    for offset in NEAR:
        arrived(offset)
        over(offset).start()
    for half in HALVES:
        for sign in (1, -1):
            over_arrived(6 * sign, half)
        other(8, half).start()
        for sign in (1, -1):
            other(5 * sign, half).start()
            other(7 * sign, half).start()
    all_arrived("z far", len(FAR))

    shift_row = jnp.sum(g_ref[mp].astype(F32), axis=0, keepdims=True) * (1.0 / FEAT)

    def add_block(block, totals):
        moved = g_ref[block].astype(F32) - shift_row
        return totals[0] + folded(moved), totals[1] + folded(moved * moved)

    def gain_columns(blocks):
        for i, block in enumerate(blocks):
            rows_ref[i : i + 1, :] = gains[block]
        turned = rows_ref[...].T
        for i, block in enumerate(blocks):
            gb_ref[block] = jnp.broadcast_to(turned[:FEAT, i : i + 1], (FEAT, 128)).astype(BF16)

    def gain_product(start):
        half = NZ * FEAT
        columns = pl.ds(pl.multiple_of(start * FEAT, half), half)
        return dot(wt_ref[:, columns], gb_ref[pl.ds(start, NZ)].reshape(half, 128))

    zero = jnp.zeros((8, PATCHES), F32)
    totals = lax.fori_loop(mine, mine + NZ, add_block, (zero, zero))
    gain_columns([mine + i for i in range(NZ)])
    gain_weights = gain_product(mine)
    all_arrived("y near", 9)
    over_blocks = [theirs + along(-offset) for offset in (0, 1, -1, 3, -3, 6, -6) + NEAR]
    far_blocks = [theirs + along(-offset) for offset in FAR]
    for block in over_blocks:
        totals = add_block(block, totals)
    gain_columns(over_blocks)
    all_arrived("other", len(FAR))
    for block in far_blocks:
        totals = add_block(block, totals)
    gain_columns(far_blocks)
    first = jnp.sum(totals[0], axis=0, keepdims=True) * (1.0 / D)
    second = jnp.sum(totals[1], axis=0, keepdims=True) * (1.0 / D)
    average = shift_row + first
    inverse = lax.rsqrt(second - first * first + EPS)

    wide = None
    for first_block in range(0, NMP, 8):
        for block in range(first_block, first_block + 8):
            factor = gb_ref[block].astype(F32)
            factor = jnp.concatenate([factor, factor], axis=1)
            normed = (g_ref[block].astype(F32) - average) * inverse
            nt_ref[block] = (normed * factor).astype(BF16)
        rows = nt_ref[first_block : first_block + 8].reshape(8 * FEAT, PATCHES)
        columns = wt_ref[:, first_block * FEAT : (first_block + 8) * FEAT]
        wide = dot(columns, rows) if wide is None else wide + dot(columns, rows)
    projected = wide.astype(BF16)
    query, query_inverse = unit_columns(projected[:HDIM].astype(F32))
    keys, keys_inverse = unit_columns(projected[HDIM : 2 * HDIM].astype(F32))
    values = projected[2 * HDIM :]
    query_r, keys_r = query.astype(BF16), keys.astype(BF16)
    scale = 1.0 / math.sqrt(HDIM)
    exponent = jnp.exp(dot(keys_r.T, query_r) * scale)
    soft = exponent / jnp.sum(exponent, axis=0, keepdims=True)
    soft_r = soft.astype(BF16)
    soft_grad = dot(values.T, cotangent)
    values_grad = dot_rows(cotangent, soft_r)
    score_grad = soft * (soft_grad - jnp.sum(soft * soft_grad, axis=0, keepdims=True))
    score_grad = (score_grad * scale).astype(BF16)
    query_grad = unit_pullback(query, query_inverse, dot(keys_r, score_grad))
    keys_grad = unit_pullback(keys, keys_inverse, dot_rows(query_r, score_grad))
    hg = jnp.concatenate([query_grad, keys_grad, values_grad], axis=0).astype(BF16)
    hg_ref[...] = hg

    def pull_rows(start):
        def pull_part(part, carry):
            block = start + part * 8
            rows = pl.ds(pl.multiple_of(block * FEAT, 8 * FEAT), 8 * FEAT)
            pull_ref[pl.ds(block, 8)] = (
                dot(w_ref[rows, :], hg_ref[...]).astype(BF16).reshape(8, FEAT, PATCHES)
            )
            return carry

        lax.fori_loop(0, 2, pull_part, 0)

    def scatter_copy(key, src, dst, target):
        return remote(src, dst, rsend.at[0], rrecv.at[SCATTER_SLOTS.index(key)], target)

    def back_over(offset, half=None):
        rows = rows_of(half)
        src = pull_ref.at[theirs + along(-offset), rows]
        return scatter_copy(("y", offset, half), src, yland.at[offset % NZ, rows], partner)

    def back_other(offset):
        key = "other" if offset in FIVES else "other near"
        src = pull_ref.at[theirs + along(-offset)]
        land = oland.at[(FIVES + NEAR).index(offset)]
        return scatter_copy(key, src, land, at_z(hub(offset) - offset))

    def back(offset, half=None):
        rows = rows_of(half)
        key = ("z far", half) if offset in FAR else ("z", offset, half)
        key = "z near" if offset in NEAR else key
        src = pull_ref.at[mine + along(-offset), rows]
        return scatter_copy(key, src, zland.at[offset % NZ, rows], at_z(hub(offset) - offset))

    def all_landed(key, part):
        scatter_copy(key, part, part, partner).wait_recv()

    def back_sums(offset, src):
        stage = 0 if offset in FAR else (2 if abs(offset) in (1, 3) else 1)
        return remote(
            src,
            sland.at[offset % NZ],
            ssend.at[0],
            srecv.at[stage],
            at_z(hub(offset) - offset),
        )

    def sums_landed(stage, count):
        part = sland.at[pl.ds(0, count)]
        remote(part, part, ssend.at[0], srecv.at[stage], partner).wait_recv()

    def part_of(ref, block, half):
        return ref[block, rows_of(half)].astype(F32)

    def gathered(offset, half, over_half, inputs):
        total = part_of(pull_ref, mine + along(-offset), half)
        if over_half == half:
            back_over(offset, half).wait_recv()
        total = total + part_of(yland, offset % NZ, half)
        for at, at_half in inputs:
            if at_half == half:
                back(at, half).wait_recv()
            total = total + part_of(zland, at % NZ, half)
        return total

    def pass_on(offset, half, total):
        pull_ref[mine + along(-offset), rows_of(half)] = total.astype(BF16)
        back(offset, half).start()

    def core_copy(shift, line_of):
        chip = line_of * 4 + place_at(shift)
        slot = shift * 2 + line_of
        return remote(
            ws_ref.at[chip * 2 + 1 - core],
            cland.at[shift, line_of],
            csend.at[0],
            crecv.at[slot],
            mate,
        )

    def core_sum(shift, line_of):
        chip = line_of * 4 + place_at(shift)
        core_copy(shift, line_of).wait_recv()
        both = cland[shift, line_of].astype(F32) + ws_ref[chip * 2 + core].astype(F32)
        cland[shift, line_of] = both.astype(BF16)

    def place_copy(shift, line_of):
        up = shift == 1 or (shift == 2 and line_of == 0)
        land = mland.at[line_of] if shift == 2 else xland.at[0 if up else 1, line_of]
        return remote(
            cland.at[shift, line_of],
            land,
            xsend.at[0],
            xrecv.at[shift * 2 - 2 + line_of],
            at_dp(0, 1 if up else 3, 0),
        )

    def merge(shift, line_of):
        place_copy(2, line_of).wait_recv()
        both = cland[shift, line_of].astype(F32) + mland[line_of].astype(F32)
        cland[shift, line_of] = both.astype(BF16)
        place_copy(shift, line_of).start()

    hgt_ref[...] = hg.T

    shifts = (2, 1, 3, 0)

    def share(shift):
        for line_of in (0, 1):
            chip = line_of * 4 + place_at(shift)
            block = dot(nt_ref[pl.ds(chip * 4, 4)].reshape(4 * FEAT, PATCHES), hgt_ref[...])
            ws_ref[pl.ds(chip * 2, 2)] = block.astype(BF16).reshape(2, ROWS, 3 * HDIM)
            core_copy(shift, line_of).start()

    def next_places():
        for shift in (1, 3):
            core_sum(shift, 0)
            core_sum(shift, 1)
        place_copy(1, 1).start()
        place_copy(3, 0).start()

    def first_place():
        for line_of in (0, 1):
            core_sum(2, line_of)
            place_copy(2, line_of).start()

    @pl.when(core == 1)
    def _():
        for shift in shifts:
            share(shift)

    pull_rows(theirs)
    for offset in FIVES:
        back_other(offset).start()
    for half in HALVES:
        for offset in (8, 7, -7):
            back_over(offset, half).start()
    for offset in NEAR:
        back_other(offset).start()
    pull_rows(mine)
    for half in HALVES:
        for offset in FIVES:
            back(offset, half).start()
    @pl.when(core == 0)
    def _():
        share(2)
        share(1)

    gain_weights = gain_weights + gain_product(theirs)
    hg_wide = hg.astype(F32)
    factor = jnp.concatenate([gain_weights, gain_weights], axis=1)
    sums[0] = jnp.sum(hg_wide * factor, axis=0, keepdims=True)
    sums[1] = jnp.sum(hg_wide * wide, axis=0, keepdims=True)
    sums_over = remote(sums, spair, ssend.at[1], srecv.at[3], partner)
    sums_over.start()

    @pl.when(core == 0)
    def _():
        first_place()
        share(3)

    all_landed("other", oland.at[pl.ds(0, 2)])
    for which, sign in enumerate((1, -1)):
        total = pull_ref[theirs + along(-6 * sign)].astype(F32) + oland[which].astype(F32)
        pull_ref[theirs + along(-6 * sign)] = total.astype(BF16)
    for half in HALVES:
        for sign in (1, -1):
            back_over(6 * sign, half).start()
    pl.when(core == 0)(next_places)
    pl.when(core == 1)(first_place)
    for half in HALVES:
        for offset in (8, 7, -7):
            pass_on(offset, half, gathered(offset, half, half, ()))
    sums_over.wait_recv()
    spair[...] = spair[...] + sums[...]
    for offset in FAR + NEAR + (1, -1):
        back_sums(offset, spair).start()
    all_landed("other near", oland.at[pl.ds(0, 4)])
    for which, sign in enumerate((1, -1)):
        total = pull_ref[theirs + along(-3 * sign)].astype(F32)
        total = total + oland[2 + which].astype(F32) + oland[4 + which].astype(F32)
        pull_ref[theirs + along(-3 * sign)] = total.astype(BF16)
        back_over(3 * sign).start()
    for offset in (1, -1, 0):
        back_over(offset).start()
    for offset in NEAR:
        back(offset).start()

    @pl.when(core == 0)
    def _():
        share(0)

    pl.when(core == 1)(next_places)
    att_ref[...] = dot(values, soft_r).T.astype(BF16)
    att_copy = pltpu.make_async_copy(att_ref, att_any, local.at[3])
    att_copy.start()

    def eighth(sign):
        return (1 - core if sign > 0 else core).astype(F32)

    for half in HALVES:
        back_over(6, half).wait_recv()
        back_over(-6, half).wait_recv()
        all_landed(("z far", half), zland.at[pl.ds(0, len(FAR)), rows_of(half)])
        for sign in (1, -1):
            total = gathered(6 * sign, half, -1, ((5 * sign, -1), (7 * sign, -1)))
            pass_on(6 * sign, half, total + eighth(sign) * part_of(zland, 8, half))
        if half == 0:
            merge(1, 0)
            merge(3, 1)
    sums_landed(0, len(FAR))
    for which, sign in enumerate((1, -1)):
        total = spair[...] + eighth(sign) * sland[8]
        spart[which] = total + sland[(5 * sign) % NZ] + sland[(7 * sign) % NZ]
        back_sums(6 * sign, spart.at[which]).start()
    core_sum(0, 0)
    core_sum(0, 1)
    for sign in (1, -1):
        back_over(3 * sign).wait_recv()
    all_landed("z near", zland.at[pl.ds(0, len(NEAR))])
    for half in HALVES:
        for sign in (1, -1):
            inputs = ((2 * sign, -1), (4 * sign, -1), (6 * sign, half))
            pass_on(3 * sign, half, gathered(3 * sign, half, -1, inputs))
    sums_landed(1, 6)
    for which, sign in enumerate((1, -1)):
        total = spair[...]
        for offset in (2 * sign, 4 * sign, 6 * sign):
            total = total + sland[offset % NZ]
        spart[2 + which] = total
        back_sums(3 * sign, spart.at[2 + which]).start()
    for offset in (1, -1):
        pass_on(offset, None, gathered(offset, None, None, ()))
    for shift in (1, 3):
        place_copy(shift, 0).wait_recv()
        place_copy(shift, 1).wait_recv()
    far = cland[0, 1 - line].astype(F32)
    for side in (0, 1):
        far = far + xland[side, 1 - line].astype(F32)
    hstage[...] = far.astype(BF16)
    line_copy = remote(hstage, hland, hsend.at[0], hrecv.at[0], across_line)
    line_copy.start()
    near = cland[0, line].astype(F32)
    for side in (0, 1):
        near = near + xland[side, line].astype(F32)
    wg_ref[...] = near

    normed = (g_ref[mp].astype(F32) - average) * inverse
    pull = gathered(0, None, None, ((1, None), (-1, None)))
    for offset in (3, -3):
        for half in HALVES:
            back(offset, half).wait_recv()
        pull = pull + part_of(zland, offset % NZ, None)
    product = pull * normed
    turned = (product[:, :128] + product[:, 128:]).T
    gstage[...] = jnp.concatenate(
        [jnp.sum(turned, axis=0, keepdims=True), jnp.zeros((1, 128 - FEAT), F32)], axis=1
    )

    for i, steps in enumerate(others):
        remote(gstage, gland.at[i], gsend.at[0], grecv.at[0], at_dp(*steps)).start()
    sums_landed(2, 4)
    sum_all = spair[...]
    for offset in (1, -1, 3, -3):
        sum_all = sum_all + sland[offset % NZ]
    own_gain = gb_ref[mp].astype(F32)
    scaled = pull * jnp.concatenate([own_gain, own_gain], axis=1)
    ig_ref[...] = (
        inverse * (scaled - sum_all[0] * (1.0 / D) - normed * (sum_all[1] * (1.0 / D)))
    ).astype(BF16)
    ig_copy = pltpu.make_async_copy(ig_ref, ig_any, local.at[4])
    ig_copy.start()
    line_copy.wait_recv()
    wg_ref[...] += hland[...].astype(F32)
    wg_copy = pltpu.make_async_copy(wg_ref, wg_any, local.at[5])
    wg_copy.start()
    Both("z far", partner, pl.ds(0, NMP - 1)).wait_send()
    part = pull_ref.at[pl.ds(0, 15 + 10 + 6)]
    scatter_copy("other", part, part, partner).wait_send()
    part = sland.at[pl.ds(0, NZ - 1)]
    remote(part, part, ssend.at[0], srecv.at[0], partner).wait_send()
    sums_over.wait_send()
    part = ws_ref.at[pl.ds(0, 8)]
    remote(part, part, csend.at[0], crecv.at[0], mate).wait_send()
    part = ws_ref.at[pl.ds(0, 6)]
    remote(part, part, xsend.at[0], xrecv.at[0], mate).wait_send()
    line_copy.wait_send()
    remote(gland, gland, gsend.at[0], grecv.at[0], mate).wait()
    gain_total = gstage[...]
    for i in range(len(others)):
        gain_total = gain_total + gland[i]
    gg_ref[...] = gain_total
    att_copy.wait()
    ig_copy.wait()
    wg_copy.wait()


def fused(x, gain, weights, out_grad):
    dma = pltpu.SemaphoreType.DMA
    return pl.pallas_call(
        fused_kernel,
        out_shape=(
            jax.ShapeDtypeStruct((PATCHES, HDIM), BF16),
            jax.ShapeDtypeStruct((FEAT, PATCHES), BF16),
            jax.ShapeDtypeStruct((ROWS, 3 * HDIM), F32),
            jax.ShapeDtypeStruct((1, 128), F32),
        ),
        in_specs=[
            pl.BlockSpec(memory_space=pltpu.HBM),
            pl.BlockSpec(memory_space=pltpu.HBM),
            pl.BlockSpec(memory_space=pltpu.HBM),
            pl.BlockSpec(memory_space=pltpu.HBM),
        ],
        out_specs=(
            pl.BlockSpec(memory_space=pltpu.HBM),
            pl.BlockSpec(memory_space=pltpu.HBM),
            pl.BlockSpec(memory_space=pltpu.HBM),
            pl.BlockSpec(memory_space=VMEM),
        ),
        scratch_shapes=[
            VMEM((PATCHES, HDIM), BF16),
            VMEM((FEAT, PATCHES), BF16),
            VMEM((ROWS, 3 * HDIM), F32),
            VMEM((D, 3 * HDIM), BF16),
            VMEM((1, FEAT), BF16),
            VMEM((PATCHES, HDIM), BF16),
            VMEM((NMP, FEAT, PATCHES), BF16),
            VMEM((NMP, 1, 128), F32),
            VMEM((3 * HDIM, D), BF16),
            VMEM((NZ, 128), F32),
            VMEM((NMP, FEAT, 128), BF16),
            VMEM((NMP, FEAT, PATCHES), BF16),
            VMEM((3 * HDIM, PATCHES), BF16),
            VMEM((PATCHES, 3 * HDIM), BF16),
            VMEM((NMP, FEAT, PATCHES), BF16),
            VMEM((2 * CHIPS, ROWS, 3 * HDIM), BF16),
            VMEM((NZ, FEAT, PATCHES), BF16),
            VMEM((NZ, FEAT, PATCHES), BF16),
            VMEM((6, FEAT, PATCHES), BF16),
            VMEM((2, 1, PATCHES), F32),
            VMEM((2, 1, PATCHES), F32),
            VMEM((NZ, 2, 1, PATCHES), F32),
            VMEM((4, 2, 1, PATCHES), F32),
            VMEM((4, 2, ROWS, 3 * HDIM), BF16),
            VMEM((2, ROWS, 3 * HDIM), BF16),
            VMEM((2, 2, ROWS, 3 * HDIM), BF16),
            VMEM((ROWS, 3 * HDIM), BF16),
            VMEM((ROWS, 3 * HDIM), BF16),
            VMEM((1, 128), F32),
            VMEM((2 * CHIPS - 1, 1, 128), F32),
            dma((7,)),
            dma((2,)),
            dma((2, len(GATHER_SLOTS))),
            dma((1,)),
            dma((len(SCATTER_SLOTS),)),
            dma((2,)),
            dma((4,)),
            dma((1,)),
            dma((8,)),
            dma((1,)),
            dma((6,)),
            dma((1,)),
            dma((1,)),
            dma((1,)),
            dma((1,)),
        ],
        compiler_params=pltpu.CompilerParams(
            collective_id=0, has_side_effects=True, vmem_limit_bytes=56 << 20
        ),
    )(x, gain, weights, out_grad)


def finish_kernel(
    att_in, ig_in, wg_in, gg_in, att_ref, ig_ref, wg_ref, gg_ref, att, ig, wg, gg, ggs, local
):
    moves = (
        (wg_in, wg, wg, wg_ref.at[:, 0, :]),
        (att_in, att, att, att_ref),
        (gg_in, gg, ggs, gg_ref),
        (ig_in, ig, ig, ig_ref),
    )
    loads = [
        pltpu.make_async_copy(move[0], move[1], local.at[0, i]) for i, move in enumerate(moves)
    ]
    stores = [
        pltpu.make_async_copy(move[2], move[3], local.at[1, i]) for i, move in enumerate(moves)
    ]
    for load in loads:
        load.start()
    for i in range(4):
        loads[i].wait()
        if i == 2:
            ggs[...] = gg[:, :FEAT]
        stores[i].start()
    for store in stores:
        store.wait()


def finish(attended, input_grad, weight_grad, gain_grad):
    hbm = pl.BlockSpec(memory_space=pltpu.HBM)
    return pl.pallas_call(
        finish_kernel,
        out_shape=(
            jax.ShapeDtypeStruct((PATCHES, HDIM), BF16),
            jax.ShapeDtypeStruct((FEAT, PATCHES), BF16),
            jax.ShapeDtypeStruct((ROWS, 1, 3 * HDIM), F32),
            jax.ShapeDtypeStruct((1, FEAT), F32),
        ),
        in_specs=[hbm] * 4,
        out_specs=(hbm,) * 4,
        scratch_shapes=[
            VMEM((PATCHES, HDIM), BF16),
            VMEM((FEAT, PATCHES), BF16),
            VMEM((ROWS, 3 * HDIM), F32),
            VMEM((1, 128), F32),
            VMEM((1, FEAT), F32),
            pltpu.SemaphoreType.DMA((2, 4)),
        ],
        compiler_params=pltpu.CompilerParams(vmem_limit_bytes=56 << 20),
    )(attended, input_grad, weight_grad, gain_grad)


def on_device(tokens, gain, w_qkv, out_grad):
    attended, input_grad, weight_grad, gain_grad = finish(
        *fused(tokens.T, gain.reshape(1, FEAT), w_qkv[:, 0, :], out_grad)
    )
    return attended, input_grad.T, weight_grad, gain_grad.reshape(FEAT)


def solution(mesh):
    in_specs = (P("dp", "mp"), P("mp"), P(None, "mp", None), P("dp", "mp"))
    out_specs = (P("dp", "mp"), P("dp", "mp"), P("dp", "mp", None), P("mp"))
    return jax.shard_map(
        on_device, mesh=mesh, in_specs=in_specs, out_specs=out_specs, check_vma=False
    )
```

```python
import math

import jax
import jax.numpy as jnp
from jax import lax
from jax.experimental import pallas as pl
from jax.experimental.pallas import tpu as pltpu
from jax.sharding import PartitionSpec as P

D = 3072
PATCHES = 256
HDIM = 128
FEAT = 96
NZ = 16
NY = 2
NMP = NZ * NY
CHIPS = 8
ROWS = 192
EPS = 1e-06
F32 = jnp.float32
BF16 = jnp.bfloat16
MESH = pl.DeviceIdType.MESH
VMEM = pltpu.VMEM


def remote(src, dst, send_sem, recv_sem, target):
    return pltpu.make_async_remote_copy(
        src_ref=src,
        dst_ref=dst,
        send_sem=send_sem,
        recv_sem=recv_sem,
        device_id=target,
        device_id_type=MESH,
    )


def folded(matrix):
    return jnp.sum(matrix.reshape(matrix.shape[0] // 8, 8, matrix.shape[1]), axis=0)


def column_mean(matrix):
    return jnp.sum(matrix, axis=0, keepdims=True) * (1.0 / matrix.shape[0])


def unit_columns(matrix):
    centred = matrix - column_mean(matrix)
    inverse = lax.rsqrt(column_mean(centred * centred) + EPS)
    return centred * inverse, inverse


def unit_pullback(normal, inverse, cotangent):
    return inverse * (
        cotangent - column_mean(cotangent) - normal * column_mean(cotangent * normal)
    )


def dot(a, b):
    return jnp.dot(a, b, preferred_element_type=F32)


def dot_rows(a, b):
    return lax.dot_general(a, b, (((1,), (1,)), ((), ())), preferred_element_type=F32)


def hub_of(offset):
    sign = 1 if offset > 0 else -1
    return sign * {1: 0, 3: 0, 2: 3, 4: 3, 6: 3, 5: 6, 7: 6}[abs(offset)]


FAR = (5, -5, 7, -7, 8)
FIVES = (5, -5)
NEAR = (2, -2, 4, -4)
HALVES = (0, 1)
GATHER_SLOTS = (
    *(("z", offset, half) for offset in (3, -3, 6, -6) for half in HALVES),
    *(("z", offset, None) for offset in (1, -1) + NEAR),
    *(("y", offset, half) for offset in (6, -6) for half in HALVES),
    "z far",
    "y near",
    "other",
)
SCATTER_SLOTS = (
    *(("z", offset, half) for offset in (6, -6, 3, -3) for half in HALVES),
    *(("z", offset, None) for offset in (1, -1)),
    *(("y", offset, half) for offset in (8, 7, -7, 6, -6) for half in HALVES),
    *(("y", offset, None) for offset in (3, -3, 1, -1, 0)),
    *(("z far", half) for half in HALVES),
    "z near",
    "other",
    "other near",
)


def rows_of(half):
    return slice(None) if half is None else pl.ds(half * (FEAT // 2), FEAT // 2)


def fused_kernel(
    x_any,
    gain_any,
    w_any,
    do_any,
    att_any,
    ig_any,
    wg_any,
    gg_ref,
    att_ref,
    ig_ref,
    wg_ref,
    w_ref,
    gain_ref,
    do_ref,
    g_ref,
    gains,
    wt_ref,
    rows_ref,
    gb_ref,
    gw_ref,
    nt_ref,
    hg_ref,
    hgt_ref,
    pull_ref,
    ws_ref,
    zland,
    yland,
    oland,
    sums,
    spair,
    sland,
    spart,
    cland,
    mland,
    xland,
    hland,
    hstage,
    gstage,
    gland,
    local,
    bsend,
    brecv,
    rsend,
    rrecv,
    ssend,
    srecv,
    csend,
    crecv,
    xsend,
    xrecv,
    hsend,
    hrecv,
    gsend,
    grecv,
):
    mp = lax.axis_index("mp")
    row, z = mp // NZ, mp % NZ
    dp = lax.axis_index("dp")
    line, place, core = dp // 8, (dp // 2) % 4, dp % 2
    sign8 = 1 - 2 * core
    mine, theirs = row * NZ, (1 - row) * NZ
    partner = {"mp": theirs + z}

    def along(offset):
        return (z + offset + 2 * NZ) % NZ

    def at_z(offset):
        return {"mp": mine + along(offset)}

    def at_dp(lines, places, cores):
        return {"dp": (((line + lines) % 2) * 4 + place_at(places)) * 2 + (core + cores) % 2}

    def place_at(shift):
        return (place + shift) % 4

    def hub(offset):
        return 6 * sign8 if offset == 8 else hub_of(offset)

    mate = at_dp(0, 0, 1)
    across_line = at_dp(1, 0, 0)
    others = [(i, j, k) for i in (0, 1) for j in range(4) for k in (0, 1) if i + j + k > 0]

    own_copy = pltpu.make_async_copy(x_any, g_ref.at[mp], local.at[0])
    w_copy = pltpu.make_async_copy(w_any, w_ref, local.at[1])
    do_copy = pltpu.make_async_copy(do_any, do_ref, local.at[2])
    own_copy.start()
    gain_copy = pltpu.make_async_copy(gain_any, gain_ref, local.at[6])
    gain_copy.start()
    barrier = pltpu.get_barrier_semaphore()
    peers = [at_z(offset) for offset in (3, -3, 2, -2, 1, -1)] + [partner]
    peers += [at_dp(*steps) for steps in others]
    for peer in peers:
        pl.semaphore_signal(barrier, inc=1, device_id=peer, device_id_type=MESH)
    w_copy.start()
    do_copy.start()
    gain_copy.wait()
    gains[mp] = jnp.concatenate(
        [gain_ref[...].astype(F32), jnp.zeros((1, 128 - FEAT), F32)], axis=1
    )
    own_copy.wait()
    pl.semaphore_wait(barrier, len(peers))

    class Both:
        def __init__(self, key, target, block, half=None):
            slot = GATHER_SLOTS.index(key)
            part = g_ref.at[block, rows_of(half)]
            self.copies = [remote(part, part, bsend.at[0], brecv.at[0, slot], target)]
            if half != 1:
                part = gains.at[block]
                self.copies.append(remote(part, part, bsend.at[1], brecv.at[1, slot], target))

        def start(self):
            for copy in self.copies:
                copy.start()

        def wait_send(self):
            for copy in self.copies:
                copy.wait_send()

        def wait_recv(self):
            for copy in self.copies:
                copy.wait_recv()

    def spread(offset, half=None):
        key = "z far" if offset in FAR else ("z", offset, half)
        return Both(key, at_z(offset - hub(offset)), mine + along(-hub(offset)), half)

    def arrived(offset, half=None):
        Both(("z", offset, half), at_z(1), mine + along(-offset), half).wait_recv()

    def over(offset, half=None):
        key = ("y", offset, half) if abs(offset) == 6 else "y near"
        return Both(key, partner, mine + along(-offset), half)

    def over_arrived(offset, half=None):
        Both(("y", offset, half), partner, theirs + along(-offset), half).wait_recv()

    def other(offset, half=None):
        return Both("other", at_z(offset - hub(offset)), theirs + along(-hub(offset)), half)

    def all_arrived(key, count):
        Both(key, partner, pl.ds(0, count)).wait_recv()

    for half in HALVES:
        for offset in (3, -3):
            spread(offset, half).start()
    over(0).start()
    for offset in (1, -1):
        spread(offset).start()
    w_copy.wait()
    for part in range(D // 256):
        wt_ref[:, part * 256 : (part + 1) * 256] = w_ref[part * 256 : (part + 1) * 256, :].T
    do_copy.wait()
    cotangent = do_ref[...].T
    for half in HALVES:
        for sign in (1, -1):
            arrived(3 * sign, half)
            spread(6 * sign, half).start()
    for sign in (1, -1):
        spread(4 * sign).start()
        spread(2 * sign).start()
        over(3 * sign).start()
    for offset in (1, -1):
        arrived(offset)
        over(offset).start()
    for half in HALVES:
        for sign in (1, -1):
            arrived(6 * sign, half)
            over(6 * sign, half).start()
        spread(8, half).start()
        for sign in (1, -1):
            spread(5 * sign, half).start()
            spread(7 * sign, half).start()
    for offset in NEAR:
        arrived(offset)
        over(offset).start()
    for half in HALVES:
        for sign in (1, -1):
            over_arrived(6 * sign, half)
        other(8, half).start()
        for sign in (1, -1):
            other(5 * sign, half).start()
            other(7 * sign, half).start()
    all_arrived("z far", len(FAR))

    shift_row = jnp.sum(g_ref[mp].astype(F32), axis=0, keepdims=True) * (1.0 / FEAT)

    def add_block(block, totals):
        moved = g_ref[block].astype(F32) - shift_row
        return totals[0] + folded(moved), totals[1] + folded(moved * moved)

    def gain_columns(blocks):
        for i, block in enumerate(blocks):
            rows_ref[i : i + 1, :] = gains[block]
        turned = rows_ref[...].T
        for i, block in enumerate(blocks):
            gb_ref[block] = jnp.broadcast_to(turned[:FEAT, i : i + 1], (FEAT, 128)).astype(BF16)

    def gain_product(start):
        half = NZ * FEAT
        columns = pl.ds(pl.multiple_of(start * FEAT, half), half)
        return dot(wt_ref[:, columns], gb_ref[pl.ds(start, NZ)].reshape(half, 128))

    zero = jnp.zeros((8, PATCHES), F32)
    totals = lax.fori_loop(mine, mine + NZ, add_block, (zero, zero))
    gain_columns([mine + i for i in range(NZ)])
    gain_weights = gain_product(mine)
    all_arrived("y near", 9)
    over_blocks = [theirs + along(-offset) for offset in (0, 1, -1, 3, -3, 6, -6) + NEAR]
    far_blocks = [theirs + along(-offset) for offset in FAR]
    for block in over_blocks:
        totals = add_block(block, totals)
    gain_columns(over_blocks)
    all_arrived("other", len(FAR))
    for block in far_blocks:
        totals = add_block(block, totals)
    gain_columns(far_blocks)
    first = jnp.sum(totals[0], axis=0, keepdims=True) * (1.0 / D)
    second = jnp.sum(totals[1], axis=0, keepdims=True) * (1.0 / D)
    average = shift_row + first
    inverse = lax.rsqrt(second - first * first + EPS)

    wide = None
    for first_block in range(0, NMP, 8):
        for block in range(first_block, first_block + 8):
            factor = gb_ref[block].astype(F32)
            factor = jnp.concatenate([factor, factor], axis=1)
            normed = (g_ref[block].astype(F32) - average) * inverse
            nt_ref[block] = (normed * factor).astype(BF16)
        rows = nt_ref[first_block : first_block + 8].reshape(8 * FEAT, PATCHES)
        columns = wt_ref[:, first_block * FEAT : (first_block + 8) * FEAT]
        wide = dot(columns, rows) if wide is None else wide + dot(columns, rows)
    projected = wide.astype(BF16)
    query, query_inverse = unit_columns(projected[:HDIM].astype(F32))
    keys, keys_inverse = unit_columns(projected[HDIM : 2 * HDIM].astype(F32))
    values = projected[2 * HDIM :]
    query_r, keys_r = query.astype(BF16), keys.astype(BF16)
    scale = 1.0 / math.sqrt(HDIM)
    exponent = jnp.exp(dot(keys_r.T, query_r) * scale)
    soft = exponent / jnp.sum(exponent, axis=0, keepdims=True)
    soft_r = soft.astype(BF16)
    soft_grad = dot(values.T, cotangent)
    values_grad = dot_rows(cotangent, soft_r)
    score_grad = soft * (soft_grad - jnp.sum(soft * soft_grad, axis=0, keepdims=True))
    score_grad = (score_grad * scale).astype(BF16)
    query_grad = unit_pullback(query, query_inverse, dot(keys_r, score_grad))
    keys_grad = unit_pullback(keys, keys_inverse, dot_rows(query_r, score_grad))
    hg = jnp.concatenate([query_grad, keys_grad, values_grad], axis=0).astype(BF16)
    hg_ref[...] = hg

    def pull_rows(start):
        def pull_part(part, carry):
            block = start + part * 8
            rows = pl.ds(pl.multiple_of(block * FEAT, 8 * FEAT), 8 * FEAT)
            pull_ref[pl.ds(block, 8)] = (
                dot(w_ref[rows, :], hg_ref[...]).astype(BF16).reshape(8, FEAT, PATCHES)
            )
            return carry

        lax.fori_loop(0, 2, pull_part, 0)

    def scatter_copy(key, src, dst, target):
        return remote(src, dst, rsend.at[0], rrecv.at[SCATTER_SLOTS.index(key)], target)

    def back_over(offset, half=None):
        rows = rows_of(half)
        src = pull_ref.at[theirs + along(-offset), rows]
        return scatter_copy(("y", offset, half), src, yland.at[offset % NZ, rows], partner)

    def back_other(offset):
        key = "other" if offset in FIVES else "other near"
        src = pull_ref.at[theirs + along(-offset)]
        land = oland.at[(FIVES + NEAR).index(offset)]
        return scatter_copy(key, src, land, at_z(hub(offset) - offset))

    def back(offset, half=None):
        rows = rows_of(half)
        key = ("z far", half) if offset in FAR else ("z", offset, half)
        key = "z near" if offset in NEAR else key
        src = pull_ref.at[mine + along(-offset), rows]
        return scatter_copy(key, src, zland.at[offset % NZ, rows], at_z(hub(offset) - offset))

    def all_landed(key, part):
        scatter_copy(key, part, part, partner).wait_recv()

    def back_sums(offset, src):
        stage = 0 if offset in FAR else (2 if abs(offset) in (1, 3) else 1)
        return remote(
            src,
            sland.at[offset % NZ],
            ssend.at[0],
            srecv.at[stage],
            at_z(hub(offset) - offset),
        )

    def sums_landed(stage, count):
        part = sland.at[pl.ds(0, count)]
        remote(part, part, ssend.at[0], srecv.at[stage], partner).wait_recv()

    def part_of(ref, block, half):
        return ref[block, rows_of(half)].astype(F32)

    def gathered(offset, half, over_half, inputs):
        total = part_of(pull_ref, mine + along(-offset), half)
        if over_half == half:
            back_over(offset, half).wait_recv()
        total = total + part_of(yland, offset % NZ, half)
        for at, at_half in inputs:
            if at_half == half:
                back(at, half).wait_recv()
            total = total + part_of(zland, at % NZ, half)
        return total

    def pass_on(offset, half, total):
        pull_ref[mine + along(-offset), rows_of(half)] = total.astype(BF16)
        back(offset, half).start()

    def core_copy(shift, line_of):
        chip = line_of * 4 + place_at(shift)
        slot = shift * 2 + line_of
        return remote(
            ws_ref.at[chip * 2 + 1 - core],
            cland.at[shift, line_of],
            csend.at[0],
            crecv.at[slot],
            mate,
        )

    def core_sum(shift, line_of):
        chip = line_of * 4 + place_at(shift)
        core_copy(shift, line_of).wait_recv()
        both = cland[shift, line_of].astype(F32) + ws_ref[chip * 2 + core].astype(F32)
        cland[shift, line_of] = both.astype(BF16)

    def place_copy(shift, line_of):
        up = shift == 1 or (shift == 2 and line_of == 0)
        land = mland.at[line_of] if shift == 2 else xland.at[0 if up else 1, line_of]
        return remote(
            cland.at[shift, line_of],
            land,
            xsend.at[0],
            xrecv.at[shift * 2 - 2 + line_of],
            at_dp(0, 1 if up else 3, 0),
        )

    def merge(shift, line_of):
        place_copy(2, line_of).wait_recv()
        both = cland[shift, line_of].astype(F32) + mland[line_of].astype(F32)
        cland[shift, line_of] = both.astype(BF16)
        place_copy(shift, line_of).start()

    hgt_ref[...] = hg.T

    shifts = (2, 1, 3, 0)

    def share(shift):
        for line_of in (0, 1):
            chip = line_of * 4 + place_at(shift)
            block = dot(nt_ref[pl.ds(chip * 4, 4)].reshape(4 * FEAT, PATCHES), hgt_ref[...])
            ws_ref[pl.ds(chip * 2, 2)] = block.astype(BF16).reshape(2, ROWS, 3 * HDIM)
            core_copy(shift, line_of).start()

    def next_places():
        for shift in (1, 3):
            core_sum(shift, 0)
            core_sum(shift, 1)
        place_copy(1, 1).start()
        place_copy(3, 0).start()

    def first_place():
        for line_of in (0, 1):
            core_sum(2, line_of)
            place_copy(2, line_of).start()

    @pl.when(core == 1)
    def _():
        for shift in shifts:
            share(shift)
        gw_ref[...] = gain_product(theirs)

    pull_rows(theirs)
    for offset in FIVES:
        back_other(offset).start()
    for half in HALVES:
        for offset in (8, 7, -7):
            back_over(offset, half).start()
    for offset in NEAR:
        back_other(offset).start()
    pull_rows(mine)
    for half in HALVES:
        for offset in FIVES:
            back(offset, half).start()
    @pl.when(core == 0)
    def _():
        share(2)
        share(1)
        gw_ref[...] = gain_product(theirs)

    gain_weights = gain_weights + gw_ref[...]
    hg_wide = hg.astype(F32)
    factor = jnp.concatenate([gain_weights, gain_weights], axis=1)
    sums[0] = jnp.sum(hg_wide * factor, axis=0, keepdims=True)
    sums[1] = jnp.sum(hg_wide * wide, axis=0, keepdims=True)
    sums_over = remote(sums, spair, ssend.at[1], srecv.at[3], partner)
    sums_over.start()

    @pl.when(core == 0)
    def _():
        first_place()
        share(3)

    all_landed("other", oland.at[pl.ds(0, 2)])
    for which, sign in enumerate((1, -1)):
        total = pull_ref[theirs + along(-6 * sign)].astype(F32) + oland[which].astype(F32)
        pull_ref[theirs + along(-6 * sign)] = total.astype(BF16)
    for half in HALVES:
        for sign in (1, -1):
            back_over(6 * sign, half).start()
    pl.when(core == 0)(next_places)
    pl.when(core == 1)(first_place)
    for half in HALVES:
        for offset in (8, 7, -7):
            pass_on(offset, half, gathered(offset, half, half, ()))
    sums_over.wait_recv()
    spair[...] = spair[...] + sums[...]
    for offset in FAR + NEAR + (1, -1):
        back_sums(offset, spair).start()
    all_landed("other near", oland.at[pl.ds(0, 4)])
    for which, sign in enumerate((1, -1)):
        total = pull_ref[theirs + along(-3 * sign)].astype(F32)
        total = total + oland[2 + which].astype(F32) + oland[4 + which].astype(F32)
        pull_ref[theirs + along(-3 * sign)] = total.astype(BF16)
        back_over(3 * sign).start()
    for offset in (1, -1, 0):
        back_over(offset).start()
    for offset in NEAR:
        back(offset).start()

    @pl.when(core == 0)
    def _():
        share(0)

    pl.when(core == 1)(next_places)
    att_ref[...] = dot(values, soft_r).T.astype(BF16)
    att_copy = pltpu.make_async_copy(att_ref, att_any, local.at[3])
    att_copy.start()

    def eighth(sign):
        return (1 - core if sign > 0 else core).astype(F32)

    for half in HALVES:
        back_over(6, half).wait_recv()
        back_over(-6, half).wait_recv()
        all_landed(("z far", half), zland.at[pl.ds(0, len(FAR)), rows_of(half)])
        for sign in (1, -1):
            total = gathered(6 * sign, half, -1, ((5 * sign, -1), (7 * sign, -1)))
            pass_on(6 * sign, half, total + eighth(sign) * part_of(zland, 8, half))
        if half == 0:
            merge(1, 0)
            merge(3, 1)
    sums_landed(0, len(FAR))
    for which, sign in enumerate((1, -1)):
        total = spair[...] + eighth(sign) * sland[8]
        spart[which] = total + sland[(5 * sign) % NZ] + sland[(7 * sign) % NZ]
        back_sums(6 * sign, spart.at[which]).start()
    core_sum(0, 0)
    core_sum(0, 1)
    for sign in (1, -1):
        back_over(3 * sign).wait_recv()
    all_landed("z near", zland.at[pl.ds(0, len(NEAR))])
    for half in HALVES:
        for sign in (1, -1):
            inputs = ((2 * sign, -1), (4 * sign, -1), (6 * sign, half))
            pass_on(3 * sign, half, gathered(3 * sign, half, -1, inputs))
    sums_landed(1, 6)
    for which, sign in enumerate((1, -1)):
        total = spair[...]
        for offset in (2 * sign, 4 * sign, 6 * sign):
            total = total + sland[offset % NZ]
        spart[2 + which] = total
        back_sums(3 * sign, spart.at[2 + which]).start()
    for offset in (1, -1):
        pass_on(offset, None, gathered(offset, None, None, ()))
    for shift in (1, 3):
        place_copy(shift, 0).wait_recv()
        place_copy(shift, 1).wait_recv()
    far = cland[0, 1 - line].astype(F32)
    for side in (0, 1):
        far = far + xland[side, 1 - line].astype(F32)
    hstage[...] = far.astype(BF16)
    line_copy = remote(hstage, hland, hsend.at[0], hrecv.at[0], across_line)
    line_copy.start()
    near = cland[0, line].astype(F32)
    for side in (0, 1):
        near = near + xland[side, line].astype(F32)
    wg_ref[...] = near

    normed = (g_ref[mp].astype(F32) - average) * inverse
    pull = gathered(0, None, None, ((1, None), (-1, None)))
    for offset in (3, -3):
        for half in HALVES:
            back(offset, half).wait_recv()
        pull = pull + part_of(zland, offset % NZ, None)
    product = pull * normed
    turned = (product[:, :128] + product[:, 128:]).T
    gstage[...] = jnp.concatenate(
        [jnp.sum(turned, axis=0, keepdims=True), jnp.zeros((1, 128 - FEAT), F32)], axis=1
    )

    for i, steps in enumerate(others):
        remote(gstage, gland.at[i], gsend.at[0], grecv.at[0], at_dp(*steps)).start()
    sums_landed(2, 4)
    sum_all = spair[...]
    for offset in (1, -1, 3, -3):
        sum_all = sum_all + sland[offset % NZ]
    own_gain = gb_ref[mp].astype(F32)
    scaled = pull * jnp.concatenate([own_gain, own_gain], axis=1)
    ig_ref[...] = (
        inverse * (scaled - sum_all[0] * (1.0 / D) - normed * (sum_all[1] * (1.0 / D)))
    ).astype(BF16)
    ig_copy = pltpu.make_async_copy(ig_ref, ig_any, local.at[4])
    ig_copy.start()
    line_copy.wait_recv()
    wg_ref[...] += hland[...].astype(F32)
    wg_copy = pltpu.make_async_copy(wg_ref, wg_any, local.at[5])
    wg_copy.start()
    Both("z far", partner, pl.ds(0, NMP - 1)).wait_send()
    part = pull_ref.at[pl.ds(0, 15 + 10 + 6)]
    scatter_copy("other", part, part, partner).wait_send()
    part = sland.at[pl.ds(0, NZ - 1)]
    remote(part, part, ssend.at[0], srecv.at[0], partner).wait_send()
    sums_over.wait_send()
    part = ws_ref.at[pl.ds(0, 8)]
    remote(part, part, csend.at[0], crecv.at[0], mate).wait_send()
    part = ws_ref.at[pl.ds(0, 6)]
    remote(part, part, xsend.at[0], xrecv.at[0], mate).wait_send()
    line_copy.wait_send()
    remote(gland, gland, gsend.at[0], grecv.at[0], mate).wait()
    gain_total = gstage[...]
    for i in range(len(others)):
        gain_total = gain_total + gland[i]
    gg_ref[...] = gain_total
    att_copy.wait()
    ig_copy.wait()
    wg_copy.wait()


def fused(x, gain, weights, out_grad):
    dma = pltpu.SemaphoreType.DMA
    return pl.pallas_call(
        fused_kernel,
        out_shape=(
            jax.ShapeDtypeStruct((PATCHES, HDIM), BF16),
            jax.ShapeDtypeStruct((FEAT, PATCHES), BF16),
            jax.ShapeDtypeStruct((ROWS, 3 * HDIM), F32),
            jax.ShapeDtypeStruct((1, 128), F32),
        ),
        in_specs=[
            pl.BlockSpec(memory_space=pltpu.HBM),
            pl.BlockSpec(memory_space=pltpu.HBM),
            pl.BlockSpec(memory_space=pltpu.HBM),
            pl.BlockSpec(memory_space=pltpu.HBM),
        ],
        out_specs=(
            pl.BlockSpec(memory_space=pltpu.HBM),
            pl.BlockSpec(memory_space=pltpu.HBM),
            pl.BlockSpec(memory_space=pltpu.HBM),
            pl.BlockSpec(memory_space=VMEM),
        ),
        scratch_shapes=[
            VMEM((PATCHES, HDIM), BF16),
            VMEM((FEAT, PATCHES), BF16),
            VMEM((ROWS, 3 * HDIM), F32),
            VMEM((D, 3 * HDIM), BF16),
            VMEM((1, FEAT), BF16),
            VMEM((PATCHES, HDIM), BF16),
            VMEM((NMP, FEAT, PATCHES), BF16),
            VMEM((NMP, 1, 128), F32),
            VMEM((3 * HDIM, D), BF16),
            VMEM((NZ, 128), F32),
            VMEM((NMP, FEAT, 128), BF16),
            VMEM((3 * HDIM, 128), F32),
            VMEM((NMP, FEAT, PATCHES), BF16),
            VMEM((3 * HDIM, PATCHES), BF16),
            VMEM((PATCHES, 3 * HDIM), BF16),
            VMEM((NMP, FEAT, PATCHES), BF16),
            VMEM((2 * CHIPS, ROWS, 3 * HDIM), BF16),
            VMEM((NZ, FEAT, PATCHES), BF16),
            VMEM((NZ, FEAT, PATCHES), BF16),
            VMEM((6, FEAT, PATCHES), BF16),
            VMEM((2, 1, PATCHES), F32),
            VMEM((2, 1, PATCHES), F32),
            VMEM((NZ, 2, 1, PATCHES), F32),
            VMEM((4, 2, 1, PATCHES), F32),
            VMEM((4, 2, ROWS, 3 * HDIM), BF16),
            VMEM((2, ROWS, 3 * HDIM), BF16),
            VMEM((2, 2, ROWS, 3 * HDIM), BF16),
            VMEM((ROWS, 3 * HDIM), BF16),
            VMEM((ROWS, 3 * HDIM), BF16),
            VMEM((1, 128), F32),
            VMEM((2 * CHIPS - 1, 1, 128), F32),
            dma((7,)),
            dma((2,)),
            dma((2, len(GATHER_SLOTS))),
            dma((1,)),
            dma((len(SCATTER_SLOTS),)),
            dma((2,)),
            dma((4,)),
            dma((1,)),
            dma((8,)),
            dma((1,)),
            dma((6,)),
            dma((1,)),
            dma((1,)),
            dma((1,)),
            dma((1,)),
        ],
        compiler_params=pltpu.CompilerParams(
            collective_id=0, has_side_effects=True, vmem_limit_bytes=56 << 20
        ),
    )(x, gain, weights, out_grad)


def finish_kernel(
    att_in, ig_in, wg_in, gg_in, att_ref, ig_ref, wg_ref, gg_ref, att, ig, wg, gg, ggs, local
):
    moves = (
        (wg_in, wg, wg, wg_ref.at[:, 0, :]),
        (att_in, att, att, att_ref),
        (gg_in, gg, ggs, gg_ref),
        (ig_in, ig, ig, ig_ref),
    )
    loads = [
        pltpu.make_async_copy(move[0], move[1], local.at[0, i]) for i, move in enumerate(moves)
    ]
    stores = [
        pltpu.make_async_copy(move[2], move[3], local.at[1, i]) for i, move in enumerate(moves)
    ]
    for load in loads:
        load.start()
    for i in range(4):
        loads[i].wait()
        if i == 2:
            ggs[...] = gg[:, :FEAT]
        stores[i].start()
    for store in stores:
        store.wait()


def finish(attended, input_grad, weight_grad, gain_grad):
    hbm = pl.BlockSpec(memory_space=pltpu.HBM)
    return pl.pallas_call(
        finish_kernel,
        out_shape=(
            jax.ShapeDtypeStruct((PATCHES, HDIM), BF16),
            jax.ShapeDtypeStruct((FEAT, PATCHES), BF16),
            jax.ShapeDtypeStruct((ROWS, 1, 3 * HDIM), F32),
            jax.ShapeDtypeStruct((1, FEAT), F32),
        ),
        in_specs=[hbm] * 4,
        out_specs=(hbm,) * 4,
        scratch_shapes=[
            VMEM((PATCHES, HDIM), BF16),
            VMEM((FEAT, PATCHES), BF16),
            VMEM((ROWS, 3 * HDIM), F32),
            VMEM((1, 128), F32),
            VMEM((1, FEAT), F32),
            pltpu.SemaphoreType.DMA((2, 4)),
        ],
        compiler_params=pltpu.CompilerParams(vmem_limit_bytes=56 << 20),
    )(attended, input_grad, weight_grad, gain_grad)


def on_device(tokens, gain, w_qkv, out_grad):
    attended, input_grad, weight_grad, gain_grad = finish(
        *fused(tokens.T, gain.reshape(1, FEAT), w_qkv[:, 0, :], out_grad)
    )
    return attended, input_grad.T, weight_grad, gain_grad.reshape(FEAT)


def solution(mesh):
    in_specs = (P("dp", "mp"), P("mp"), P(None, "mp", None), P("dp", "mp"))
    out_specs = (P("dp", "mp"), P("dp", "mp"), P("dp", "mp", None), P("mp"))
    return jax.shard_map(
        on_device, mesh=mesh, in_specs=in_specs, out_specs=out_specs, check_vma=False
    )
```

```python
import math

import jax
import jax.numpy as jnp
from jax import lax
from jax.experimental import pallas as pl
from jax.experimental.pallas import tpu as pltpu
from jax.sharding import PartitionSpec as P

D = 3072
PATCHES = 256
HDIM = 128
FEAT = 96
NZ = 16
NY = 2
NMP = NZ * NY
CHIPS = 8
ROWS = 192
EPS = 1e-06
F32 = jnp.float32
BF16 = jnp.bfloat16
MESH = pl.DeviceIdType.MESH
VMEM = pltpu.VMEM


def remote(src, dst, send_sem, recv_sem, target):
    return pltpu.make_async_remote_copy(
        src_ref=src,
        dst_ref=dst,
        send_sem=send_sem,
        recv_sem=recv_sem,
        device_id=target,
        device_id_type=MESH,
    )


def folded(matrix):
    return jnp.sum(matrix.reshape(matrix.shape[0] // 8, 8, matrix.shape[1]), axis=0)


def column_mean(matrix):
    return jnp.sum(matrix, axis=0, keepdims=True) * (1.0 / matrix.shape[0])


def unit_columns(matrix):
    centred = matrix - column_mean(matrix)
    inverse = lax.rsqrt(column_mean(centred * centred) + EPS)
    return centred * inverse, inverse


def unit_pullback(normal, inverse, cotangent):
    return inverse * (
        cotangent - column_mean(cotangent) - normal * column_mean(cotangent * normal)
    )


def dot(a, b):
    return jnp.dot(a, b, preferred_element_type=F32)


def dot_rows(a, b):
    return lax.dot_general(a, b, (((1,), (1,)), ((), ())), preferred_element_type=F32)


def hub_of(offset):
    sign = 1 if offset > 0 else -1
    return sign * {1: 0, 3: 0, 2: 3, 4: 3, 6: 3, 5: 6, 7: 6}[abs(offset)]


FAR = (5, -5, 7, -7, 8)
FIVES = (5, -5)
NEAR = (2, -2, 4, -4)
HALVES = (0, 1)
GATHER_SLOTS = (
    *(("z", offset, half) for offset in (3, -3, 6, -6) for half in HALVES),
    *(("z", offset, None) for offset in (1, -1) + NEAR),
    *(("y", offset, half) for offset in (6, -6) for half in HALVES),
    "z far",
    "y near",
    "other",
)
SCATTER_SLOTS = (
    *(("z", offset, half) for offset in (6, -6, 3, -3) for half in HALVES),
    *(("z", offset, None) for offset in (1, -1)),
    *(("y", offset, half) for offset in (8, 7, -7, 6, -6) for half in HALVES),
    *(("y", offset, None) for offset in (3, -3, 1, -1, 0)),
    *(("z far", half) for half in HALVES),
    "z near",
    "other",
    "other near",
)


def rows_of(half):
    return slice(None) if half is None else pl.ds(half * (FEAT // 2), FEAT // 2)


def fused_kernel(
    x_any,
    gain_any,
    w_any,
    do_any,
    att_any,
    ig_any,
    wg_any,
    gg_ref,
    att_ref,
    ig_ref,
    wg_ref,
    w_ref,
    gain_ref,
    do_ref,
    g_ref,
    gains,
    wt_ref,
    rows_ref,
    gb_ref,
    nt_ref,
    hg_ref,
    hgt_ref,
    pull_ref,
    ws_ref,
    zland,
    yland,
    oland,
    sums,
    spair,
    sland,
    spart,
    cland,
    mland,
    xland,
    hland,
    hstage,
    gstage,
    gland,
    local,
    bsend,
    brecv,
    rsend,
    rrecv,
    ssend,
    srecv,
    csend,
    crecv,
    xsend,
    xrecv,
    hsend,
    hrecv,
    gsend,
    grecv,
):
    mp = lax.axis_index("mp")
    row, z = mp // NZ, mp % NZ
    dp = lax.axis_index("dp")
    line, place, core = dp // 8, (dp // 2) % 4, dp % 2
    sign8 = 1 - 2 * core
    mine, theirs = row * NZ, (1 - row) * NZ
    partner = {"mp": theirs + z}

    def along(offset):
        return (z + offset + 2 * NZ) % NZ

    def at_z(offset):
        return {"mp": mine + along(offset)}

    def at_dp(lines, places, cores):
        return {"dp": (((line + lines) % 2) * 4 + place_at(places)) * 2 + (core + cores) % 2}

    def place_at(shift):
        return (place + shift) % 4

    def hub(offset):
        return 6 * sign8 if offset == 8 else hub_of(offset)

    mate = at_dp(0, 0, 1)
    across_line = at_dp(1, 0, 0)
    others = [(i, j, k) for i in (0, 1) for j in range(4) for k in (0, 1) if i + j + k > 0]

    own_copy = pltpu.make_async_copy(x_any, g_ref.at[mp], local.at[0])
    w_copy = pltpu.make_async_copy(w_any, w_ref, local.at[1])
    do_copy = pltpu.make_async_copy(do_any, do_ref, local.at[2])
    own_copy.start()
    gain_copy = pltpu.make_async_copy(gain_any, gain_ref, local.at[6])
    gain_copy.start()
    barrier = pltpu.get_barrier_semaphore()
    peers = [at_z(offset) for offset in (3, -3, 2, -2, 1, -1)] + [partner]
    peers += [at_dp(*steps) for steps in others]
    for peer in peers:
        pl.semaphore_signal(barrier, inc=1, device_id=peer, device_id_type=MESH)
    w_copy.start()
    do_copy.start()
    gain_copy.wait()
    gains[mp] = jnp.concatenate(
        [gain_ref[...].astype(F32), jnp.zeros((1, 128 - FEAT), F32)], axis=1
    )
    own_copy.wait()
    pl.semaphore_wait(barrier, len(peers))

    class Both:
        def __init__(self, key, target, block, half=None):
            slot = GATHER_SLOTS.index(key)
            part = g_ref.at[block, rows_of(half)]
            self.copies = [remote(part, part, bsend.at[0], brecv.at[0, slot], target)]
            if half != 1:
                part = gains.at[block]
                self.copies.append(remote(part, part, bsend.at[1], brecv.at[1, slot], target))

        def start(self):
            for copy in self.copies:
                copy.start()

        def wait_send(self):
            for copy in self.copies:
                copy.wait_send()

        def wait_recv(self):
            for copy in self.copies:
                copy.wait_recv()

    def spread(offset, half=None):
        key = "z far" if offset in FAR else ("z", offset, half)
        return Both(key, at_z(offset - hub(offset)), mine + along(-hub(offset)), half)

    def arrived(offset, half=None):
        Both(("z", offset, half), at_z(1), mine + along(-offset), half).wait_recv()

    def over(offset, half=None):
        key = ("y", offset, half) if abs(offset) == 6 else "y near"
        return Both(key, partner, mine + along(-offset), half)

    def over_arrived(offset, half=None):
        Both(("y", offset, half), partner, theirs + along(-offset), half).wait_recv()

    def other(offset, half=None):
        return Both("other", at_z(offset - hub(offset)), theirs + along(-hub(offset)), half)

    def all_arrived(key, count):
        Both(key, partner, pl.ds(0, count)).wait_recv()

    for half in HALVES:
        for offset in (3, -3):
            spread(offset, half).start()
    over(0).start()
    for offset in (1, -1):
        spread(offset).start()
    w_copy.wait()
    for part in range(D // 256):
        wt_ref[:, part * 256 : (part + 1) * 256] = w_ref[part * 256 : (part + 1) * 256, :].T
    do_copy.wait()
    cotangent = do_ref[...].T
    for half in HALVES:
        for sign in (1, -1):
            arrived(3 * sign, half)
            spread(6 * sign, half).start()
    for sign in (1, -1):
        spread(4 * sign).start()
        spread(2 * sign).start()
        over(3 * sign).start()
    for offset in (1, -1):
        arrived(offset)
        over(offset).start()
    for half in HALVES:
        for sign in (1, -1):
            arrived(6 * sign, half)
            over(6 * sign, half).start()
        spread(8, half).start()
        for sign in (1, -1):
            spread(5 * sign, half).start()
            spread(7 * sign, half).start()
    for offset in NEAR:
        arrived(offset)
        over(offset).start()
    for half in HALVES:
        for sign in (1, -1):
            over_arrived(6 * sign, half)
        other(8, half).start()
        for sign in (1, -1):
            other(5 * sign, half).start()
            other(7 * sign, half).start()
    all_arrived("z far", len(FAR))

    shift_row = jnp.sum(g_ref[mp].astype(F32), axis=0, keepdims=True) * (1.0 / FEAT)

    def add_block(block, totals):
        moved = g_ref[block].astype(F32) - shift_row
        return totals[0] + folded(moved), totals[1] + folded(moved * moved)

    def gain_columns(blocks):
        for i, block in enumerate(blocks):
            rows_ref[i : i + 1, :] = gains[block]
        turned = rows_ref[...].T
        for i, block in enumerate(blocks):
            gb_ref[block] = jnp.broadcast_to(turned[:FEAT, i : i + 1], (FEAT, 128)).astype(BF16)

    def gain_product(start):
        half = NZ * FEAT
        columns = pl.ds(pl.multiple_of(start * FEAT, half), half)
        return dot(wt_ref[:, columns], gb_ref[pl.ds(start, NZ)].reshape(half, 128))

    zero = jnp.zeros((8, PATCHES), F32)
    totals = lax.fori_loop(mine, mine + NZ, add_block, (zero, zero))
    gain_columns([mine + i for i in range(NZ)])
    gain_weights = gain_product(mine)
    all_arrived("y near", 9)
    over_blocks = [theirs + along(-offset) for offset in (0, 1, -1, 3, -3, 6, -6) + NEAR]
    far_blocks = [theirs + along(-offset) for offset in FAR]
    for block in over_blocks:
        totals = add_block(block, totals)
    gain_columns(over_blocks)
    all_arrived("other", len(FAR))
    for block in far_blocks:
        totals = add_block(block, totals)
    gain_columns(far_blocks)
    first = jnp.sum(totals[0], axis=0, keepdims=True) * (1.0 / D)
    second = jnp.sum(totals[1], axis=0, keepdims=True) * (1.0 / D)
    average = shift_row + first
    inverse = lax.rsqrt(second - first * first + EPS)

    wide = None
    for first_block in range(0, NMP, 8):
        for block in range(first_block, first_block + 8):
            factor = gb_ref[block].astype(F32)
            factor = jnp.concatenate([factor, factor], axis=1)
            normed = (g_ref[block].astype(F32) - average) * inverse
            nt_ref[block] = (normed * factor).astype(BF16)
        rows = nt_ref[first_block : first_block + 8].reshape(8 * FEAT, PATCHES)
        columns = wt_ref[:, first_block * FEAT : (first_block + 8) * FEAT]
        wide = dot(columns, rows) if wide is None else wide + dot(columns, rows)
    projected = wide.astype(BF16)
    query, query_inverse = unit_columns(projected[:HDIM].astype(F32))
    keys, keys_inverse = unit_columns(projected[HDIM : 2 * HDIM].astype(F32))
    values = projected[2 * HDIM :]
    query_r, keys_r = query.astype(BF16), keys.astype(BF16)
    scale = 1.0 / math.sqrt(HDIM)
    exponent = jnp.exp(dot(keys_r.T, query_r) * scale)
    soft = exponent / jnp.sum(exponent, axis=0, keepdims=True)
    soft_r = soft.astype(BF16)
    soft_grad = dot(values.T, cotangent)
    values_grad = dot_rows(cotangent, soft_r)
    score_grad = soft * (soft_grad - jnp.sum(soft * soft_grad, axis=0, keepdims=True))
    score_grad = (score_grad * scale).astype(BF16)
    query_grad = unit_pullback(query, query_inverse, dot(keys_r, score_grad))
    keys_grad = unit_pullback(keys, keys_inverse, dot_rows(query_r, score_grad))
    hg = jnp.concatenate([query_grad, keys_grad, values_grad], axis=0).astype(BF16)
    hg_ref[...] = hg

    def pull_rows(start):
        def pull_part(part, carry):
            block = start + part * 8
            rows = pl.ds(pl.multiple_of(block * FEAT, 8 * FEAT), 8 * FEAT)
            pull_ref[pl.ds(block, 8)] = (
                dot(w_ref[rows, :], hg_ref[...]).astype(BF16).reshape(8, FEAT, PATCHES)
            )
            return carry

        lax.fori_loop(0, 2, pull_part, 0)

    def scatter_copy(key, src, dst, target):
        return remote(src, dst, rsend.at[0], rrecv.at[SCATTER_SLOTS.index(key)], target)

    def back_over(offset, half=None):
        rows = rows_of(half)
        src = pull_ref.at[theirs + along(-offset), rows]
        return scatter_copy(("y", offset, half), src, yland.at[offset % NZ, rows], partner)

    def back_other(offset):
        key = "other" if offset in FIVES else "other near"
        src = pull_ref.at[theirs + along(-offset)]
        land = oland.at[(FIVES + NEAR).index(offset)]
        return scatter_copy(key, src, land, at_z(hub(offset) - offset))

    def back(offset, half=None):
        rows = rows_of(half)
        key = ("z far", half) if offset in FAR else ("z", offset, half)
        key = "z near" if offset in NEAR else key
        src = pull_ref.at[mine + along(-offset), rows]
        return scatter_copy(key, src, zland.at[offset % NZ, rows], at_z(hub(offset) - offset))

    def all_landed(key, part):
        scatter_copy(key, part, part, partner).wait_recv()

    def back_sums(offset, src):
        stage = 0 if offset in FAR else (2 if abs(offset) in (1, 3) else 1)
        return remote(
            src,
            sland.at[offset % NZ],
            ssend.at[0],
            srecv.at[stage],
            at_z(hub(offset) - offset),
        )

    def sums_landed(stage, count):
        part = sland.at[pl.ds(0, count)]
        remote(part, part, ssend.at[0], srecv.at[stage], partner).wait_recv()

    def part_of(ref, block, half):
        return ref[block, rows_of(half)].astype(F32)

    def gathered(offset, half, over_half, inputs):
        total = part_of(pull_ref, mine + along(-offset), half)
        if over_half == half:
            back_over(offset, half).wait_recv()
        total = total + part_of(yland, offset % NZ, half)
        for at, at_half in inputs:
            if at_half == half:
                back(at, half).wait_recv()
            total = total + part_of(zland, at % NZ, half)
        return total

    def pass_on(offset, half, total):
        pull_ref[mine + along(-offset), rows_of(half)] = total.astype(BF16)
        back(offset, half).start()

    def core_copy(shift, line_of):
        chip = line_of * 4 + place_at(shift)
        slot = shift * 2 + line_of
        return remote(
            ws_ref.at[chip * 2 + 1 - core],
            cland.at[shift, line_of],
            csend.at[0],
            crecv.at[slot],
            mate,
        )

    def core_sum(shift, line_of):
        chip = line_of * 4 + place_at(shift)
        core_copy(shift, line_of).wait_recv()
        both = cland[shift, line_of].astype(F32) + ws_ref[chip * 2 + core].astype(F32)
        cland[shift, line_of] = both.astype(BF16)

    def place_copy(shift, line_of):
        up = shift == 1 or (shift == 2 and line_of == 0)
        land = mland.at[line_of] if shift == 2 else xland.at[0 if up else 1, line_of]
        return remote(
            cland.at[shift, line_of],
            land,
            xsend.at[0],
            xrecv.at[shift * 2 - 2 + line_of],
            at_dp(0, 1 if up else 3, 0),
        )

    def merge(shift, line_of):
        place_copy(2, line_of).wait_recv()
        both = cland[shift, line_of].astype(F32) + mland[line_of].astype(F32)
        cland[shift, line_of] = both.astype(BF16)
        place_copy(shift, line_of).start()

    hgt_ref[...] = hg.T

    shifts = (2, 1, 3, 0)

    def share(shift):
        for line_of in (0, 1):
            chip = line_of * 4 + place_at(shift)
            block = dot(nt_ref[pl.ds(chip * 4, 4)].reshape(4 * FEAT, PATCHES), hgt_ref[...])
            ws_ref[pl.ds(chip * 2, 2)] = block.astype(BF16).reshape(2, ROWS, 3 * HDIM)
            core_copy(shift, line_of).start()

    def next_places():
        for shift in (1, 3):
            core_sum(shift, 0)
            core_sum(shift, 1)
        place_copy(1, 1).start()
        place_copy(3, 0).start()

    def first_place():
        for line_of in (0, 1):
            core_sum(2, line_of)
            place_copy(2, line_of).start()

    @pl.when(core == 1)
    def _():
        for shift in shifts[:-1]:
            share(shift)

    pull_rows(theirs)
    for offset in FIVES:
        back_other(offset).start()
    for half in HALVES:
        for offset in (8, 7, -7):
            back_over(offset, half).start()
    for offset in NEAR:
        back_other(offset).start()
    pull_rows(mine)
    for half in HALVES:
        for offset in FIVES:
            back(offset, half).start()
    @pl.when(core == 0)
    def _():
        share(2)
        share(1)

    gain_weights = gain_weights + gain_product(theirs)
    hg_wide = hg.astype(F32)
    factor = jnp.concatenate([gain_weights, gain_weights], axis=1)
    sums[0] = jnp.sum(hg_wide * factor, axis=0, keepdims=True)
    sums[1] = jnp.sum(hg_wide * wide, axis=0, keepdims=True)
    sums_over = remote(sums, spair, ssend.at[1], srecv.at[3], partner)
    sums_over.start()

    @pl.when(core == 0)
    def _():
        first_place()
        share(3)

    all_landed("other", oland.at[pl.ds(0, 2)])
    for which, sign in enumerate((1, -1)):
        total = pull_ref[theirs + along(-6 * sign)].astype(F32) + oland[which].astype(F32)
        pull_ref[theirs + along(-6 * sign)] = total.astype(BF16)
    for half in HALVES:
        for sign in (1, -1):
            back_over(6 * sign, half).start()
    pl.when(core == 0)(next_places)
    pl.when(core == 1)(first_place)
    for half in HALVES:
        for offset in (8, 7, -7):
            pass_on(offset, half, gathered(offset, half, half, ()))
    sums_over.wait_recv()
    spair[...] = spair[...] + sums[...]
    for offset in FAR + NEAR + (1, -1):
        back_sums(offset, spair).start()
    all_landed("other near", oland.at[pl.ds(0, 4)])
    for which, sign in enumerate((1, -1)):
        total = pull_ref[theirs + along(-3 * sign)].astype(F32)
        total = total + oland[2 + which].astype(F32) + oland[4 + which].astype(F32)
        pull_ref[theirs + along(-3 * sign)] = total.astype(BF16)
        back_over(3 * sign).start()
    for offset in (1, -1, 0):
        back_over(offset).start()
    for offset in NEAR:
        back(offset).start()

    share(0)
    pl.when(core == 1)(next_places)
    att_ref[...] = dot(values, soft_r).T.astype(BF16)
    att_copy = pltpu.make_async_copy(att_ref, att_any, local.at[3])
    att_copy.start()

    def eighth(sign):
        return (1 - core if sign > 0 else core).astype(F32)

    for half in HALVES:
        back_over(6, half).wait_recv()
        back_over(-6, half).wait_recv()
        all_landed(("z far", half), zland.at[pl.ds(0, len(FAR)), rows_of(half)])
        for sign in (1, -1):
            total = gathered(6 * sign, half, -1, ((5 * sign, -1), (7 * sign, -1)))
            pass_on(6 * sign, half, total + eighth(sign) * part_of(zland, 8, half))
        if half == 0:
            merge(1, 0)
            merge(3, 1)
    sums_landed(0, len(FAR))
    for which, sign in enumerate((1, -1)):
        total = spair[...] + eighth(sign) * sland[8]
        spart[which] = total + sland[(5 * sign) % NZ] + sland[(7 * sign) % NZ]
        back_sums(6 * sign, spart.at[which]).start()
    core_sum(0, 0)
    core_sum(0, 1)
    for sign in (1, -1):
        back_over(3 * sign).wait_recv()
    all_landed("z near", zland.at[pl.ds(0, len(NEAR))])
    for half in HALVES:
        for sign in (1, -1):
            inputs = ((2 * sign, -1), (4 * sign, -1), (6 * sign, half))
            pass_on(3 * sign, half, gathered(3 * sign, half, -1, inputs))
    sums_landed(1, 6)
    for which, sign in enumerate((1, -1)):
        total = spair[...]
        for offset in (2 * sign, 4 * sign, 6 * sign):
            total = total + sland[offset % NZ]
        spart[2 + which] = total
        back_sums(3 * sign, spart.at[2 + which]).start()
    for offset in (1, -1):
        pass_on(offset, None, gathered(offset, None, None, ()))
    for shift in (1, 3):
        place_copy(shift, 0).wait_recv()
        place_copy(shift, 1).wait_recv()
    far = cland[0, 1 - line].astype(F32)
    for side in (0, 1):
        far = far + xland[side, 1 - line].astype(F32)
    hstage[...] = far.astype(BF16)
    line_copy = remote(hstage, hland, hsend.at[0], hrecv.at[0], across_line)
    line_copy.start()
    near = cland[0, line].astype(F32)
    for side in (0, 1):
        near = near + xland[side, line].astype(F32)
    wg_ref[...] = near

    normed = (g_ref[mp].astype(F32) - average) * inverse
    pull = gathered(0, None, None, ((1, None), (-1, None)))
    for offset in (3, -3):
        for half in HALVES:
            back(offset, half).wait_recv()
        pull = pull + part_of(zland, offset % NZ, None)
    product = pull * normed
    turned = (product[:, :128] + product[:, 128:]).T
    gstage[...] = jnp.concatenate(
        [jnp.sum(turned, axis=0, keepdims=True), jnp.zeros((1, 128 - FEAT), F32)], axis=1
    )

    for i, steps in enumerate(others):
        remote(gstage, gland.at[i], gsend.at[0], grecv.at[0], at_dp(*steps)).start()
    sums_landed(2, 4)
    sum_all = spair[...]
    for offset in (1, -1, 3, -3):
        sum_all = sum_all + sland[offset % NZ]
    own_gain = gb_ref[mp].astype(F32)
    scaled = pull * jnp.concatenate([own_gain, own_gain], axis=1)
    ig_ref[...] = (
        inverse * (scaled - sum_all[0] * (1.0 / D) - normed * (sum_all[1] * (1.0 / D)))
    ).astype(BF16)
    ig_copy = pltpu.make_async_copy(ig_ref, ig_any, local.at[4])
    ig_copy.start()
    line_copy.wait_recv()
    wg_ref[...] += hland[...].astype(F32)
    wg_copy = pltpu.make_async_copy(wg_ref, wg_any, local.at[5])
    wg_copy.start()
    Both("z far", partner, pl.ds(0, NMP - 1)).wait_send()
    part = pull_ref.at[pl.ds(0, 15 + 10 + 6)]
    scatter_copy("other", part, part, partner).wait_send()
    part = sland.at[pl.ds(0, NZ - 1)]
    remote(part, part, ssend.at[0], srecv.at[0], partner).wait_send()
    sums_over.wait_send()
    part = ws_ref.at[pl.ds(0, 8)]
    remote(part, part, csend.at[0], crecv.at[0], mate).wait_send()
    part = ws_ref.at[pl.ds(0, 6)]
    remote(part, part, xsend.at[0], xrecv.at[0], mate).wait_send()
    line_copy.wait_send()
    remote(gland, gland, gsend.at[0], grecv.at[0], mate).wait()
    gain_total = gstage[...]
    for i in range(len(others)):
        gain_total = gain_total + gland[i]
    gg_ref[...] = gain_total
    att_copy.wait()
    ig_copy.wait()
    wg_copy.wait()


def fused(x, gain, weights, out_grad):
    dma = pltpu.SemaphoreType.DMA
    return pl.pallas_call(
        fused_kernel,
        out_shape=(
            jax.ShapeDtypeStruct((PATCHES, HDIM), BF16),
            jax.ShapeDtypeStruct((FEAT, PATCHES), BF16),
            jax.ShapeDtypeStruct((ROWS, 3 * HDIM), F32),
            jax.ShapeDtypeStruct((1, 128), F32),
        ),
        in_specs=[
            pl.BlockSpec(memory_space=pltpu.HBM),
            pl.BlockSpec(memory_space=pltpu.HBM),
            pl.BlockSpec(memory_space=pltpu.HBM),
            pl.BlockSpec(memory_space=pltpu.HBM),
        ],
        out_specs=(
            pl.BlockSpec(memory_space=pltpu.HBM),
            pl.BlockSpec(memory_space=pltpu.HBM),
            pl.BlockSpec(memory_space=pltpu.HBM),
            pl.BlockSpec(memory_space=VMEM),
        ),
        scratch_shapes=[
            VMEM((PATCHES, HDIM), BF16),
            VMEM((FEAT, PATCHES), BF16),
            VMEM((ROWS, 3 * HDIM), F32),
            VMEM((D, 3 * HDIM), BF16),
            VMEM((1, FEAT), BF16),
            VMEM((PATCHES, HDIM), BF16),
            VMEM((NMP, FEAT, PATCHES), BF16),
            VMEM((NMP, 1, 128), F32),
            VMEM((3 * HDIM, D), BF16),
            VMEM((NZ, 128), F32),
            VMEM((NMP, FEAT, 128), BF16),
            VMEM((NMP, FEAT, PATCHES), BF16),
            VMEM((3 * HDIM, PATCHES), BF16),
            VMEM((PATCHES, 3 * HDIM), BF16),
            VMEM((NMP, FEAT, PATCHES), BF16),
            VMEM((2 * CHIPS, ROWS, 3 * HDIM), BF16),
            VMEM((NZ, FEAT, PATCHES), BF16),
            VMEM((NZ, FEAT, PATCHES), BF16),
            VMEM((6, FEAT, PATCHES), BF16),
            VMEM((2, 1, PATCHES), F32),
            VMEM((2, 1, PATCHES), F32),
            VMEM((NZ, 2, 1, PATCHES), F32),
            VMEM((4, 2, 1, PATCHES), F32),
            VMEM((4, 2, ROWS, 3 * HDIM), BF16),
            VMEM((2, ROWS, 3 * HDIM), BF16),
            VMEM((2, 2, ROWS, 3 * HDIM), BF16),
            VMEM((ROWS, 3 * HDIM), BF16),
            VMEM((ROWS, 3 * HDIM), BF16),
            VMEM((1, 128), F32),
            VMEM((2 * CHIPS - 1, 1, 128), F32),
            dma((7,)),
            dma((2,)),
            dma((2, len(GATHER_SLOTS))),
            dma((1,)),
            dma((len(SCATTER_SLOTS),)),
            dma((2,)),
            dma((4,)),
            dma((1,)),
            dma((8,)),
            dma((1,)),
            dma((6,)),
            dma((1,)),
            dma((1,)),
            dma((1,)),
            dma((1,)),
        ],
        compiler_params=pltpu.CompilerParams(
            collective_id=0, has_side_effects=True, vmem_limit_bytes=56 << 20
        ),
    )(x, gain, weights, out_grad)


def finish_kernel(
    att_in, ig_in, wg_in, gg_in, att_ref, ig_ref, wg_ref, gg_ref, att, ig, wg, gg, ggs, local
):
    moves = (
        (wg_in, wg, wg, wg_ref.at[:, 0, :]),
        (att_in, att, att, att_ref),
        (gg_in, gg, ggs, gg_ref),
        (ig_in, ig, ig, ig_ref),
    )
    loads = [
        pltpu.make_async_copy(move[0], move[1], local.at[0, i]) for i, move in enumerate(moves)
    ]
    stores = [
        pltpu.make_async_copy(move[2], move[3], local.at[1, i]) for i, move in enumerate(moves)
    ]
    for load in loads:
        load.start()
    for i in range(4):
        loads[i].wait()
        if i == 2:
            ggs[...] = gg[:, :FEAT]
        stores[i].start()
    for store in stores:
        store.wait()


def finish(attended, input_grad, weight_grad, gain_grad):
    hbm = pl.BlockSpec(memory_space=pltpu.HBM)
    return pl.pallas_call(
        finish_kernel,
        out_shape=(
            jax.ShapeDtypeStruct((PATCHES, HDIM), BF16),
            jax.ShapeDtypeStruct((FEAT, PATCHES), BF16),
            jax.ShapeDtypeStruct((ROWS, 1, 3 * HDIM), F32),
            jax.ShapeDtypeStruct((1, FEAT), F32),
        ),
        in_specs=[hbm] * 4,
        out_specs=(hbm,) * 4,
        scratch_shapes=[
            VMEM((PATCHES, HDIM), BF16),
            VMEM((FEAT, PATCHES), BF16),
            VMEM((ROWS, 3 * HDIM), F32),
            VMEM((1, 128), F32),
            VMEM((1, FEAT), F32),
            pltpu.SemaphoreType.DMA((2, 4)),
        ],
        compiler_params=pltpu.CompilerParams(vmem_limit_bytes=56 << 20),
    )(attended, input_grad, weight_grad, gain_grad)


def on_device(tokens, gain, w_qkv, out_grad):
    attended, input_grad, weight_grad, gain_grad = finish(
        *fused(tokens.T, gain.reshape(1, FEAT), w_qkv[:, 0, :], out_grad)
    )
    return attended, input_grad.T, weight_grad, gain_grad.reshape(FEAT)


def solution(mesh):
    in_specs = (P("dp", "mp"), P("mp"), P(None, "mp", None), P("dp", "mp"))
    out_specs = (P("dp", "mp"), P("dp", "mp"), P("dp", "mp", None), P("mp"))
    return jax.shard_map(
        on_device, mesh=mesh, in_specs=in_specs, out_specs=out_specs, check_vma=False
    )
```
